32 devices in a mesh: outer: 2 (over core), inner: 16 (over z, y, x).
Axes of the slice: x: 2, y: 2, z: 4, core: 2. Of those that a mesh axis runs over, the one named last changes fastest.
Arguments:
- cotangent: bfloat16 [4096, 2048], P(('outer', 'inner')), may hold values from -1.5 to 1.5
- hidden: bfloat16 [4096, 8, 384], P(('outer', 'inner')), may hold values from -6 to 6
- probs: float32 [4096, 8], P(('outer', 'inner')), may hold values from 0.02 to 0.5
- expert_ids: int32 [4096, 8], P(('outer', 'inner')), may hold values from 0 to 63, all different within a row; in each aligned block of 128 rows (0 to 127, 128 to 255, ...) at most 24 rows name the same one
- secondary: bfloat16 [384, 64, 2048], P(None, 'inner'), may hold values from -0.3125 to 0.3125
- weight: float32 [384, 64, 2048], P('outer', 'inner'), may hold values from -0.3125 to 0.3125
- moment1: float32 [384, 64, 2048], P('outer', 'inner'), may hold values from -4 to 4
- moment2: float32 [384, 64, 2048], P('outer', 'inner'), may hold values from 0.05 to 2
Outputs:
- d_hidden: bfloat16 [4096, 8, 384], P(('outer', 'inner'))
- d_probs: float32 [4096, 8], P(('outer', 'inner'))
- new_weight: float32 [384, 64, 2048], P('outer', 'inner')
- new_moment1: float32 [384, 64, 2048], P('outer', 'inner')
- new_moment2: float32 [384, 64, 2048], P('outer', 'inner')
- new_secondary: bfloat16 [384, 64, 2048], P(None, 'inner')
The draws below stay inside these ranges and needn't reach their ends.
Inputs may be any that keep to these rules, and one draw needn't show every extreme that they name: `expert_ids`: each token names 8 different experts. Among the 1024 choices of the rows of one device (aligned blocks of 128 tokens), no expert is named more than 24 times, a bound that some block reaches.
All inputs are finite; a program needn't handle non-finite values.
Results may differ from the reference program's by a relative error of at most 0.0085.
Values may be sent and summed in bfloat16 or wider, within the bound.
No kernel may reach another device: no remote copies, remote signals or barrier semaphores. Data moves between devices by JAX's collectives and lax.ppermute only.
A program may use at most 128 MiB of HBM per device.

```python
import math
import jax
import jax.numpy as jnp
import numpy as np
from jax import lax

D = 2048
H = 384
EXPERTS = 64
TOP = 8
TOK_DEV = 128
CAP = 24
TOKENS = 4096
N_OUTER = 2
N_INNER = 16


def spiked(drawn, rng, source, target, parts, factor):
    def block_of(axis_at):
        return (jnp.arange(drawn.shape[axis_at]) // (drawn.shape[axis_at] // parts)).reshape((-1,) + (1,) * (drawn.ndim - 1 - axis_at))

    near = jax.random.permutation(rng, parts)[block_of(target)]
    second = (block_of(target) + parts // 2) % parts
    return jnp.where((block_of(source) == near) | (block_of(source) == second), factor * drawn, drawn)


def shard_levels(stream_key, extent, pieces, least, largest):
    level = 1.0
    for dim, shards_of in pieces:
        draws = jax.random.uniform(jax.random.fold_in(jax.random.fold_in(stream_key, 6), dim), (shards_of,), jnp.float32, least / len(pieces), largest / len(pieces))
        level = level * jnp.repeat(jnp.exp(draws), extent[dim] // shards_of).reshape((-1,) + (1,) * (len(extent) - 1 - dim))
    return level


def routed_block(own_key, own, number, rows, number_of, top, most, skew):
    order = jax.random.permutation(own_key, number_of)
    crowded, common = shares(number_of, rows * top, most, skew, True), shares(number_of, rows * top, most, skew, False)
    places = jnp.arange(number_of)

    def named(tallies, turn):
        used = int((tallies > 0).sum())
        fixed = max(1, used // 4)
        moved = fixed + (places - fixed + turn * (used - fixed)) % max(1, number_of - fixed)
        return jnp.zeros((number_of,), jnp.int32).at[order[jnp.where(places < fixed, places, moved)]].set(jnp.asarray(tallies, jnp.int32))

    tallies = jnp.where(number % 4 == 0, named(crowded, number // 4), named(common, number - number // 4 - 1))
    mixed = jax.random.permutation(jax.random.fold_in(own, 3), number_of)
    giver, taker = mixed[0:number_of // 2 * 2:2], mixed[1:number_of // 2 * 2:2]
    slack = jnp.minimum(tallies[giver] - 1, most - tallies[taker]) // 2
    slack = jnp.where((giver == order[0]) | (taker == order[0]) | (tallies[taker] == 0), 0, jnp.maximum(slack, 0))
    moved = jax.random.randint(jax.random.fold_in(own, 4), (number_of // 2,), 0, 1 << 20) % (slack + 1)
    tallies = tallies.at[giver].add(-moved).at[taker].add(moved)
    items = jnp.searchsorted(jnp.cumsum(tallies), jnp.arange(rows * top), side="right").astype(jnp.int32)
    table = items.reshape(top, rows).T
    table = table[jax.random.permutation(jax.random.fold_in(own, 1), rows)]
    turn = jax.random.randint(jax.random.fold_in(own, 2), (rows, 1), 0, top)
    return jnp.take_along_axis(table, (jnp.arange(top)[None, :] + turn) % top, axis=1)


def shares(amount, total, limit, slope, full):
    loads = [(1 << 20) // math.isqrt(grade ** slope) + 1 for grade in range(1, amount + 1)]
    largest = limit if full else min(limit, max(-(-total // amount), total * loads[0] // sum(loads)))
    least = 1 if total - largest >= amount - 1 else 0
    holding, spare = [largest] + [least] * (amount - 1), total - largest - least * (amount - 1)
    while spare > 0:
        movable = [i for i in range(1, amount) if holding[i] < largest] or [i for i in range(1, amount) if holding[i] < limit]
        whole, budget = sum([loads[i] for i in movable]), spare
        for i in movable:
            addition = min(limit - holding[i], max(1, budget * loads[i] // whole), spare)
            holding[i] = holding[i] + addition
            spare = spare - addition
    return np.array(holding)


def bell_draw(key, shape, spread, limit, split=(), kind=jnp.bfloat16):
    loudness = shard_levels(key, shape, split, -0.22, 0.18) if split else 1.0
    array = jax.random.normal(key, shape, jnp.float32) * spread * loudness
    return jnp.minimum(jnp.maximum(array, -limit), limit).astype(kind)


def bell_draw_with(key, extent, spread, most, pieces, heavy, kind=jnp.bfloat16):
    array = spread * jax.random.normal(key, extent, jnp.float32)
    if pieces:
        array = array * shard_levels(key, extent, pieces, -0.22, 0.18)
    return jnp.clip(spiked(array, jax.random.fold_in(key, 3), *heavy), -most, most).astype(kind)


def setup_inputs(seed: int = 0) -> dict:
    arg_keys = jax.random.split(jax.random.key(seed), 9)
    cotangent = bell_draw(arg_keys[0], (TOKENS, D), (TOKENS // 256) ** -0.5, 1.5, ((0, 32),))
    hidden = bell_draw_with(arg_keys[1], (TOKENS, TOP, H), 1.0, 6.0, ((0, 32),), (0, 2, 32, 2.75))
    probs = jnp.clip(jnp.exp(math.log(0.5) - 3.218876 * jax.random.uniform(arg_keys[2], (TOKENS, TOP), jnp.float32) ** shard_levels(arg_keys[2], (TOKENS, TOP), ((0, 32),), -0.2, 0.2)), 0.02, 0.5)
    expert_ids_keys = jax.random.split(jax.random.fold_in(arg_keys[3], 1), TOKENS // TOK_DEV)
    expert_ids_turns = jax.random.permutation(jax.random.fold_in(arg_keys[3], 3), TOKENS // TOK_DEV)
    expert_ids = jax.vmap(lambda own, number: routed_block(jax.random.fold_in(arg_keys[3], 2), own, number, TOK_DEV, EXPERTS, TOP, CAP, 0))(expert_ids_keys, expert_ids_turns).reshape((TOKENS, TOP))
    secondary = bell_draw(arg_keys[4], (H, EXPERTS, D), H ** -0.5, 0.3125, ((1, 16),))
    weight = bell_draw(arg_keys[5], (H, EXPERTS, D), H ** -0.5, 0.3125, ((0, 2), (1, 16)), jnp.float32)
    moment1 = bell_draw(arg_keys[6], (H, EXPERTS, D), 0.5, 4.0, ((0, 2), (1, 16)), jnp.float32)
    moment2 = jnp.clip(jnp.exp(math.log(2.0) - 3.6888794 * jax.random.uniform(arg_keys[7], (H, EXPERTS, D), jnp.float32) ** shard_levels(arg_keys[7], (H, EXPERTS, D), ((0, 2), (1, 16)), -0.2, 0.2)), 0.05, 2.0)
    return dict(cotangent=cotangent, hidden=hidden, probs=probs, expert_ids=expert_ids, secondary=secondary, weight=weight, moment1=moment1, moment2=moment2)


beta_one = 0.9
beta_two = 0.95
adam_epsilon = 1e-08
learn_rate = 0.003
decay_rate = 0.1
bias_one = 1.0 - 0.9 ** 20
bias_two = 1.0 - 0.95 ** 20

def slot_table(flat_ids):
    count = flat_ids.shape[0]
    onehot = (jnp.arange(EXPERTS, dtype=jnp.int32)[:, None] == flat_ids[None, :]).astype(jnp.int32)
    ranking = jnp.cumsum(onehot, axis=1) - onehot
    position = lax.optimization_barrier(jnp.sum(ranking * onehot, axis=0))
    target = flat_ids * CAP + position
    order = jnp.arange(count, dtype=jnp.int32)
    inverse = jnp.zeros((EXPERTS * CAP,), jnp.int32).at[target].set(order)
    filled = jnp.zeros((EXPERTS * CAP,), jnp.int32).at[target].set(1)
    return (target, inverse, filled)

def reference(cotangent, hidden, probs, expert_ids, secondary, weight, moment1, moment2):
    span = N_INNER * TOK_DEV
    per_device = TOK_DEV * TOP
    second_f = secondary.astype(jnp.float32)

    def group(total, index):
        start = (index * span).astype(jnp.int32)
        cot_rows = lax.dynamic_slice_in_dim(cotangent, start, span, 0).astype(jnp.float32)
        hid_rows = lax.dynamic_slice_in_dim(hidden, start, span, 0)
        prob_rows = lax.dynamic_slice_in_dim(probs, start, span, 0)
        id_rows = lax.dynamic_slice_in_dim(expert_ids, start, span, 0).reshape(N_INNER, per_device)
        target, inverse, filled = jax.vmap(slot_table)(id_rows)
        weighted = (prob_rows[..., None] * hid_rows.astype(jnp.float32)).astype(jnp.bfloat16)
        weighted = lax.optimization_barrier(weighted).astype(jnp.float32).reshape(N_INNER, per_device, H)
        source = jnp.arange(N_INNER, dtype=jnp.int32)[:, None]
        keep = filled.astype(jnp.float32)[..., None]
        w_slots = (weighted[source, inverse] * keep).reshape(N_INNER, EXPERTS, CAP, H)
        token_rows = source * TOK_DEV + inverse // TOP
        d_slots = (cot_rows[token_rows] * keep).reshape(N_INNER, EXPERTS, CAP, D)
        grads = jnp.einsum('jecd,hed->jech', d_slots, second_f).astype(jnp.bfloat16)
        partial_value = jnp.einsum('jech,jecd->hed', w_slots, d_slots)
        partial_value = lax.optimization_barrier(partial_value.astype(jnp.bfloat16)).astype(jnp.float32)
        back = lax.optimization_barrier(grads).astype(jnp.float32).reshape(N_INNER, EXPERTS * CAP, H)
        g_rows = back[source, target].reshape(span, TOP, H)
        d_hid = (prob_rows[..., None] * g_rows).astype(jnp.bfloat16)
        d_prob = lax.optimization_barrier(jnp.sum(hid_rows.astype(jnp.float32) * g_rows, axis=-1))
        return (total + partial_value, (d_hid, d_prob))
    grad, (d_hid, d_prob) = lax.scan(group, jnp.zeros((H, EXPERTS, D), jnp.float32), jnp.arange(N_OUTER, dtype=jnp.int32))
    d_hidden = d_hid.reshape(TOKENS, TOP, H)
    d_probs = d_prob.reshape(TOKENS, TOP)
    new_moment1 = beta_one * moment1 + (1.0 - beta_one) * grad
    new_moment2 = beta_two * moment2 + (1.0 - beta_two) * grad * grad
    update = new_moment1 / bias_one / (jnp.sqrt(new_moment2 / bias_two) + adam_epsilon) + decay_rate * weight
    new_weight = weight - learn_rate * update
    new_secondary = new_weight.astype(jnp.bfloat16)
    return (d_hidden, d_probs, new_weight, new_moment1, new_moment2, new_secondary)
```

```python
import functools

import jax
import jax.numpy as jnp
from jax import lax
from jax.experimental import pallas as pl
from jax.experimental.pallas import tpu as pltpu
from jax.sharding import PartitionSpec as P

EXPERTS = 64
CAP = 24
LANES = 128
MIB = 1 << 20


beta_one = 0.9
beta_two = 0.95
adam_epsilon = 1e-08
learn_rate = 0.003
decay_rate = 0.1
bias_one = 1.0 - 0.9**20
bias_two = 1.0 - 0.95**20

KERNEL_VMEM = 56 * MIB
ANY = pl.BlockSpec(memory_space=pl.ANY)


def slot_targets(flat_ids):
    count = flat_ids.shape[0]
    block = 128
    blocks = count // block
    onehot = (jnp.arange(EXPERTS, dtype=jnp.int32)[:, None] == flat_ids[None, :]).astype(
        jnp.bfloat16
    )
    tiles = onehot.reshape(EXPERTS, blocks, block)
    lower = (jnp.arange(block)[:, None] < jnp.arange(block)[None, :]).astype(jnp.bfloat16)
    within = jnp.einsum("ebk,kj->ebj", tiles, lower, preferred_element_type=jnp.float32)
    totals = jnp.sum(tiles.astype(jnp.float32), axis=2)
    small = (jnp.arange(blocks)[:, None] < jnp.arange(blocks)[None, :]).astype(jnp.float32)
    before = jnp.dot(totals, small, precision=lax.Precision.HIGHEST)
    ranking = (within + before[..., None]).reshape(EXPERTS, count)
    position = jnp.sum(ranking * onehot.astype(jnp.float32), axis=0).astype(jnp.int32)
    return flat_ids * CAP + position


def line_ring(length):
    return [0] + list(range(1, length, 2)) + list(range(2, length, 2))[::-1]


def ring_place(plane, length):
    return jnp.where(plane % 2 == 1, (plane + 1) // 2, (length - plane // 2) % length)


def ring_plane(place, length):
    up = 2 * place - 1
    down = 2 * (length - place)
    return jnp.where(place == 0, 0, jnp.where(up < length, up, down))


def step_perm(size, steps, flip):
    ring = line_ring(size // 4)
    after = {at: ring[(i + steps) % len(ring)] for i, at in enumerate(ring)}
    return [(i, after[i // 4] * 4 + (i % 4 ^ flip)) for i in range(size)]


def source_order(size):
    me = lax.axis_index("inner")
    length = size // 4
    steps = jnp.arange(length, dtype=jnp.int32)
    flips = jnp.arange(4, dtype=jnp.int32)
    at = ring_plane((ring_place(me // 4, length) - steps) % length, length)
    return (at[:, None] * 4 + (me % 4 ^ flips)[None, :]).reshape(size)


def gather_groups(shard, size):
    half = shard.shape[0] // 2
    length = size // 4

    def move(block, steps, flip):
        return lax.ppermute(block, "inner", step_perm(size, steps, flip))

    own, here, by_x, by_y = shard, None, None, None
    for k in range(length + 1):
        moving = {}
        if k < length - 1:
            moving["own"] = move(own, 1, 0)
        if k < length:
            moving["x"] = move(own, 0, 1)
            moving["y"] = move(own, 0, 2)
        if k > 0:
            moving["low"] = move(by_x[:half], 0, 2)
            moving["high"] = move(by_y[half:], 0, 1)
        moved = yield moving
        if k > 0:
            yield (here, by_x, by_y, moved["low"], moved["high"])
        else:
            yield None
        here, own = own, moved.get("own")
        by_x, by_y = moved.get("x"), moved.get("y")


def grads_kernel(order, match, a, x, y, low, high, by_expert, *refs):
    d_out, g_all, match_in, rows, weights, d_rows, grads, sems = refs[-8:]
    experts, width, features = by_expert.shape
    count = d_out.shape[0] // experts
    pieces = (a, x, y, low, high)
    loads, at = [], 0
    for piece in pieces:
        loads.append((piece, rows.at[pl.ds(at, piece.shape[0])]))
        at += piece.shape[0]
    loads.append((match, match_in))
    loads += [(by_expert.at[e], weights.at[e]) for e in range(experts)]
    loads = [pltpu.make_async_copy(s, d, sems.at[i]) for i, (s, d) in enumerate(loads)]
    for load in loads:
        load.start()
    for load in loads[:6]:
        load.wait()
    step = min(512, features)
    for at in range(0, features, step):
        d_rows[:, at : at + step] = jnp.dot(
            match_in[...], rows[:, at : at + step], preferred_element_type=jnp.float32
        ).astype(jnp.bfloat16)
    first = 6 + experts
    stores = [pltpu.make_async_copy(d_rows, d_out, sems.at[first])]
    stores[0].start()
    parts = []
    for e in range(experts):
        loads[6 + e].wait()
        parts.append(
            lax.dot_general(
                d_rows[e * count : (e + 1) * count],
                weights[e],
                (((1,), (1,)), ((), ())),
                preferred_element_type=jnp.float32,
            )
        )
    for c in range(4):
        mine = [p[c * CAP : (c + 1) * CAP] for p in parts]
        grads[c] = jnp.concatenate(mine, axis=0).astype(jnp.bfloat16)
        store = pltpu.make_async_copy(grads.at[c], g_all.at[order[c]], sems.at[first + 1 + c])
        store.start()
        stores.append(store)
    for store in stores:
        store.wait()


def chunk_grads(order, match, part, by_expert, g_all, size):
    experts, width, features = by_expert.shape
    count, tokens = match.shape
    before = [] if g_all is None else [g_all]
    return pl.pallas_call(
        grads_kernel,
        out_shape=(
            jax.ShapeDtypeStruct((count, features), jnp.bfloat16),
            jax.ShapeDtypeStruct((size, experts * CAP, width), jnp.bfloat16),
        ),
        in_specs=[pl.BlockSpec(memory_space=pltpu.SMEM)] + [ANY] * (7 + len(before)),
        out_specs=(ANY, ANY),
        scratch_shapes=[
            pltpu.VMEM((count, tokens), jnp.bfloat16),
            pltpu.VMEM((tokens, features), jnp.bfloat16),
            pltpu.VMEM(by_expert.shape, jnp.bfloat16),
            pltpu.VMEM((count, features), jnp.bfloat16),
            pltpu.VMEM((4, experts * CAP, width), jnp.bfloat16),
            pltpu.SemaphoreType.DMA((11 + experts,)),
        ],
        input_output_aliases={8: 1} if before else {},
        compiler_params=pltpu.CompilerParams(vmem_limit_bytes=KERNEL_VMEM),
        cost_estimate=pl.CostEstimate(
            flops=2 * count * features * (tokens + width),
            bytes_accessed=2 * (by_expert.size + 2 * tokens * features),
            transcendentals=0,
        ),
    )(order, match, *part, by_expert, *before)


def partial_kernel(weighted, *refs):
    blocks, (out, w_in, rows, sums, sems) = refs[:-5], refs[-5:]
    experts, _, features = out.shape
    count = blocks[0].shape[0] // experts
    first = pltpu.make_async_copy(weighted, w_in, sems.at[0])
    first.start()
    loads = []
    for e in range(experts):
        for k, block in enumerate(blocks):
            loads.append(
                pltpu.make_async_copy(
                    block.at[pl.ds(e * count, count)],
                    rows.at[e, pl.ds(k * count, count)],
                    sems.at[len(loads) + 1],
                )
            )
            loads[-1].start()
    first.wait()
    stores = []
    step = min(1024, features)
    for e in range(experts):
        for load in loads[e * len(blocks) : (e + 1) * len(blocks)]:
            load.wait()
        for at in range(0, features, step):
            sums[e, :, at : at + step] = jnp.dot(
                w_in[e], rows[e, :, at : at + step], preferred_element_type=jnp.float32
            ).astype(jnp.bfloat16)
        store = pltpu.make_async_copy(sums.at[e], out.at[e], sems.at[len(loads) + 1 + e])
        store.start()
        stores.append(store)
    for store in stores:
        store.wait()


def partial_rows(weighted, blocks):
    experts, rows, slots = weighted.shape
    features = blocks[0].shape[1]
    return pl.pallas_call(
        partial_kernel,
        out_shape=jax.ShapeDtypeStruct((experts, rows, features), jnp.bfloat16),
        in_specs=[ANY] * (1 + len(blocks)),
        out_specs=ANY,
        scratch_shapes=[
            pltpu.VMEM(weighted.shape, jnp.bfloat16),
            pltpu.VMEM((experts, slots, features), jnp.bfloat16),
            pltpu.VMEM((experts, rows, features), jnp.bfloat16),
            pltpu.SemaphoreType.DMA((experts * (len(blocks) + 1) + 1,)),
        ],
        compiler_params=pltpu.CompilerParams(vmem_limit_bytes=KERNEL_VMEM),
        cost_estimate=pl.CostEstimate(
            flops=2 * weighted.size * features,
            bytes_accessed=2 * (experts * rows + experts * slots) * features,
            transcendentals=0,
        ),
    )(weighted, *blocks)


def adam_kernel(count, at, *refs):
    del at
    partials, (w, m1, m2, new_w, new_m1, new_m2, copy, full, grad) = refs[:count], refs[count:]
    experts, rows, features = partials[0].shape
    tiles = features // LANES
    for e in range(experts):
        total = partials[0][e].astype(jnp.float32)
        for part in partials[1:]:
            total = total + part[e].astype(jnp.float32)
        for t in range(tiles):
            grad[pl.ds(t * experts + e, rows, stride=tiles * experts), :] = total[
                :, t * LANES : (t + 1) * LANES
            ]
    g = grad[...]
    one = beta_one * m1[...] + (1.0 - beta_one) * g
    two = beta_two * m2[...] + (1.0 - beta_two) * g * g
    new_m1[...] = one
    new_m2[...] = two
    old = w[...]
    update = one * (1.0 / bias_one) / (jnp.sqrt(two * (1.0 / bias_two)) + adam_epsilon)
    new = old - learn_rate * (update + decay_rate * old)
    new_w[...] = new
    copy[...] = new.astype(jnp.bfloat16)
    full[...] = new.astype(jnp.bfloat16)


def adam_rows(at, partials, w, m1, m2, total_rows):
    experts, rows, features = partials[0].shape
    block = 16
    steps = rows // block
    flat = block * experts * features // LANES
    count = len(partials)
    part = pl.BlockSpec((experts, block, features), lambda i, at: (0, i, 0))
    line = pl.BlockSpec((flat, LANES), lambda i, at: (i, 0))
    placed = pl.BlockSpec((flat, LANES), lambda i, at: (at[0] * steps + i, 0))
    return pl.pallas_call(
        functools.partial(adam_kernel, count),
        grid_spec=pltpu.PrefetchScalarGridSpec(
            num_scalar_prefetch=1,
            grid=(steps,),
            in_specs=[part] * count + [line] * 3,
            out_specs=[line] * 4 + [placed],
            scratch_shapes=[pltpu.VMEM((flat, LANES), jnp.float32)],
        ),
        out_shape=[jax.ShapeDtypeStruct(w.shape, jnp.float32)] * 3
        + [
            jax.ShapeDtypeStruct(w.shape, jnp.bfloat16),
            jax.ShapeDtypeStruct((total_rows, LANES), jnp.bfloat16),
        ],
        compiler_params=pltpu.CompilerParams(vmem_limit_bytes=KERNEL_VMEM),
        cost_estimate=pl.CostEstimate(
            flops=20 * w.size, bytes_accessed=32 * w.size, transcendentals=2 * w.size
        ),
    )(at, *partials, w, m1, m2)


def place_kernel(owner, got, full, out):
    del owner, full
    out[...] = got[...]


def place_rows(owner, got, full):
    block = min(got.shape[0], 3072)
    steps = got.shape[0] // block
    return pl.pallas_call(
        place_kernel,
        grid_spec=pltpu.PrefetchScalarGridSpec(
            num_scalar_prefetch=1,
            grid=(steps,),
            in_specs=[pl.BlockSpec((block, LANES), lambda i, at: (i, 0)), ANY],
            out_specs=pl.BlockSpec((block, LANES), lambda i, at: (at[0] * steps + i, 0)),
        ),
        out_shape=jax.ShapeDtypeStruct(full.shape, full.dtype),
        input_output_aliases={2: 0},
        compiler_params=pltpu.CompilerParams(vmem_limit_bytes=KERNEL_VMEM),
        cost_estimate=pl.CostEstimate(flops=0, bytes_accessed=4 * got.size, transcendentals=0),
    )(owner, got, full)


def finish_kernel(target, probs, hidden, rows, d_hidden, d_probs):
    choices, width = hidden.shape
    slots = rows.shape[0]
    places = lax.broadcasted_iota(jnp.int32, (choices, slots), 1)
    onehot = jnp.where(places == target[...], 1.0, 0.0).astype(jnp.bfloat16)
    g = jnp.dot(onehot, rows[...], preferred_element_type=jnp.float32)
    d_hidden[...] = (probs[...] * g).astype(jnp.bfloat16)
    d_probs[...] = lax.dot_general(
        jnp.ones((8, width), jnp.float32),
        hidden[...].astype(jnp.float32) * g,
        (((1,), (1,)), ((), ())),
        precision=lax.Precision.HIGHEST,
        preferred_element_type=jnp.float32,
    )


def finish(target, probs, hidden, back):
    choices, width = hidden.shape
    slots = back.shape[0]
    step = 256
    column = pl.BlockSpec((step, 1), lambda i: (i, 0))
    block = pl.BlockSpec((step, width), lambda i: (i, 0))
    return pl.pallas_call(
        finish_kernel,
        grid=(choices // step,),
        out_shape=(
            jax.ShapeDtypeStruct((choices, width), jnp.bfloat16),
            jax.ShapeDtypeStruct((8, choices), jnp.float32),
        ),
        in_specs=[column, column, block, pl.BlockSpec((slots, width), lambda i: (0, 0))],
        out_specs=(block, pl.BlockSpec((8, step), lambda i: (0, i))),
        compiler_params=pltpu.CompilerParams(vmem_limit_bytes=KERNEL_VMEM),
        cost_estimate=pl.CostEstimate(
            flops=2 * choices * slots * width, bytes_accessed=8 * hidden.size, transcendentals=0
        ),
    )(target, probs, hidden, back)


def lane_view(array):
    h, e, d = array.shape
    return array.reshape(h, e, d // LANES, LANES).transpose(0, 2, 1, 3).reshape(-1, LANES)


def lane_unview(rows, shape):
    h, e, d = shape
    return rows.reshape(h, d // LANES, e, LANES).transpose(0, 2, 1, 3).reshape(shape)


def local(cotangent, hidden, probs, expert_ids, secondary, weight, moment1, moment2):
    token_count = cotangent.shape[0]
    top_k = expert_ids.shape[1]
    hidden_width = hidden.shape[2]
    experts = secondary.shape[1]
    size = lax.axis_size("inner")
    length = size // 4
    outer_size = lax.axis_size("outer")
    outer_at = lax.axis_index("outer")
    choices = token_count * top_k
    slots = experts * CAP
    rows = weight.shape[0]

    flat_ids = expert_ids.reshape(choices)
    target = slot_targets(flat_ids)
    all_slots = jnp.arange(EXPERTS * CAP, dtype=jnp.int32)
    matches = (all_slots[:, None] == target[None, :]).astype(jnp.bfloat16)
    weighted = (
        (probs[..., None] * hidden.astype(jnp.float32))
        .astype(jnp.bfloat16)
        .reshape(choices, hidden_width)
    )
    w_send = jnp.dot(matches, weighted, preferred_element_type=jnp.float32).astype(jnp.bfloat16)
    w_send = w_send.reshape(size, slots, hidden_width)
    number = (jnp.arange(choices, dtype=jnp.int32) // top_k + 1).astype(jnp.bfloat16)
    token_at = jnp.dot(matches, number[:, None], preferred_element_type=jnp.float32)
    token_at = token_at.astype(jnp.bfloat16).reshape(size, 1, slots)
    token_at = jnp.pad(token_at, ((0, 0), (0, 7), (0, hidden_width - slots)))
    w_send = jnp.concatenate([w_send, token_at], axis=1)
    by_expert = jnp.transpose(secondary, (1, 0, 2))
    columns = (target[:, None], probs.reshape(choices, 1))
    order = source_order(size).reshape(length, 4)
    g_all = None

    def prepare(w_recv):
        w_recv = jnp.take(w_recv, order.reshape(size), axis=0)
        slot_token = w_recv[:, slots, :slots].astype(jnp.int32).reshape(length, 4, experts, CAP)
        first = token_count * jnp.arange(4, dtype=jnp.int32)[None, :, None, None] - 1
        slot_row = jnp.where(slot_token > 0, slot_token + first, -1)
        slot_row = slot_row.transpose(0, 2, 1, 3).reshape(length, 4 * slots)
        tokens = jnp.arange(4 * token_count, dtype=jnp.int32)
        match = [(slot_row[k][:, None] == tokens).astype(jnp.bfloat16) for k in range(length)]
        w_slots = w_recv[:, :slots].reshape(size, experts, CAP, hidden_width)
        w_slots = w_slots.transpose(1, 3, 0, 2).reshape(experts, hidden_width, size * CAP)
        owners = [
            lax.dynamic_slice_in_dim(w_slots, (outer_at + r) % outer_size * rows, rows, 1)
            for r in range(outer_size)
        ]
        return match, owners

    groups = gather_groups(cotangent, size)
    parts, d_rows = [], []
    for k in range(length + 1):
        moving = next(groups)
        if k == 0:
            moving, w_send = lax.optimization_barrier((moving, w_send))
            w_recv = lax.all_to_all(w_send, "inner", split_axis=0, concat_axis=0, tiled=True)
        elif k == 1:
            moving, by_expert, columns = lax.optimization_barrier((moving, by_expert, columns))
        elif k >= 3:
            if k == 3:
                match, owners = prepare(w_recv)
            for j in (k - 3,) if k < length else (k - 3, k - 2):
                d_chunk, g_all = chunk_grads(order[j], match[j], parts[j], by_expert, g_all, size)
                d_rows.append(d_chunk)
            moving, d_rows, g_all, match, owners = lax.optimization_barrier(
                (moving, d_rows, g_all, match, owners)
            )
        part = groups.send(moving)
        if part is not None:
            parts.append(part)
    last = length - 1
    d_chunk, g_all = chunk_grads(order[last], match[last], parts[last], by_expert, g_all, size)
    d_rows.append(d_chunk)
    back = lax.all_to_all(g_all, "inner", split_axis=0, concat_axis=0, tiled=True)

    def outer_perm(steps):
        return [(i, (i + steps) % outer_size) for i in range(outer_size)]

    partials = []
    for r in range(1, outer_size):
        sent = partial_rows(owners[r], d_rows)
        partials.append(lax.ppermute(sent, "outer", outer_perm(r)))
    partials.append(partial_rows(owners[0], d_rows))

    new_weight, new_moment1, new_moment2, copy, full = adam_rows(
        outer_at.astype(jnp.int32)[None],
        partials,
        lane_view(weight),
        lane_view(moment1),
        lane_view(moment2),
        secondary.size // LANES,
    )
    for r in range(1, outer_size):
        got = lax.ppermute(copy, "outer", outer_perm(r))
        owner = (outer_at + outer_size - r) % outer_size
        full = place_rows(owner.astype(jnp.int32)[None], got, full)

    d_hidden, d_probs = finish(
        *columns,
        hidden.reshape(choices, hidden_width),
        back.reshape(size * slots, hidden_width),
    )
    return (
        d_hidden.reshape(hidden.shape),
        d_probs[0].reshape(probs.shape),
        lane_unview(new_weight, weight.shape),
        lane_unview(new_moment1, weight.shape),
        lane_unview(new_moment2, weight.shape),
        lane_unview(full, secondary.shape),
    )


def solution(mesh):
    in_specs = (
        P(("outer", "inner"), None),
        P(("outer", "inner"), None, None),
        P(("outer", "inner"), None),
        P(("outer", "inner"), None),
        P(None, "inner", None),
        P("outer", "inner", None),
        P("outer", "inner", None),
        P("outer", "inner", None),
    )
    out_specs = (
        P(("outer", "inner"), None, None),
        P(("outer", "inner"), None),
        P("outer", "inner", None),
        P("outer", "inner", None),
        P("outer", "inner", None),
        P(None, "inner", None),
    )
    return jax.shard_map(local, mesh=mesh, in_specs=in_specs, out_specs=out_specs, check_vma=False)
```

```python
import functools
import math

import jax
import jax.numpy as jnp
from jax import lax
from jax.experimental import pallas as pl
from jax.experimental.pallas import tpu as pltpu
from jax.sharding import PartitionSpec as P

EXPERTS = 64
CAP = 24
TOP = 8
LANES = 128
MIB = 1 << 20


beta_one = 0.9
beta_two = 0.95
adam_epsilon = 1e-08
learn_rate = 0.003
decay_rate = 0.1
bias_one = 1.0 - 0.9**20
bias_two = 1.0 - 0.95**20

HBM = pl.BlockSpec(memory_space=pltpu.HBM)
INSIDE = pl.BlockSpec(memory_space=pltpu.VMEM)


def slot_targets(flat_ids):
    count = flat_ids.shape[0]
    block = 128
    blocks = count // block
    onehot = (jnp.arange(EXPERTS, dtype=jnp.int32)[:, None] == flat_ids[None, :]).astype(
        jnp.bfloat16
    )
    tiles = onehot.reshape(EXPERTS, blocks, block)
    lower = (jnp.arange(block)[:, None] < jnp.arange(block)[None, :]).astype(jnp.bfloat16)
    within = jnp.einsum("ebk,kj->ebj", tiles, lower, preferred_element_type=jnp.float32)
    totals = jnp.sum(tiles.astype(jnp.float32), axis=2)
    small = (jnp.arange(blocks)[:, None] < jnp.arange(blocks)[None, :]).astype(jnp.float32)
    before = jnp.dot(totals, small, precision=lax.Precision.HIGHEST)
    ranking = (within + before[..., None]).reshape(EXPERTS, count)
    position = jnp.sum(ranking * onehot.astype(jnp.float32), axis=0).astype(jnp.int32)
    return flat_ids * CAP + position


def line_ring(length):
    return [0] + list(range(1, length, 2)) + list(range(2, length, 2))[::-1]


def ring_place(plane, length):
    return jnp.where(plane % 2 == 1, (plane + 1) // 2, (length - plane // 2) % length)


def ring_plane(place, length):
    up = 2 * place - 1
    down = 2 * (length - place)
    return jnp.where(place == 0, 0, jnp.where(up < length, up, down))


def step_perm(size, steps, flip):
    ring = line_ring(size // 4)
    after = {at: ring[(i + steps) % len(ring)] for i, at in enumerate(ring)}
    return [(i, after[i // 4] * 4 + (i % 4 ^ flip)) for i in range(size)]


def source_order(size):
    me = lax.axis_index("inner")
    length = size // 4
    steps = jnp.arange(length, dtype=jnp.int32)
    flips = jnp.arange(4, dtype=jnp.int32)
    at = ring_plane((ring_place(me // 4, length) - steps) % length, length)
    return (at[:, None] * 4 + (me % 4 ^ flips)[None, :]).reshape(size)


def grads_kernel(first, a, x, y, low, high, by_expert, d_out, g_out, *scratch):
    rows, match, d_rows, grads, sems = scratch
    experts, width, features = by_expert.shape
    tokens = rows.shape[0] // 4
    slots = experts * CAP
    pieces = (a, x, y, low, high)
    loads, at = [], 0
    for i, piece in enumerate(pieces):
        place = rows.at[pl.ds(at, piece.shape[0])]
        loads.append(pltpu.make_async_copy(piece, place, sems.at[i]))
        loads[-1].start()
        at += piece.shape[0]
    for load in loads:
        load.wait()

    slot = lax.broadcasted_iota(jnp.int32, (slots, tokens), 0)
    expert = first[0] + slot // CAP
    place = (slot % CAP).astype(jnp.float32)
    expert = expert.astype(jnp.float32)
    earlier = lax.broadcasted_iota(jnp.int32, (tokens, tokens), 0)
    earlier = earlier < lax.broadcasted_iota(jnp.int32, (tokens, tokens), 1)
    earlier = jnp.where(earlier, 1.0, 0.0).astype(jnp.bfloat16)
    hits = []
    for c in range(4):
        ids = rows[c * tokens : (c + 1) * tokens, features:].astype(jnp.float32).T
        named = jnp.zeros((slots, tokens), jnp.float32)
        for k in range(TOP):
            named = jnp.where(expert == ids[k : k + 1], 1.0, named)
        rank = jnp.dot(
            named.astype(jnp.bfloat16), earlier, preferred_element_type=jnp.float32
        )
        hits.append(jnp.where(rank == place, named, 0.0))
    blank = jnp.zeros((CAP, tokens), jnp.float32)
    lines = []
    for e in range(experts):
        for c in range(4):
            line = [blank] * 4
            line[c] = hits[c][e * CAP : (e + 1) * CAP]
            lines.append(jnp.concatenate(line, axis=1))
    match[...] = jnp.concatenate(lines, axis=0).astype(jnp.bfloat16)

    step = min(512, features)
    for at in range(0, features, step):
        d_rows[:, at : at + step] = jnp.dot(
            match[...], rows[:, at : at + step], preferred_element_type=jnp.float32
        ).astype(jnp.bfloat16)
    stores = [pltpu.make_async_copy(d_rows, d_out, sems.at[5])]
    stores[0].start()
    count = 4 * CAP
    found = [
        lax.dot_general(
            d_rows[e * count : (e + 1) * count],
            by_expert[e],
            (((1,), (1,)), ((), ())),
            preferred_element_type=jnp.float32,
        )
        for e in range(experts)
    ]
    for c in range(4):
        mine = [f[c * CAP : (c + 1) * CAP] for f in found]
        grads[c] = jnp.concatenate(mine, axis=0).astype(jnp.bfloat16)
    stores.append(pltpu.make_async_copy(grads, g_out, sems.at[6]))
    stores[1].start()
    for store in stores:
        store.wait()


def chunk_grads(first, part, by_expert):
    experts, width, features = by_expert.shape
    tokens, columns = part[0].shape
    slots = experts * CAP
    return pl.pallas_call(
        grads_kernel,
        out_shape=(
            jax.ShapeDtypeStruct((4 * slots, features), jnp.bfloat16),
            jax.ShapeDtypeStruct((4, slots, width), jnp.bfloat16),
        ),
        in_specs=[pl.BlockSpec(memory_space=pltpu.SMEM)]
        + [HBM] * 5
        + [INSIDE],
        out_specs=(HBM, HBM),
        scratch_shapes=[
            pltpu.VMEM((4 * tokens, columns), jnp.bfloat16),
            pltpu.VMEM((4 * slots, 4 * tokens), jnp.bfloat16),
            pltpu.VMEM((4 * slots, features), jnp.bfloat16),
            pltpu.VMEM((4, slots, width), jnp.bfloat16),
            pltpu.SemaphoreType.DMA((7,)),
        ],
        compiler_params=pltpu.CompilerParams(vmem_limit_bytes=14 * MIB),
        cost_estimate=pl.CostEstimate(
            flops=8 * slots * features * (4 * tokens + width),
            bytes_accessed=8 * (slots + tokens) * features,
            transcendentals=0,
        ),
    )(first, *part, by_expert)


def order_kernel(pieces, *refs):
    arrays, (out, rows, wide, turned, sems) = refs[:-5], refs[-5:]
    size, slots, width = rows.shape
    experts = slots // CAP
    loads = [
        pltpu.make_async_copy(arrays[a].at[i], rows.at[n], sems.at[n])
        for n, (a, i) in enumerate(pieces)
    ]
    for load in loads:
        load.start()
    for n, load in enumerate(loads):
        load.wait()
        wide[n] = rows[n].astype(jnp.float32)
    for e in range(experts):
        mine = [wide[n, e * CAP : (e + 1) * CAP] for n in range(size)]
        turned[e] = jnp.concatenate(mine, axis=0).T.astype(jnp.bfloat16)
    store = pltpu.make_async_copy(turned, out, sems.at[size])
    store.start()
    store.wait()


def order_slots(arrays, pieces):
    slots, width = arrays[0].shape[1:]
    size = len(pieces)
    shape = (slots // CAP, width, size * CAP)
    return pl.pallas_call(
        functools.partial(order_kernel, pieces),
        out_shape=jax.ShapeDtypeStruct(shape, jnp.bfloat16),
        in_specs=[HBM] * len(arrays),
        out_specs=HBM,
        scratch_shapes=[
            pltpu.VMEM((size, slots, width), jnp.bfloat16),
            pltpu.VMEM((size, slots, width), jnp.float32),
            pltpu.VMEM(shape, jnp.bfloat16),
            pltpu.SemaphoreType.DMA((size + 1,)),
        ],
        compiler_params=pltpu.CompilerParams(vmem_limit_bytes=10 * MIB),
        cost_estimate=pl.CostEstimate(
            flops=0, bytes_accessed=8 * size * slots * width, transcendentals=0
        ),
    )(*arrays)


def regroup_kernel(*refs):
    count = len(refs) - 5
    arrays, outs, (held, sems) = refs[:count], refs[count:-2], refs[-2:]
    loads = [
        pltpu.make_async_copy(a.at[pl.ds(1, 3)], held.at[k], sems.at[k])
        for k, a in enumerate(arrays)
    ]
    for load in loads:
        load.start()
    for load in loads:
        load.wait()
    stores = [
        pltpu.make_async_copy(held.at[:, c], out, sems.at[count + c])
        for c, out in enumerate(outs)
    ]
    for store in stores:
        store.start()
    for store in stores:
        store.wait()


def regroup(arrays):
    _, slots, width = arrays[0].shape
    count = len(arrays)
    return pl.pallas_call(
        regroup_kernel,
        out_shape=[jax.ShapeDtypeStruct((count, slots, width), jnp.bfloat16)] * 3,
        in_specs=[HBM] * count,
        out_specs=[HBM] * 3,
        scratch_shapes=[
            pltpu.VMEM((count, 3, slots, width), jnp.bfloat16),
            pltpu.SemaphoreType.DMA((count + 3,)),
        ],
        compiler_params=pltpu.CompilerParams(vmem_limit_bytes=6 * MIB),
        cost_estimate=pl.CostEstimate(
            flops=0, bytes_accessed=12 * count * slots * width, transcendentals=0
        ),
    )(*arrays)


def partial_kernel(owners, weighted, *refs):
    count = owners.shape[0]
    blocks, outs = refs[: -4 - count], refs[-4 - count : -4]
    w_in, rows, sums, sems = refs[-4:]
    experts, width, features = sums.shape
    share = width // count
    slots = blocks[0].shape[0] // experts
    loads = []
    for e in range(experts):
        mine = [(weighted.at[e], w_in.at[e])] + [
            (block.at[pl.ds(e * slots, slots)], rows.at[e, pl.ds(k * slots, slots)])
            for k, block in enumerate(blocks)
        ]
        loads.append(
            [
                pltpu.make_async_copy(source, place, sems.at[e, i])
                for i, (source, place) in enumerate(mine)
            ]
        )
    stores = []
    step = min(1024, features)
    for load in loads[0]:
        load.start()
    for e in range(experts):
        if e + 1 < experts:
            for load in loads[e + 1]:
                load.start()
        for load in loads[e]:
            load.wait()
        for at in range(0, features, step):
            sums[e, :, at : at + step] = jnp.dot(
                w_in[e], rows[e, :, at : at + step], preferred_element_type=jnp.float32
            ).astype(jnp.bfloat16)
        for r, out in enumerate(outs):
            at = pl.multiple_of(owners[r] * share, share)
            store = pltpu.make_async_copy(
                sums.at[e, pl.ds(at, share)], out.at[e], sems.at[e, len(blocks) + 1 + r]
            )
            store.start()
            stores.append(store)
    for store in stores:
        store.wait()


def partial_rows(owners, weighted, blocks):
    experts, width, slots = weighted.shape
    features = blocks[0].shape[1]
    count = owners.shape[0]
    return pl.pallas_call(
        partial_kernel,
        out_shape=[jax.ShapeDtypeStruct((experts, width // count, features), jnp.bfloat16)]
        * count,
        in_specs=[pl.BlockSpec(memory_space=pltpu.SMEM)] + [HBM] * (1 + len(blocks)),
        out_specs=[HBM] * count,
        scratch_shapes=[
            pltpu.VMEM((experts, width, slots), jnp.bfloat16),
            pltpu.VMEM((experts, slots, features), jnp.bfloat16),
            pltpu.VMEM((experts, width, features), jnp.bfloat16),
            pltpu.SemaphoreType.DMA((experts, 1 + len(blocks) + count)),
        ],
        compiler_params=pltpu.CompilerParams(vmem_limit_bytes=20 * MIB),
        cost_estimate=pl.CostEstimate(
            flops=2 * experts * width * slots * features,
            bytes_accessed=2 * experts * (width + slots) * features,
            transcendentals=0,
        ),
    )(owners, weighted, *blocks)


def root_of(x):
    inverse = lax.rsqrt(x)
    root = x * inverse
    return root + 0.5 * inverse * (x - root * root)


def reciprocal(x):
    estimate = pl.reciprocal(x, approx=True)
    return estimate * (2.0 - x * estimate)


def adam_kernel(count, kept, first, at, *refs):
    del at
    partials, (w, m1, m2) = refs[:count], refs[count : count + 3]
    new_w, new_m1, new_m2, full, copy, grad = refs[count + 3 + kept :]
    experts, rows, features = partials[0].shape
    tiles = features // LANES
    for e in range(experts):
        total = partials[0][e].astype(jnp.float32)
        for part in partials[1:]:
            total = total + part[e].astype(jnp.float32)
        for t in range(tiles):
            grad[pl.ds(t * experts + e, rows, stride=tiles * experts), :] = total[
                :, t * LANES : (t + 1) * LANES
            ]
    block = grad.shape[0]
    base = pl.multiple_of((first + pl.program_id(0)) * block, block)
    for start in range(0, block, 128):
        here = slice(start, start + 128)
        there = pl.ds(base + start, 128)
        g = grad[here]
        one = beta_one * m1[there] + (1.0 - beta_one) * g
        two = beta_two * m2[there] + (1.0 - beta_two) * g * g
        new_m1[here] = one
        new_m2[here] = two
        old = w[there]
        root = reciprocal(root_of(two * (1.0 / bias_two)) + adam_epsilon)
        new = old - learn_rate * (one * (1.0 / bias_one) * root + decay_rate * old)
        new_w[here] = new
        copy[here] = new.astype(jnp.bfloat16)
        full[here] = new.astype(jnp.bfloat16)


def adam_rows(at, partials, w, m1, m2, total_rows, before, first, steps):
    experts, rows, features = partials[0].shape
    block = 16
    flat = block * experts * features // LANES
    count, kept = len(partials), len(before)
    whole = rows // block
    part = pl.BlockSpec((experts, block, features), lambda i, at: (0, first + i, 0))
    line = pl.BlockSpec((flat, LANES), lambda i, at: (first + i, 0))
    placed = pl.BlockSpec((flat, LANES), lambda i, at: (at[0] * whole + first + i, 0))
    return pl.pallas_call(
        functools.partial(adam_kernel, count, kept, first),
        grid_spec=pltpu.PrefetchScalarGridSpec(
            num_scalar_prefetch=1,
            grid=(steps,),
            in_specs=[part] * count + [INSIDE] * 3 + [HBM] * kept,
            out_specs=[line] * 3 + [placed, pl.BlockSpec((flat, LANES), lambda i, at: (i, 0))],
            scratch_shapes=[pltpu.VMEM((flat, LANES), jnp.float32)],
        ),
        out_shape=[jax.ShapeDtypeStruct(w.shape, jnp.float32)] * 3
        + [
            jax.ShapeDtypeStruct((total_rows, LANES), jnp.bfloat16),
            jax.ShapeDtypeStruct((steps * flat, LANES), jnp.bfloat16),
        ],
        input_output_aliases={4 + count + i: i for i in range(kept)},
        compiler_params=pltpu.CompilerParams(vmem_limit_bytes=10 * MIB),
        cost_estimate=pl.CostEstimate(
            flops=20 * steps * flat * LANES,
            bytes_accessed=20 * steps * flat * LANES,
            transcendentals=0,
        ),
    )(at, *partials, w, m1, m2, *before)


def place_kernel(cut, at, low, high, full, out):
    del at, full
    here = pl.program_id(0)

    @pl.when(here < cut)
    def _():
        out[...] = low[...]

    @pl.when(here >= cut)
    def _():
        out[...] = high[...]


def place_rows(owner, low, high, full):
    block = math.gcd(low.shape[0], high.shape[0])
    cut = low.shape[0] // block
    steps = cut + high.shape[0] // block
    shape = (block, LANES)
    return pl.pallas_call(
        functools.partial(place_kernel, cut),
        grid_spec=pltpu.PrefetchScalarGridSpec(
            num_scalar_prefetch=1,
            grid=(steps,),
            in_specs=[
                pl.BlockSpec(shape, lambda i, at: (jnp.minimum(i, cut - 1), 0)),
                pl.BlockSpec(shape, lambda i, at: (jnp.maximum(i - cut, 0), 0)),
                HBM,
            ],
            out_specs=pl.BlockSpec(shape, lambda i, at: (at[0] * steps + i, 0)),
        ),
        out_shape=jax.ShapeDtypeStruct(full.shape, full.dtype),
        input_output_aliases={3: 0},
        compiler_params=pltpu.CompilerParams(vmem_limit_bytes=14 * MIB),
        cost_estimate=pl.CostEstimate(
            flops=0, bytes_accessed=4 * (low.size + high.size), transcendentals=0
        ),
    )(owner, low, high, full)


def finish_kernel(pieces, target, probs, hidden, *refs):
    back, (d_hidden, d_probs, rows, states, outs, sums, sems) = refs[:-7], refs[-7:]
    count = back[0].shape[1]
    choices, width = hidden.shape
    slots = rows.shape[0]
    loads = [
        pltpu.make_async_copy(back[a].at[i], rows.at[pl.ds(n * count, count)], sems.at[n])
        for n, (a, i) in enumerate(pieces)
    ]
    loads.append(pltpu.make_async_copy(hidden, states, sems.at[len(pieces)]))
    for load in loads:
        load.start()
    targets, scales = target[...].T, probs[...].T
    for load in loads:
        load.wait()
    ones = jnp.ones((8, width), jnp.bfloat16)
    across = (((1,), (1,)), ((), ()))
    step = 2 * LANES
    stores = []
    for n, at in enumerate(range(0, choices, step)):
        here = slice(at, at + step)

        def column(table):
            return jnp.concatenate([table[:, 2 * n : 2 * n + 1], table[:, 2 * n + 1 : 2 * n + 2]])

        places = lax.broadcasted_iota(jnp.int32, (step, slots), 1)
        onehot = jnp.where(places == column(targets).astype(jnp.int32), 1.0, 0.0)
        g = jnp.dot(onehot.astype(jnp.bfloat16), rows[...], preferred_element_type=jnp.float32)
        outs[here] = (column(scales) * g).astype(jnp.bfloat16)
        stores.append(
            pltpu.make_async_copy(outs.at[here], d_hidden.at[here], sems.at[len(loads) + n])
        )
        stores[n].start()
        product = states[here].astype(jnp.float32) * g
        high = product.astype(jnp.bfloat16)
        low = (product - high.astype(jnp.float32)).astype(jnp.bfloat16)
        sums[:, here] = lax.dot_general(
            ones, high, across, preferred_element_type=jnp.float32
        ) + lax.dot_general(ones, low, across, preferred_element_type=jnp.float32)
    d_probs[...] = sums[...]
    for store in stores:
        store.wait()


def finish(target, probs, hidden, back, pieces):
    choices, width = hidden.shape
    slots = len(pieces) * back[0].shape[1]
    steps = choices // (2 * LANES)
    return pl.pallas_call(
        functools.partial(finish_kernel, pieces),
        out_shape=(
            jax.ShapeDtypeStruct((choices, width), jnp.bfloat16),
            jax.ShapeDtypeStruct((8, choices), jnp.float32),
        ),
        in_specs=[INSIDE, INSIDE] + [HBM] * (1 + len(back)),
        out_specs=(HBM, INSIDE),
        scratch_shapes=[
            pltpu.VMEM((slots, width), jnp.bfloat16),
            pltpu.VMEM((choices, width), jnp.bfloat16),
            pltpu.VMEM((choices, width), jnp.bfloat16),
            pltpu.VMEM((8, choices), jnp.float32),
            pltpu.SemaphoreType.DMA((len(pieces) + 1 + steps,)),
        ],
        compiler_params=pltpu.CompilerParams(vmem_limit_bytes=12 * MIB),
        cost_estimate=pl.CostEstimate(
            flops=2 * choices * slots * width, bytes_accessed=8 * hidden.size, transcendentals=0
        ),
    )(target, probs, hidden, *back)


def lane_view(array):
    h, e, d = array.shape
    return array.reshape(h, e, d // LANES, LANES).transpose(0, 2, 1, 3).reshape(-1, LANES)


def lane_unview(rows, shape):
    h, e, d = shape
    return rows.reshape(h, d // LANES, e, LANES).transpose(0, 2, 1, 3).reshape(shape)


def local(cotangent, hidden, probs, expert_ids, secondary, weight, moment1, moment2):
    token_count = cotangent.shape[0]
    top_k = expert_ids.shape[1]
    hidden_width = hidden.shape[2]
    experts = secondary.shape[1]
    size = lax.axis_size("inner")
    length = size // 4
    outer_size = lax.axis_size("outer")
    outer_at = lax.axis_index("outer")
    me = lax.axis_index("inner")
    choices = token_count * top_k
    slots = experts * CAP
    rows = weight.shape[0]

    flat_ids = expert_ids.reshape(choices)
    target = slot_targets(flat_ids)
    device = flat_ids // experts
    ring_steps = (ring_place(device // 4, length) - ring_place(me // 4, length)) % length
    relative = ring_steps * 4 + (device % 4 ^ me % 4)
    target = (relative - device) * slots + target
    all_slots = jnp.arange(size * slots, dtype=jnp.int32)
    matches = (all_slots[:, None] == target[None, :]).astype(jnp.bfloat16)
    weighted = (
        (probs[..., None] * hidden.astype(jnp.float32))
        .astype(jnp.bfloat16)
        .reshape(choices, hidden_width)
    )
    w_send = jnp.dot(matches, weighted, preferred_element_type=jnp.float32).astype(jnp.bfloat16)
    w_send = w_send.reshape(length, 4, slots, hidden_width)
    columns = tuple(
        v.astype(jnp.float32).reshape(choices // LANES, LANES) for v in (target, probs)
    )
    state = tuple(lane_view(a) for a in (weight, moment1, moment2))

    def move(block, steps, flip):
        return lax.ppermute(block, "inner", step_perm(size, steps, flip))

    tie = lax.optimization_barrier
    last = length - 1
    half = token_count // 2
    first = (me * experts).astype(jnp.int32)[None]
    tags = jnp.pad(expert_ids.astype(jnp.bfloat16), ((0, 0), (0, LANES - top_k)))
    own = jnp.concatenate([cotangent, tags], axis=1)
    by_expert = jnp.transpose(secondary, (1, 0, 2))
    near, parts, w_parts = {}, {}, {}
    d_rows, grads, back = {}, {}, {}

    def add_chunk(j):
        d_rows[j], grads[j] = chunk_grads(first, parts[j], by_expert)

    def flips(arrays):
        return [move(a, 0, c) for c, a in enumerate(arrays, 1)]

    def far(j):
        _, by_x, by_y = near[j]
        return (move(by_x[:half], 0, 2), move(by_y[half:], 0, 1))

    for k in range(length + 1):
        moving = {}
        if k < last:
            moving["own"] = move(own, 1, 0)
        if k < length:
            moving["x"] = move(own, 0, 1)
            moving["y"] = move(own, 0, 2)
        if k > 1:
            moving["far"] = far(k - 1)
        if k == length:
            moving["first"] = far(0)
        if k > 2:
            add_chunk(k - 2)
        if k == 0:
            moving["columns"] = columns
        if k == last - 1:
            moving["weights"] = by_expert
            w_parts[1] = move(w_send[1], 1, 0)
        if k == last:
            for j in range(last, 1, -1):
                w_parts[j] = move(w_send[j], j, 0)
        moving["done"] = (d_rows, grads, w_parts, w_send)
        if k == length:
            last_far = moving.pop("far")
            first_far = moving.pop("first")
        moved = tie(moving)
        d_rows, grads, w_parts, w_send = moved["done"]
        if k == 0:
            columns = moved["columns"]
        if k == last - 1:
            by_expert = moved["weights"]
        if k == last:
            w_parts[0] = w_send[0]
            w_arrays = [w_parts[j] for j in range(length)]
            w_flipped = flips(regroup(w_arrays))
        if 1 < k < length:
            parts[k - 1] = near[k - 1] + moved["far"]
        if k < length:
            near[k] = (own, moved["x"], moved["y"])
        own = moved.get("own")
    parts[last] = near[last] + last_far
    parts[0] = near[0] + first_far
    for j in range(1, last):
        back[j] = move(grads[j], -j, 0)
    add_chunk(last)
    back[last] = move(grads[last], -last, 0)
    add_chunk(0)
    back[0] = grads[0]
    back = [back[j] for j in range(length)]
    pieces = tuple((k, 0) if c == 0 else (length + c - 1, k) for k in range(length) for c in range(4))
    w_slots = order_slots(w_arrays + w_flipped, pieces)
    d_rows, leaving = tie(([d_rows[j] for j in range(length)], regroup(back)))
    flipped = flips(leaving)

    def outer_perm(steps):
        return [(i, (i + steps) % outer_size) for i in range(outer_size)]

    owners = (outer_at + jnp.arange(outer_size, dtype=jnp.int32)) % outer_size
    mine, *sent = partial_rows(owners, w_slots, d_rows)
    partials = [mine] + [
        lax.ppermute(part, "outer", outer_perm(r)) for r, part in enumerate(sent, 1)
    ]
    at = outer_at.astype(jnp.int32)[None]
    total_rows = secondary.size // LANES
    blocks = rows // 16
    cuts = [0, blocks // 2, blocks]
    outs, copies = [], []
    for start, stop in zip(cuts[:-1], cuts[1:]):
        if start:
            partials, flipped = tie((partials, flipped))
        *outs, copy = adam_rows(
            at, partials, *state, total_rows, outs, start, stop - start
        )
        copies.append(copy)
    sent = [
        [lax.ppermute(copy, "outer", outer_perm(r)) for r in range(1, outer_size)]
        for copy in copies
    ]
    new_weight, new_moment1, new_moment2, full = outs
    for r in range(1, outer_size):
        owner = (outer_at + outer_size - r) % outer_size
        full = place_rows(
            owner.astype(jnp.int32)[None], sent[0][r - 1], sent[1][r - 1], full
        )

    d_hidden, d_probs = finish(
        *columns, hidden.reshape(choices, hidden_width), back + flipped, pieces
    )
    return (
        d_hidden.reshape(hidden.shape),
        d_probs[0].reshape(probs.shape),
        lane_unview(new_weight, weight.shape),
        lane_unview(new_moment1, weight.shape),
        lane_unview(new_moment2, weight.shape),
        lane_unview(full, secondary.shape),
    )


def solution(mesh):
    in_specs = (
        P(("outer", "inner"), None),
        P(("outer", "inner"), None, None),
        P(("outer", "inner"), None),
        P(("outer", "inner"), None),
        P(None, "inner", None),
        P("outer", "inner", None),
        P("outer", "inner", None),
        P("outer", "inner", None),
    )
    out_specs = (
        P(("outer", "inner"), None, None),
        P(("outer", "inner"), None),
        P("outer", "inner", None),
        P("outer", "inner", None),
        P("outer", "inner", None),
        P(None, "inner", None),
    )
    return jax.shard_map(local, mesh=mesh, in_specs=in_specs, out_specs=out_specs, check_vma=False)
```

```python
import functools
import math

import jax
import jax.numpy as jnp
from jax import lax
from jax.experimental import pallas as pl
from jax.experimental.pallas import tpu as pltpu
from jax.sharding import PartitionSpec as P

EXPERTS = 64
CAP = 24
TOP = 8
LANES = 128
MIB = 1 << 20


beta_one = 0.9
beta_two = 0.95
adam_epsilon = 1e-08
learn_rate = 0.003
decay_rate = 0.1
bias_one = 1.0 - 0.9**20
bias_two = 1.0 - 0.95**20

HBM = pl.BlockSpec(memory_space=pltpu.HBM)
INSIDE = pl.BlockSpec(memory_space=pltpu.VMEM)


def slot_targets(flat_ids):
    count = flat_ids.shape[0]
    block = 128
    blocks = count // block
    onehot = (jnp.arange(EXPERTS, dtype=jnp.int32)[:, None] == flat_ids[None, :]).astype(
        jnp.bfloat16
    )
    tiles = onehot.reshape(EXPERTS, blocks, block)
    lower = (jnp.arange(block)[:, None] < jnp.arange(block)[None, :]).astype(jnp.bfloat16)
    within = jnp.einsum("ebk,kj->ebj", tiles, lower, preferred_element_type=jnp.float32)
    totals = jnp.sum(tiles.astype(jnp.float32), axis=2)
    small = (jnp.arange(blocks)[:, None] < jnp.arange(blocks)[None, :]).astype(jnp.float32)
    before = jnp.dot(totals, small, precision=lax.Precision.HIGHEST)
    ranking = (within + before[..., None]).reshape(EXPERTS, count)
    position = jnp.sum(ranking * onehot.astype(jnp.float32), axis=0).astype(jnp.int32)
    return flat_ids * CAP + position


def line_ring(length):
    return [0] + list(range(1, length, 2)) + list(range(2, length, 2))[::-1]


def ring_place(plane, length):
    return jnp.where(plane % 2 == 1, (plane + 1) // 2, (length - plane // 2) % length)


def ring_plane(place, length):
    up = 2 * place - 1
    down = 2 * (length - place)
    return jnp.where(place == 0, 0, jnp.where(up < length, up, down))


def step_perm(size, steps, flip):
    ring = line_ring(size // 4)
    after = {at: ring[(i + steps) % len(ring)] for i, at in enumerate(ring)}
    return [(i, after[i // 4] * 4 + (i % 4 ^ flip)) for i in range(size)]


def source_order(size):
    me = lax.axis_index("inner")
    length = size // 4
    steps = jnp.arange(length, dtype=jnp.int32)
    flips = jnp.arange(4, dtype=jnp.int32)
    at = ring_plane((ring_place(me // 4, length) - steps) % length, length)
    return (at[:, None] * 4 + (me % 4 ^ flips)[None, :]).reshape(size)


def grads_kernel(first, a, x, y, low, high, by_expert, d_out, g_out, *scratch):
    rows, match, d_rows, grads, weights, sems = scratch
    experts, width, features = by_expert.shape
    tokens = rows.shape[0] // 4
    slots = experts * CAP
    pieces = (a, x, y, low, high)
    loads, at = [], 0
    for i, piece in enumerate(pieces):
        place = rows.at[pl.ds(at, piece.shape[0])]
        loads.append(pltpu.make_async_copy(piece, place, sems.at[i]))
        loads[-1].start()
        at += piece.shape[0]
    for load in loads:
        load.wait()
    loads = [
        pltpu.make_async_copy(by_expert.at[e], weights.at[e], sems.at[7 + e])
        for e in range(experts)
    ]
    for load in loads:
        load.start()

    slot = lax.broadcasted_iota(jnp.int32, (slots, tokens), 0)
    expert = first[0] + slot // CAP
    place = (slot % CAP).astype(jnp.float32)
    expert = expert.astype(jnp.float32)
    earlier = lax.broadcasted_iota(jnp.int32, (tokens, tokens), 0)
    earlier = earlier < lax.broadcasted_iota(jnp.int32, (tokens, tokens), 1)
    earlier = jnp.where(earlier, 1.0, 0.0).astype(jnp.bfloat16)
    hits = []
    for c in range(4):
        ids = rows[c * tokens : (c + 1) * tokens, features:].astype(jnp.float32).T
        named = jnp.zeros((slots, tokens), jnp.float32)
        for k in range(TOP):
            named = jnp.where(expert == ids[k : k + 1], 1.0, named)
        rank = jnp.dot(
            named.astype(jnp.bfloat16), earlier, preferred_element_type=jnp.float32
        )
        hits.append(jnp.where(rank == place, named, 0.0))
    blank = jnp.zeros((CAP, tokens), jnp.float32)
    lines = []
    for e in range(experts):
        for c in range(4):
            line = [blank] * 4
            line[c] = hits[c][e * CAP : (e + 1) * CAP]
            lines.append(jnp.concatenate(line, axis=1))
    match[...] = jnp.concatenate(lines, axis=0).astype(jnp.bfloat16)

    step = min(512, features)
    for at in range(0, features, step):
        d_rows[:, at : at + step] = jnp.dot(
            match[...], rows[:, at : at + step], preferred_element_type=jnp.float32
        ).astype(jnp.bfloat16)
    stores = [pltpu.make_async_copy(d_rows, d_out, sems.at[5])]
    stores[0].start()
    count = 4 * CAP
    found = []
    for e in range(experts):
        loads[e].wait()
        found.append(
            lax.dot_general(
                d_rows[e * count : (e + 1) * count],
                weights[e],
                (((1,), (1,)), ((), ())),
                preferred_element_type=jnp.float32,
            )
        )
    for c in range(4):
        mine = [f[c * CAP : (c + 1) * CAP] for f in found]
        grads[c] = jnp.concatenate(mine, axis=0).astype(jnp.bfloat16)
    stores.append(pltpu.make_async_copy(grads, g_out, sems.at[6]))
    stores[1].start()
    for store in stores:
        store.wait()


def chunk_grads(first, part, by_expert):
    experts, width, features = by_expert.shape
    tokens, columns = part[0].shape
    slots = experts * CAP
    return pl.pallas_call(
        grads_kernel,
        out_shape=(
            jax.ShapeDtypeStruct((4 * slots, features), jnp.bfloat16),
            jax.ShapeDtypeStruct((4, slots, width), jnp.bfloat16),
        ),
        in_specs=[pl.BlockSpec(memory_space=pltpu.SMEM)]
        + [HBM] * 6,
        out_specs=(HBM, HBM),
        scratch_shapes=[
            pltpu.VMEM((4 * tokens, columns), jnp.bfloat16),
            pltpu.VMEM((4 * slots, 4 * tokens), jnp.bfloat16),
            pltpu.VMEM((4 * slots, features), jnp.bfloat16),
            pltpu.VMEM((4, slots, width), jnp.bfloat16),
            pltpu.VMEM(by_expert.shape, jnp.bfloat16),
            pltpu.SemaphoreType.DMA((7 + experts,)),
        ],
        compiler_params=pltpu.CompilerParams(vmem_limit_bytes=56 * MIB),
        cost_estimate=pl.CostEstimate(
            flops=8 * slots * features * (4 * tokens + width),
            bytes_accessed=8 * (slots + tokens) * features,
            transcendentals=0,
        ),
    )(first, *part, by_expert)


def order_kernel(pieces, *refs):
    arrays, (out, rows, wide, turned, sems) = refs[:-5], refs[-5:]
    size, slots, width = rows.shape
    experts = slots // CAP
    loads = [
        pltpu.make_async_copy(arrays[a].at[i], rows.at[n], sems.at[n])
        for n, (a, i) in enumerate(pieces)
    ]
    for load in loads:
        load.start()
    for n, load in enumerate(loads):
        load.wait()
        wide[n] = rows[n].astype(jnp.float32)
    for e in range(experts):
        mine = [wide[n, e * CAP : (e + 1) * CAP] for n in range(size)]
        turned[e] = jnp.concatenate(mine, axis=0).T.astype(jnp.bfloat16)
    store = pltpu.make_async_copy(turned, out, sems.at[size])
    store.start()
    store.wait()


def order_slots(arrays, pieces):
    slots, width = arrays[0].shape[1:]
    size = len(pieces)
    shape = (slots // CAP, width, size * CAP)
    return pl.pallas_call(
        functools.partial(order_kernel, pieces),
        out_shape=jax.ShapeDtypeStruct(shape, jnp.bfloat16),
        in_specs=[HBM] * len(arrays),
        out_specs=HBM,
        scratch_shapes=[
            pltpu.VMEM((size, slots, width), jnp.bfloat16),
            pltpu.VMEM((size, slots, width), jnp.float32),
            pltpu.VMEM(shape, jnp.bfloat16),
            pltpu.SemaphoreType.DMA((size + 1,)),
        ],
        compiler_params=pltpu.CompilerParams(vmem_limit_bytes=10 * MIB),
        cost_estimate=pl.CostEstimate(
            flops=0, bytes_accessed=8 * size * slots * width, transcendentals=0
        ),
    )(*arrays)


def regroup_kernel(*refs):
    count = len(refs) - 5
    arrays, outs, (held, sems) = refs[:count], refs[count:-2], refs[-2:]
    loads = [
        pltpu.make_async_copy(a.at[pl.ds(1, 3)], held.at[k], sems.at[k])
        for k, a in enumerate(arrays)
    ]
    for load in loads:
        load.start()
    for load in loads:
        load.wait()
    stores = [
        pltpu.make_async_copy(held.at[:, c], out, sems.at[count + c])
        for c, out in enumerate(outs)
    ]
    for store in stores:
        store.start()
    for store in stores:
        store.wait()


def regroup(arrays):
    _, slots, width = arrays[0].shape
    count = len(arrays)
    return pl.pallas_call(
        regroup_kernel,
        out_shape=[jax.ShapeDtypeStruct((count, slots, width), jnp.bfloat16)] * 3,
        in_specs=[HBM] * count,
        out_specs=[HBM] * 3,
        scratch_shapes=[
            pltpu.VMEM((count, 3, slots, width), jnp.bfloat16),
            pltpu.SemaphoreType.DMA((count + 3,)),
        ],
        compiler_params=pltpu.CompilerParams(vmem_limit_bytes=10 * MIB),
        cost_estimate=pl.CostEstimate(
            flops=0, bytes_accessed=12 * count * slots * width, transcendentals=0
        ),
    )(*arrays)


def partial_kernel(owners, weighted, *refs):
    count = owners.shape[0]
    blocks, outs = refs[: -4 - count], refs[-4 - count : -4]
    w_in, rows, sums, sems = refs[-4:]
    experts, width, features = sums.shape
    share = width // count
    slots = blocks[0].shape[0] // experts
    loads = []
    for e in range(experts):
        mine = [(weighted.at[e], w_in.at[e])] + [
            (block.at[pl.ds(e * slots, slots)], rows.at[e, pl.ds(k * slots, slots)])
            for k, block in enumerate(blocks)
        ]
        loads.append(
            [
                pltpu.make_async_copy(source, place, sems.at[e, i])
                for i, (source, place) in enumerate(mine)
            ]
        )
    stores = []
    step = min(1024, features)
    for load in loads[0]:
        load.start()
    for e in range(experts):
        if e + 1 < experts:
            for load in loads[e + 1]:
                load.start()
        for load in loads[e]:
            load.wait()
        for at in range(0, features, step):
            sums[e, :, at : at + step] = jnp.dot(
                w_in[e], rows[e, :, at : at + step], preferred_element_type=jnp.float32
            ).astype(jnp.bfloat16)
        for r, out in enumerate(outs):
            at = pl.multiple_of(owners[r] * share, share)
            store = pltpu.make_async_copy(
                sums.at[e, pl.ds(at, share)], out.at[e], sems.at[e, len(blocks) + 1 + r]
            )
            store.start()
            stores.append(store)
    for store in stores:
        store.wait()


def partial_rows(owners, weighted, blocks):
    experts, width, slots = weighted.shape
    features = blocks[0].shape[1]
    count = owners.shape[0]
    return pl.pallas_call(
        partial_kernel,
        out_shape=[jax.ShapeDtypeStruct((experts, width // count, features), jnp.bfloat16)]
        * count,
        in_specs=[pl.BlockSpec(memory_space=pltpu.SMEM)] + [HBM] * (1 + len(blocks)),
        out_specs=[HBM] * count,
        scratch_shapes=[
            pltpu.VMEM((experts, width, slots), jnp.bfloat16),
            pltpu.VMEM((experts, slots, features), jnp.bfloat16),
            pltpu.VMEM((experts, width, features), jnp.bfloat16),
            pltpu.SemaphoreType.DMA((experts, 1 + len(blocks) + count)),
        ],
        compiler_params=pltpu.CompilerParams(vmem_limit_bytes=30 * MIB),
        cost_estimate=pl.CostEstimate(
            flops=2 * experts * width * slots * features,
            bytes_accessed=2 * experts * (width + slots) * features,
            transcendentals=0,
        ),
    )(owners, weighted, *blocks)


def root_of(x):
    inverse = lax.rsqrt(x)
    root = x * inverse
    return root + 0.5 * inverse * (x - root * root)


def reciprocal(x):
    estimate = pl.reciprocal(x, approx=True)
    return estimate * (2.0 - x * estimate)


def adam_kernel(count, kept, first, at, *refs):
    del at
    partials, (w, m1, m2) = refs[:count], refs[count : count + 3]
    new_w, new_m1, new_m2, full, copy, grad = refs[count + 3 + kept :]
    experts, rows, features = partials[0].shape
    tiles = features // LANES
    for e in range(experts):
        total = partials[0][e].astype(jnp.float32)
        for part in partials[1:]:
            total = total + part[e].astype(jnp.float32)
        for t in range(tiles):
            grad[pl.ds(t * experts + e, rows, stride=tiles * experts), :] = total[
                :, t * LANES : (t + 1) * LANES
            ]
    block = grad.shape[0]
    base = pl.multiple_of((first + pl.program_id(0)) * block, block)
    for start in range(0, block, 128):
        here = slice(start, start + 128)
        there = pl.ds(base + start, 128)
        g = grad[here]
        one = beta_one * m1[there] + (1.0 - beta_one) * g
        two = beta_two * m2[there] + (1.0 - beta_two) * g * g
        new_m1[here] = one
        new_m2[here] = two
        old = w[there]
        root = reciprocal(root_of(two * (1.0 / bias_two)) + adam_epsilon)
        new = old - learn_rate * (one * (1.0 / bias_one) * root + decay_rate * old)
        new_w[here] = new
        copy[here] = new.astype(jnp.bfloat16)
        full[here] = new.astype(jnp.bfloat16)


def adam_rows(at, partials, w, m1, m2, total_rows, before, first, steps):
    experts, rows, features = partials[0].shape
    block = 16
    flat = block * experts * features // LANES
    count, kept = len(partials), len(before)
    whole = rows // block
    part = pl.BlockSpec((experts, block, features), lambda i, at: (0, first + i, 0))
    line = pl.BlockSpec((flat, LANES), lambda i, at: (first + i, 0))
    placed = pl.BlockSpec((flat, LANES), lambda i, at: (at[0] * whole + first + i, 0))
    return pl.pallas_call(
        functools.partial(adam_kernel, count, kept, first),
        grid_spec=pltpu.PrefetchScalarGridSpec(
            num_scalar_prefetch=1,
            grid=(steps,),
            in_specs=[part] * count + [INSIDE] * 3 + [HBM] * kept,
            out_specs=[line] * 3 + [placed, pl.BlockSpec((flat, LANES), lambda i, at: (i, 0))],
            scratch_shapes=[pltpu.VMEM((flat, LANES), jnp.float32)],
        ),
        out_shape=[jax.ShapeDtypeStruct(w.shape, jnp.float32)] * 3
        + [
            jax.ShapeDtypeStruct((total_rows, LANES), jnp.bfloat16),
            jax.ShapeDtypeStruct((steps * flat, LANES), jnp.bfloat16),
        ],
        input_output_aliases={4 + count + i: i for i in range(kept)},
        compiler_params=pltpu.CompilerParams(vmem_limit_bytes=10 * MIB),
        cost_estimate=pl.CostEstimate(
            flops=20 * steps * flat * LANES,
            bytes_accessed=20 * steps * flat * LANES,
            transcendentals=0,
        ),
    )(at, *partials, w, m1, m2, *before)


def place_kernel(cut, at, low, high, full, out):
    del at, full
    here = pl.program_id(0)

    @pl.when(here < cut)
    def _():
        out[...] = low[...]

    @pl.when(here >= cut)
    def _():
        out[...] = high[...]


def place_rows(owner, low, high, full):
    block = math.gcd(low.shape[0], high.shape[0])
    cut = low.shape[0] // block
    steps = cut + high.shape[0] // block
    shape = (block, LANES)
    return pl.pallas_call(
        functools.partial(place_kernel, cut),
        grid_spec=pltpu.PrefetchScalarGridSpec(
            num_scalar_prefetch=1,
            grid=(steps,),
            in_specs=[
                pl.BlockSpec(shape, lambda i, at: (jnp.minimum(i, cut - 1), 0)),
                pl.BlockSpec(shape, lambda i, at: (jnp.maximum(i - cut, 0), 0)),
                HBM,
            ],
            out_specs=pl.BlockSpec(shape, lambda i, at: (at[0] * steps + i, 0)),
        ),
        out_shape=jax.ShapeDtypeStruct(full.shape, full.dtype),
        input_output_aliases={3: 0},
        compiler_params=pltpu.CompilerParams(vmem_limit_bytes=12 * MIB),
        cost_estimate=pl.CostEstimate(
            flops=0, bytes_accessed=4 * (low.size + high.size), transcendentals=0
        ),
    )(owner, low, high, full)


def finish_kernel(pieces, target, probs, hidden, *refs):
    back, (d_hidden, d_probs, rows, states, outs, sums, sems) = refs[:-7], refs[-7:]
    count = back[0].shape[1]
    choices, width = hidden.shape
    slots = rows.shape[0]
    loads = [
        pltpu.make_async_copy(back[a].at[i], rows.at[pl.ds(n * count, count)], sems.at[n])
        for n, (a, i) in enumerate(pieces)
    ]
    loads.append(pltpu.make_async_copy(hidden, states, sems.at[len(pieces)]))
    for load in loads:
        load.start()
    targets, scales = target[...].T, probs[...].T
    for load in loads:
        load.wait()
    ones = jnp.ones((8, width), jnp.bfloat16)
    across = (((1,), (1,)), ((), ()))
    step = 2 * LANES
    stores = []
    for n, at in enumerate(range(0, choices, step)):
        here = slice(at, at + step)

        def column(table):
            return jnp.concatenate([table[:, 2 * n : 2 * n + 1], table[:, 2 * n + 1 : 2 * n + 2]])

        places = lax.broadcasted_iota(jnp.int32, (step, slots), 1)
        onehot = jnp.where(places == column(targets).astype(jnp.int32), 1.0, 0.0)
        g = jnp.dot(onehot.astype(jnp.bfloat16), rows[...], preferred_element_type=jnp.float32)
        outs[here] = (column(scales) * g).astype(jnp.bfloat16)
        stores.append(
            pltpu.make_async_copy(outs.at[here], d_hidden.at[here], sems.at[len(loads) + n])
        )
        stores[n].start()
        product = states[here].astype(jnp.float32) * g
        high = product.astype(jnp.bfloat16)
        low = (product - high.astype(jnp.float32)).astype(jnp.bfloat16)
        sums[:, here] = lax.dot_general(
            ones, high, across, preferred_element_type=jnp.float32
        ) + lax.dot_general(ones, low, across, preferred_element_type=jnp.float32)
    d_probs[...] = sums[...]
    for store in stores:
        store.wait()


def finish(target, probs, hidden, back, pieces):
    choices, width = hidden.shape
    slots = len(pieces) * back[0].shape[1]
    steps = choices // (2 * LANES)
    return pl.pallas_call(
        functools.partial(finish_kernel, pieces),
        out_shape=(
            jax.ShapeDtypeStruct((choices, width), jnp.bfloat16),
            jax.ShapeDtypeStruct((8, choices), jnp.float32),
        ),
        in_specs=[INSIDE, INSIDE] + [HBM] * (1 + len(back)),
        out_specs=(HBM, INSIDE),
        scratch_shapes=[
            pltpu.VMEM((slots, width), jnp.bfloat16),
            pltpu.VMEM((choices, width), jnp.bfloat16),
            pltpu.VMEM((choices, width), jnp.bfloat16),
            pltpu.VMEM((8, choices), jnp.float32),
            pltpu.SemaphoreType.DMA((len(pieces) + 1 + steps,)),
        ],
        compiler_params=pltpu.CompilerParams(vmem_limit_bytes=12 * MIB),
        cost_estimate=pl.CostEstimate(
            flops=2 * choices * slots * width, bytes_accessed=8 * hidden.size, transcendentals=0
        ),
    )(target, probs, hidden, *back)


def lane_view(array):
    h, e, d = array.shape
    return array.reshape(h, e, d // LANES, LANES).transpose(0, 2, 1, 3).reshape(-1, LANES)


def lane_unview(rows, shape):
    h, e, d = shape
    return rows.reshape(h, d // LANES, e, LANES).transpose(0, 2, 1, 3).reshape(shape)


def local(cotangent, hidden, probs, expert_ids, secondary, weight, moment1, moment2):
    token_count = cotangent.shape[0]
    top_k = expert_ids.shape[1]
    hidden_width = hidden.shape[2]
    experts = secondary.shape[1]
    size = lax.axis_size("inner")
    length = size // 4
    outer_size = lax.axis_size("outer")
    outer_at = lax.axis_index("outer")
    me = lax.axis_index("inner")
    choices = token_count * top_k
    slots = experts * CAP
    rows = weight.shape[0]

    flat_ids = expert_ids.reshape(choices)
    target = slot_targets(flat_ids)
    device = flat_ids // experts
    ring_steps = (ring_place(device // 4, length) - ring_place(me // 4, length)) % length
    relative = ring_steps * 4 + (device % 4 ^ me % 4)
    target = (relative - device) * slots + target
    all_slots = jnp.arange(size * slots, dtype=jnp.int32)
    matches = (all_slots[:, None] == target[None, :]).astype(jnp.bfloat16)
    weighted = (
        (probs[..., None] * hidden.astype(jnp.float32))
        .astype(jnp.bfloat16)
        .reshape(choices, hidden_width)
    )
    w_send = jnp.dot(matches, weighted, preferred_element_type=jnp.float32).astype(jnp.bfloat16)
    w_send = w_send.reshape(length, 4, slots, hidden_width)
    columns = tuple(
        v.astype(jnp.float32).reshape(choices // LANES, LANES) for v in (target, probs)
    )
    state = tuple(lane_view(a) for a in (weight, moment1, moment2))

    def move(block, steps, flip):
        return lax.ppermute(block, "inner", step_perm(size, steps, flip))

    tie = lax.optimization_barrier
    last = length - 1
    half = token_count // 2
    first = (me * experts).astype(jnp.int32)[None]
    tags = jnp.pad(expert_ids.astype(jnp.bfloat16), ((0, 0), (0, LANES - top_k)))
    own = jnp.concatenate([cotangent, tags], axis=1)
    by_expert = jnp.transpose(secondary, (1, 0, 2))
    near, parts, w_parts = {}, {}, {}
    d_rows, grads, back = {}, {}, {}

    def add_chunk(j):
        d_rows[j], grads[j] = chunk_grads(first, parts[j], by_expert)

    def flips(arrays):
        return [move(a, 0, c) for c, a in enumerate(arrays, 1)]

    def halves(j):
        _, by_x, by_y = near[j]
        return (by_x[:half], by_y[half:])

    def far(low, high):
        return (move(low, 0, 2), move(high, 0, 1))

    for k in range(length + 1):
        moving = {}
        if k < last:
            moving["own"] = move(own, 1, 0)
        if k < length:
            moving["x"] = move(own, 0, 1)
            moving["y"] = move(own, 0, 2)
        if k > 1:
            moving["far"] = far(*halves(k - 1))
        if k == length:
            moving["first"] = far(*first_cut)
        if k > 2:
            add_chunk(k - 2)
        if k == 0:
            moving["columns"] = columns
        if k == 1:
            moving["cut"] = halves(0)
        if k == last - 1:
            moving["weights"] = by_expert
            w_parts[1] = move(w_send[1], 1, 0)
        if k == last:
            for j in range(last, 1, -1):
                w_parts[j] = move(w_send[j], j, 0)
        moving["done"] = (d_rows, grads, w_parts, w_send)
        if k == length:
            last_far = moving.pop("far")
            first_far = moving.pop("first")
        moved = tie(moving)
        d_rows, grads, w_parts, w_send = moved["done"]
        if k == 0:
            columns = moved["columns"]
        if k == 1:
            first_cut = moved["cut"]
        if k == last - 1:
            by_expert = moved["weights"]
        if k == last:
            w_parts[0] = w_send[0]
            w_arrays = [w_parts[j] for j in range(length)]
            w_flipped = flips(regroup(w_arrays))
        if 1 < k < length:
            parts[k - 1] = near[k - 1] + moved["far"]
        if k < length:
            near[k] = (own, moved["x"], moved["y"])
        own = moved.get("own")
    parts[last] = near[last] + last_far
    parts[0] = near[0] + first_far
    for j in range(1, last):
        back[j] = move(grads[j], -j, 0)
    add_chunk(last)
    back[last] = move(grads[last], -last, 0)
    add_chunk(0)
    back[0] = grads[0]
    back = [back[j] for j in range(length)]
    pieces = tuple((k, 0) if c == 0 else (length + c - 1, k) for k in range(length) for c in range(4))
    w_slots = order_slots(w_arrays + w_flipped, pieces)
    d_rows, leaving = tie(([d_rows[j] for j in range(length)], regroup(back)))
    def outer_perm(steps):
        return [(i, (i + steps) % outer_size) for i in range(outer_size)]

    owners = (outer_at + jnp.arange(outer_size, dtype=jnp.int32)) % outer_size
    mine, *sent = partial_rows(owners, w_slots, d_rows)
    partials = [mine] + [
        lax.ppermute(part, "outer", outer_perm(r)) for r, part in enumerate(sent, 1)
    ]
    partials, leaving = tie((partials, leaving))
    flipped = flips(leaving)

    at = outer_at.astype(jnp.int32)[None]
    total_rows = secondary.size // LANES
    blocks = rows // 16
    cuts = [0, blocks // 2, blocks]
    outs, copies = [], []
    for start, stop in zip(cuts[:-1], cuts[1:]):
        if start:
            partials, flipped = tie((partials, flipped))
        *outs, copy = adam_rows(
            at, partials, *state, total_rows, outs, start, stop - start
        )
        copies.append(copy)
    sent = [
        [lax.ppermute(copy, "outer", outer_perm(r)) for r in range(1, outer_size)]
        for copy in copies
    ]
    new_weight, new_moment1, new_moment2, full = outs
    for r in range(1, outer_size):
        owner = (outer_at + outer_size - r) % outer_size
        full = place_rows(
            owner.astype(jnp.int32)[None], sent[0][r - 1], sent[1][r - 1], full
        )

    d_hidden, d_probs = finish(
        *columns, hidden.reshape(choices, hidden_width), back + flipped, pieces
    )
    return (
        d_hidden.reshape(hidden.shape),
        d_probs[0].reshape(probs.shape),
        lane_unview(new_weight, weight.shape),
        lane_unview(new_moment1, weight.shape),
        lane_unview(new_moment2, weight.shape),
        lane_unview(full, secondary.shape),
    )


def solution(mesh):
    in_specs = (
        P(("outer", "inner"), None),
        P(("outer", "inner"), None, None),
        P(("outer", "inner"), None),
        P(("outer", "inner"), None),
        P(None, "inner", None),
        P("outer", "inner", None),
        P("outer", "inner", None),
        P("outer", "inner", None),
    )
    out_specs = (
        P(("outer", "inner"), None, None),
        P(("outer", "inner"), None),
        P("outer", "inner", None),
        P("outer", "inner", None),
        P("outer", "inner", None),
        P(None, "inner", None),
    )
    return jax.shard_map(local, mesh=mesh, in_specs=in_specs, out_specs=out_specs, check_vma=False)
```

```python
import functools
import math

import jax
import jax.numpy as jnp
from jax import lax
from jax.experimental import pallas as pl
from jax.experimental.pallas import tpu as pltpu
from jax.sharding import PartitionSpec as P

EXPERTS = 64
CAP = 24
TOP = 8
LANES = 128
MIB = 1 << 20


beta_one = 0.9
beta_two = 0.95
adam_epsilon = 1e-08
learn_rate = 0.003
decay_rate = 0.1
bias_one = 1.0 - 0.9**20
bias_two = 1.0 - 0.95**20

HBM = pl.BlockSpec(memory_space=pltpu.HBM)
INSIDE = pl.BlockSpec(memory_space=pltpu.VMEM)


def slot_targets(flat_ids):
    count = flat_ids.shape[0]
    block = 128
    blocks = count // block
    onehot = (jnp.arange(EXPERTS, dtype=jnp.int32)[:, None] == flat_ids[None, :]).astype(
        jnp.bfloat16
    )
    tiles = onehot.reshape(EXPERTS, blocks, block)
    lower = (jnp.arange(block)[:, None] < jnp.arange(block)[None, :]).astype(jnp.bfloat16)
    within = jnp.einsum("ebk,kj->ebj", tiles, lower, preferred_element_type=jnp.float32)
    totals = jnp.sum(tiles.astype(jnp.float32), axis=2)
    small = (jnp.arange(blocks)[:, None] < jnp.arange(blocks)[None, :]).astype(jnp.float32)
    before = jnp.dot(totals, small, precision=lax.Precision.HIGHEST)
    ranking = (within + before[..., None]).reshape(EXPERTS, count)
    position = jnp.sum(ranking * onehot.astype(jnp.float32), axis=0).astype(jnp.int32)
    return flat_ids * CAP + position


def line_ring(length):
    return [0] + list(range(1, length, 2)) + list(range(2, length, 2))[::-1]


def ring_place(plane, length):
    return jnp.where(plane % 2 == 1, (plane + 1) // 2, (length - plane // 2) % length)


def ring_plane(place, length):
    up = 2 * place - 1
    down = 2 * (length - place)
    return jnp.where(place == 0, 0, jnp.where(up < length, up, down))


def step_perm(size, steps, flip):
    ring = line_ring(size // 4)
    after = {at: ring[(i + steps) % len(ring)] for i, at in enumerate(ring)}
    return [(i, after[i // 4] * 4 + (i % 4 ^ flip)) for i in range(size)]


def source_order(size):
    me = lax.axis_index("inner")
    length = size // 4
    steps = jnp.arange(length, dtype=jnp.int32)
    flips = jnp.arange(4, dtype=jnp.int32)
    at = ring_plane((ring_place(me // 4, length) - steps) % length, length)
    return (at[:, None] * 4 + (me % 4 ^ flips)[None, :]).reshape(size)


def grads_kernel(spans, first, *refs):
    chunks = len(spans)
    parts = [
        [ref.at[pl.ds(*span)] for ref, span in zip(refs[5 * j :], spans[j])]
        for j in range(chunks)
    ]
    by_expert, outs = refs[5 * chunks], refs[5 * chunks + 1 : 7 * chunks + 1]
    all_rows, match, all_d_rows, all_grads, weights, sems, weight_sems = refs[-7:]
    experts, width, features = by_expert.shape
    tokens = all_rows.shape[1] // 4
    slots = experts * CAP
    loads = []
    for j, pieces in enumerate(parts):
        at = 0
        loads.append([])
        for i, piece in enumerate(pieces):
            place = all_rows.at[j, pl.ds(at, piece.shape[0])]
            loads[j].append(pltpu.make_async_copy(piece, place, sems.at[j, i]))
            loads[j][i].start()
            at += piece.shape[0]
    weight_loads = [
        pltpu.make_async_copy(by_expert.at[e], weights.at[e], weight_sems.at[e])
        for e in range(experts)
    ]

    slot = lax.broadcasted_iota(jnp.int32, (slots, tokens), 0)
    expert = (first[0] + slot // CAP).astype(jnp.float32)
    place = (slot % CAP).astype(jnp.float32)
    earlier = lax.broadcasted_iota(jnp.int32, (tokens, tokens), 0)
    earlier = earlier < lax.broadcasted_iota(jnp.int32, (tokens, tokens), 1)
    earlier = jnp.where(earlier, 1.0, 0.0).astype(jnp.bfloat16)
    stores = []
    for j in range(chunks):
        rows, d_rows, grads = all_rows.at[j], all_d_rows.at[j], all_grads.at[j]
        for load in loads[j]:
            load.wait()
        if j == 0:
            for load in weight_loads:
                load.start()
        hits = []
        for c in range(4):
            ids = rows[c * tokens : (c + 1) * tokens, features:].astype(jnp.float32).T
            named = jnp.zeros((slots, tokens), jnp.float32)
            for k in range(TOP):
                named = jnp.where(expert == ids[k : k + 1], 1.0, named)
            rank = jnp.dot(
                named.astype(jnp.bfloat16), earlier, preferred_element_type=jnp.float32
            )
            hits.append(jnp.where(rank == place, named, 0.0))
        blank = jnp.zeros((CAP, tokens), jnp.float32)
        lines = []
        for e in range(experts):
            for c in range(4):
                line = [blank] * 4
                line[c] = hits[c][e * CAP : (e + 1) * CAP]
                lines.append(jnp.concatenate(line, axis=1))
        match[...] = jnp.concatenate(lines, axis=0).astype(jnp.bfloat16)

        step = min(512, features)
        for at in range(0, features, step):
            d_rows[:, at : at + step] = jnp.dot(
                match[...], rows[:, at : at + step], preferred_element_type=jnp.float32
            ).astype(jnp.bfloat16)
        stores.append(pltpu.make_async_copy(d_rows, outs[2 * j], sems.at[j, 5]))
        stores[-1].start()
        count = 4 * CAP
        found = []
        for e in range(experts):
            if j == 0:
                weight_loads[e].wait()
            found.append(
                lax.dot_general(
                    d_rows[e * count : (e + 1) * count, :],
                    weights[e],
                    (((1,), (1,)), ((), ())),
                    preferred_element_type=jnp.float32,
                )
            )
        for c in range(4):
            mine = [f[c * CAP : (c + 1) * CAP] for f in found]
            grads[c] = jnp.concatenate(mine, axis=0).astype(jnp.bfloat16)
        stores.append(pltpu.make_async_copy(grads, outs[2 * j + 1], sems.at[j, 6]))
        stores[-1].start()
    for store in stores:
        store.wait()


def chunk_grads(first, parts, by_expert):
    experts, width, features = by_expert.shape
    tokens, columns = parts[0][0][0].shape
    spans = tuple(tuple(piece[1:] for piece in part) for part in parts)
    slots = experts * CAP
    chunks = len(parts)
    found = pl.pallas_call(
        functools.partial(grads_kernel, spans),
        out_shape=[
            jax.ShapeDtypeStruct((4 * slots, features), jnp.bfloat16),
            jax.ShapeDtypeStruct((4, slots, width), jnp.bfloat16),
        ]
        * chunks,
        in_specs=[pl.BlockSpec(memory_space=pltpu.SMEM)] + [HBM] * (5 * chunks + 1),
        out_specs=[HBM] * (2 * chunks),
        scratch_shapes=[
            pltpu.VMEM((chunks, 4 * tokens, columns), jnp.bfloat16),
            pltpu.VMEM((4 * slots, 4 * tokens), jnp.bfloat16),
            pltpu.VMEM((chunks, 4 * slots, features), jnp.bfloat16),
            pltpu.VMEM((chunks, 4, slots, width), jnp.bfloat16),
            pltpu.VMEM(by_expert.shape, jnp.bfloat16),
            pltpu.SemaphoreType.DMA((chunks, 7)),
            pltpu.SemaphoreType.DMA((experts,)),
        ],
        compiler_params=pltpu.CompilerParams(vmem_limit_bytes=56 * MIB),
        cost_estimate=pl.CostEstimate(
            flops=8 * chunks * slots * features * (4 * tokens + width),
            bytes_accessed=8 * chunks * (slots + tokens) * features,
            transcendentals=0,
        ),
    )(first, *(piece[0] for part in parts for piece in part), by_expert)
    return found[::2], found[1::2]


def order_kernel(pieces, *refs):
    arrays, (out, rows, wide, turned, sems) = refs[:-5], refs[-5:]
    size, slots, width = rows.shape
    experts = slots // CAP
    loads = [
        pltpu.make_async_copy(arrays[a].at[i], rows.at[n], sems.at[n])
        for n, (a, i) in enumerate(pieces)
    ]
    for load in loads:
        load.start()
    for n, load in enumerate(loads):
        load.wait()
        wide[n] = rows[n].astype(jnp.float32)
    for e in range(experts):
        mine = [wide[n, e * CAP : (e + 1) * CAP] for n in range(size)]
        turned[e] = jnp.concatenate(mine, axis=0).T.astype(jnp.bfloat16)
    store = pltpu.make_async_copy(turned, out, sems.at[size])
    store.start()
    store.wait()


def order_slots(arrays, pieces):
    slots, width = arrays[0].shape[1:]
    size = len(pieces)
    shape = (slots // CAP, width, size * CAP)
    return pl.pallas_call(
        functools.partial(order_kernel, pieces),
        out_shape=jax.ShapeDtypeStruct(shape, jnp.bfloat16),
        in_specs=[HBM] * len(arrays),
        out_specs=HBM,
        scratch_shapes=[
            pltpu.VMEM((size, slots, width), jnp.bfloat16),
            pltpu.VMEM((size, slots, width), jnp.float32),
            pltpu.VMEM(shape, jnp.bfloat16),
            pltpu.SemaphoreType.DMA((size + 1,)),
        ],
        compiler_params=pltpu.CompilerParams(vmem_limit_bytes=10 * MIB),
        cost_estimate=pl.CostEstimate(
            flops=0, bytes_accessed=8 * size * slots * width, transcendentals=0
        ),
    )(*arrays)


def regroup_kernel(*refs):
    count = len(refs) - 5
    arrays, outs, (held, sems) = refs[:count], refs[count:-2], refs[-2:]
    loads = [
        pltpu.make_async_copy(a.at[pl.ds(1, 3)], held.at[k], sems.at[k])
        for k, a in enumerate(arrays)
    ]
    for load in loads:
        load.start()
    for load in loads:
        load.wait()
    stores = [
        pltpu.make_async_copy(held.at[:, c], out, sems.at[count + c])
        for c, out in enumerate(outs)
    ]
    for store in stores:
        store.start()
    for store in stores:
        store.wait()


def regroup(arrays):
    _, slots, width = arrays[0].shape
    count = len(arrays)
    return pl.pallas_call(
        regroup_kernel,
        out_shape=[jax.ShapeDtypeStruct((count, slots, width), jnp.bfloat16)] * 3,
        in_specs=[HBM] * count,
        out_specs=[HBM] * 3,
        scratch_shapes=[
            pltpu.VMEM((count, 3, slots, width), jnp.bfloat16),
            pltpu.SemaphoreType.DMA((count + 3,)),
        ],
        compiler_params=pltpu.CompilerParams(vmem_limit_bytes=10 * MIB),
        cost_estimate=pl.CostEstimate(
            flops=0, bytes_accessed=12 * count * slots * width, transcendentals=0
        ),
    )(*arrays)


def partial_kernel(start, total, owners, weighted, *refs):
    count = owners.shape[0]
    blocks, outs = refs[: -4 - count], refs[-4 - count : -4]
    w_in, rows, sums, sems = refs[-4:]
    experts, width, features = sums.shape
    share = width // count
    slots = blocks[0].shape[0] // total
    loads = []
    for e in range(experts):
        mine = [(weighted.at[start + e], w_in.at[e])] + [
            (block.at[pl.ds((start + e) * slots, slots)], rows.at[e, pl.ds(k * slots, slots)])
            for k, block in enumerate(blocks)
        ]
        loads.append(
            [
                pltpu.make_async_copy(source, place, sems.at[e, i])
                for i, (source, place) in enumerate(mine)
            ]
        )
    stores = []
    step = min(1024, features)
    for load in loads[0]:
        load.start()
    for e in range(experts):
        if e + 1 < experts:
            for load in loads[e + 1]:
                load.start()
        for load in loads[e]:
            load.wait()
        for at in range(0, features, step):
            sums[e, :, at : at + step] = jnp.dot(
                w_in[e], rows[e, :, at : at + step], preferred_element_type=jnp.float32
            ).astype(jnp.bfloat16)
        for r, out in enumerate(outs):
            at = pl.multiple_of(owners[r] * share, share)
            store = pltpu.make_async_copy(
                sums.at[e, pl.ds(at, share)], out.at[e], sems.at[e, len(blocks) + 1 + r]
            )
            store.start()
            stores.append(store)
    for store in stores:
        store.wait()


def partial_rows(owners, weighted, blocks, start, stop):
    total, width, slots = weighted.shape
    experts = stop - start
    features = blocks[0].shape[1]
    count = owners.shape[0]
    return pl.pallas_call(
        functools.partial(partial_kernel, start, total),
        out_shape=[jax.ShapeDtypeStruct((experts, width // count, features), jnp.bfloat16)]
        * count,
        in_specs=[pl.BlockSpec(memory_space=pltpu.SMEM)] + [HBM] * (1 + len(blocks)),
        out_specs=[HBM] * count,
        scratch_shapes=[
            pltpu.VMEM((experts, width, slots), jnp.bfloat16),
            pltpu.VMEM((experts, slots, features), jnp.bfloat16),
            pltpu.VMEM((experts, width, features), jnp.bfloat16),
            pltpu.SemaphoreType.DMA((experts, 1 + len(blocks) + count)),
        ],
        compiler_params=pltpu.CompilerParams(vmem_limit_bytes=16 * MIB),
        cost_estimate=pl.CostEstimate(
            flops=2 * experts * width * slots * features,
            bytes_accessed=2 * experts * (width + slots) * features,
            transcendentals=0,
        ),
    )(owners, weighted, *blocks)


def root_of(x):
    inverse = lax.rsqrt(x)
    root = x * inverse
    return root + 0.5 * inverse * (x - root * root)


def reciprocal(x):
    estimate = pl.reciprocal(x, approx=True)
    return estimate * (2.0 - x * estimate)


def adam_kernel(count, owners, kept, first, at, *refs):
    del at
    partials, (w, m1, m2) = refs[:count], refs[count : count + 3]
    partials = [partials[i : i + owners] for i in range(0, count, owners)]
    new_w, new_m1, new_m2, full, copy, grad = refs[count + 3 + kept :]
    _, rows, features = partials[0][0].shape
    tiles = features // LANES
    places = [(span, e) for span in partials for e in range(span[0].shape[0])]
    experts = len(places)
    for e, (span, at) in enumerate(places):
        total = span[0][at].astype(jnp.float32)
        for part in span[1:]:
            total = total + part[at].astype(jnp.float32)
        for t in range(tiles):
            grad[pl.ds(t * experts + e, rows, stride=tiles * experts), :] = total[
                :, t * LANES : (t + 1) * LANES
            ]
    block = grad.shape[0]
    base = pl.multiple_of((first + pl.program_id(0)) * block, block)
    for start in range(0, block, 128):
        here = slice(start, start + 128)
        there = pl.ds(base + start, 128)
        g = grad[here]
        one = beta_one * m1[there] + (1.0 - beta_one) * g
        two = beta_two * m2[there] + (1.0 - beta_two) * g * g
        new_m1[here] = one
        new_m2[here] = two
        old = w[there]
        root = reciprocal(root_of(two * (1.0 / bias_two)) + adam_epsilon)
        new = old - learn_rate * (one * (1.0 / bias_one) * root + decay_rate * old)
        new_w[here] = new
        copy[here] = new.astype(jnp.bfloat16)
        full[here] = new.astype(jnp.bfloat16)


def adam_rows(at, partials, w, m1, m2, total_rows, before, first, steps):
    owners = len(partials[0])
    partials = [part for span in partials for part in span]
    _, rows, features = partials[0].shape
    experts = sum(part.shape[0] for part in partials) // owners
    block = 16
    flat = block * experts * features // LANES
    count, kept = len(partials), len(before)
    whole = rows // block
    parts = [
        pl.BlockSpec((part.shape[0], block, features), lambda i, at: (0, first + i, 0))
        for part in partials
    ]
    line = pl.BlockSpec((flat, LANES), lambda i, at: (first + i, 0))
    placed = pl.BlockSpec((flat, LANES), lambda i, at: (at[0] * whole + first + i, 0))
    return pl.pallas_call(
        functools.partial(adam_kernel, count, owners, kept, first),
        grid_spec=pltpu.PrefetchScalarGridSpec(
            num_scalar_prefetch=1,
            grid=(steps,),
            in_specs=parts + [INSIDE] * 3 + [HBM] * kept,
            out_specs=[line] * 3 + [placed, pl.BlockSpec((flat, LANES), lambda i, at: (i, 0))],
            scratch_shapes=[pltpu.VMEM((flat, LANES), jnp.float32)],
        ),
        out_shape=[jax.ShapeDtypeStruct(w.shape, jnp.float32)] * 3
        + [
            jax.ShapeDtypeStruct((total_rows, LANES), jnp.bfloat16),
            jax.ShapeDtypeStruct((steps * flat, LANES), jnp.bfloat16),
        ],
        input_output_aliases={4 + count + i: i for i in range(kept)},
        compiler_params=pltpu.CompilerParams(vmem_limit_bytes=10 * MIB),
        cost_estimate=pl.CostEstimate(
            flops=20 * steps * flat * LANES,
            bytes_accessed=20 * steps * flat * LANES,
            transcendentals=0,
        ),
    )(at, *partials, w, m1, m2, *before)


def place_kernel(cut, at, low, high, full, out):
    del at, full
    here = pl.program_id(0)

    @pl.when(here < cut)
    def _():
        out[...] = low[...]

    @pl.when(here >= cut)
    def _():
        out[...] = high[...]


def place_rows(owner, low, high, full):
    block = math.gcd(low.shape[0], high.shape[0])
    block = block // 3 if block % 3 == 0 else block
    cut = low.shape[0] // block
    steps = cut + high.shape[0] // block
    shape = (block, LANES)
    return pl.pallas_call(
        functools.partial(place_kernel, cut),
        grid_spec=pltpu.PrefetchScalarGridSpec(
            num_scalar_prefetch=1,
            grid=(steps,),
            in_specs=[
                pl.BlockSpec(shape, lambda i, at: (jnp.minimum(i, cut - 1), 0)),
                pl.BlockSpec(shape, lambda i, at: (jnp.maximum(i - cut, 0), 0)),
                HBM,
            ],
            out_specs=pl.BlockSpec(shape, lambda i, at: (at[0] * steps + i, 0)),
        ),
        out_shape=jax.ShapeDtypeStruct(full.shape, full.dtype),
        input_output_aliases={3: 0},
        compiler_params=pltpu.CompilerParams(vmem_limit_bytes=12 * MIB),
        cost_estimate=pl.CostEstimate(
            flops=0, bytes_accessed=4 * (low.size + high.size), transcendentals=0
        ),
    )(owner, low, high, full)


def finish_kernel(pieces, target, probs, hidden, *refs):
    back, (d_hidden, d_probs, rows, states, outs, sums, sems) = refs[:-7], refs[-7:]
    count = back[0].shape[1]
    choices, width = hidden.shape
    slots = rows.shape[0]
    loads = [
        pltpu.make_async_copy(back[a].at[i], rows.at[pl.ds(n * count, count)], sems.at[n])
        for n, (a, i) in enumerate(pieces)
    ]
    loads.append(pltpu.make_async_copy(hidden, states, sems.at[len(pieces)]))
    for load in loads:
        load.start()
    targets, scales = target[...].T, probs[...].T
    for load in loads:
        load.wait()
    ones = jnp.ones((8, width), jnp.bfloat16)
    across = (((1,), (1,)), ((), ()))
    step = 2 * LANES
    stores = []
    for n, at in enumerate(range(0, choices, step)):
        here = slice(at, at + step)

        def column(table):
            return jnp.concatenate([table[:, 2 * n : 2 * n + 1], table[:, 2 * n + 1 : 2 * n + 2]])

        places = lax.broadcasted_iota(jnp.int32, (step, slots), 1)
        onehot = jnp.where(places == column(targets).astype(jnp.int32), 1.0, 0.0)
        g = jnp.dot(onehot.astype(jnp.bfloat16), rows[...], preferred_element_type=jnp.float32)
        outs[here] = (column(scales) * g).astype(jnp.bfloat16)
        stores.append(
            pltpu.make_async_copy(outs.at[here], d_hidden.at[here], sems.at[len(loads) + n])
        )
        stores[n].start()
        product = states[here].astype(jnp.float32) * g
        high = product.astype(jnp.bfloat16)
        low = (product - high.astype(jnp.float32)).astype(jnp.bfloat16)
        sums[:, here] = lax.dot_general(
            ones, high, across, preferred_element_type=jnp.float32
        ) + lax.dot_general(ones, low, across, preferred_element_type=jnp.float32)
    d_probs[...] = sums[...]
    for store in stores:
        store.wait()


def finish(target, probs, hidden, back, pieces):
    choices, width = hidden.shape
    slots = len(pieces) * back[0].shape[1]
    steps = choices // (2 * LANES)
    return pl.pallas_call(
        functools.partial(finish_kernel, pieces),
        out_shape=(
            jax.ShapeDtypeStruct((choices, width), jnp.bfloat16),
            jax.ShapeDtypeStruct((8, choices), jnp.float32),
        ),
        in_specs=[INSIDE, INSIDE] + [HBM] * (1 + len(back)),
        out_specs=(HBM, INSIDE),
        scratch_shapes=[
            pltpu.VMEM((slots, width), jnp.bfloat16),
            pltpu.VMEM((choices, width), jnp.bfloat16),
            pltpu.VMEM((choices, width), jnp.bfloat16),
            pltpu.VMEM((8, choices), jnp.float32),
            pltpu.SemaphoreType.DMA((len(pieces) + 1 + steps,)),
        ],
        compiler_params=pltpu.CompilerParams(vmem_limit_bytes=56 * MIB),
        cost_estimate=pl.CostEstimate(
            flops=2 * choices * slots * width, bytes_accessed=8 * hidden.size, transcendentals=0
        ),
    )(target, probs, hidden, *back)


def lane_view(array):
    h, e, d = array.shape
    return array.reshape(h, e, d // LANES, LANES).transpose(0, 2, 1, 3).reshape(-1, LANES)


def lane_unview(rows, shape):
    h, e, d = shape
    return rows.reshape(h, d // LANES, e, LANES).transpose(0, 2, 1, 3).reshape(shape)


def local(cotangent, hidden, probs, expert_ids, secondary, weight, moment1, moment2):
    token_count = cotangent.shape[0]
    top_k = expert_ids.shape[1]
    hidden_width = hidden.shape[2]
    experts = secondary.shape[1]
    size = lax.axis_size("inner")
    length = size // 4
    outer_size = lax.axis_size("outer")
    outer_at = lax.axis_index("outer")
    me = lax.axis_index("inner")
    choices = token_count * top_k
    slots = experts * CAP
    rows = weight.shape[0]

    flat_ids = expert_ids.reshape(choices)
    target = slot_targets(flat_ids)
    device = flat_ids // experts
    ring_steps = (ring_place(device // 4, length) - ring_place(me // 4, length)) % length
    relative = ring_steps * 4 + (device % 4 ^ me % 4)
    target = (relative - device) * slots + target
    all_slots = jnp.arange(size * slots, dtype=jnp.int32)
    matches = (all_slots[:, None] == target[None, :]).astype(jnp.bfloat16)
    weighted = (
        (probs[..., None] * hidden.astype(jnp.float32))
        .astype(jnp.bfloat16)
        .reshape(choices, hidden_width)
    )
    w_send = jnp.dot(matches, weighted, preferred_element_type=jnp.float32).astype(jnp.bfloat16)
    w_send = w_send.reshape(length, 4, slots, hidden_width)
    columns = tuple(
        v.astype(jnp.float32).reshape(choices // LANES, LANES) for v in (target, probs)
    )
    state = tuple(lane_view(a) for a in (weight, moment1, moment2))

    def move(block, steps, flip):
        return lax.ppermute(block, "inner", step_perm(size, steps, flip))

    tie = lax.optimization_barrier
    last = length - 1
    half = token_count // 2
    first = (me * experts).astype(jnp.int32)[None]
    tags = jnp.pad(expert_ids.astype(jnp.bfloat16), ((0, 0), (0, LANES - top_k)))
    own = jnp.concatenate([cotangent, tags], axis=1)
    by_expert = jnp.transpose(secondary, (1, 0, 2))
    near, parts, w_parts = {}, {}, {}
    d_rows, grads, back = {}, {}, {}

    def add_chunks(*chunks):
        found = chunk_grads(first, [parts[j] for j in chunks], by_expert)
        for j, d_chunk, g_chunk in zip(chunks, *found):
            d_rows[j], grads[j] = d_chunk, g_chunk

    def flips(arrays):
        return [move(a, 0, c) for c, a in enumerate(arrays, 1)]

    def whole(*arrays):
        return tuple((a, 0, a.shape[0]) for a in arrays)

    def halves(j):
        _, by_x, by_y = near[j]
        return (by_x[:half], by_y[half:])

    def far(low, high):
        return (move(low, 0, 2), move(high, 0, 1))

    for k in range(length + 1):
        moving = {}
        if k < last:
            moving["own"] = move(own, 1, 0)
        if k < length:
            moving["x"] = move(own, 0, 1)
            moving["y"] = move(own, 0, 2)
        if 1 < k < length:
            moving["far"] = far(*halves(k - 1))
        if k == length:
            both = zip(halves(last), first_cut)
            moving["far"] = far(*(jnp.concatenate(pair) for pair in both))
            for j in range(1, last - 1):
                back[j] = move(grads[j], -j, 0)
            moving["back"] = back
        if k > 2:
            add_chunks(k - 2)
        if k == 0:
            moving["columns"] = columns
        if k == 1:
            moving["cut"] = halves(0)
        if k == last - 1:
            moving["weights"] = by_expert
            w_parts[1] = move(w_send[1], 1, 0)
        if k == last:
            for j in range(last, 1, -1):
                w_parts[j] = move(w_send[j], j, 0)
        moving["done"] = (d_rows, grads, w_parts, w_send)
        moved = tie(moving)
        d_rows, grads, w_parts, w_send = moved["done"]
        if k == 0:
            columns = moved["columns"]
        if k == 1:
            first_cut = moved["cut"]
        if k == last - 1:
            by_expert = moved["weights"]
        if k == last:
            w_parts[0] = w_send[0]
            w_arrays = [w_parts[j] for j in range(length)]
            w_flipped = flips(regroup(w_arrays))
        if 1 < k < length:
            parts[k - 1] = whole(*near[k - 1]) + whole(*moved["far"])
        if k < length:
            near[k] = (own, moved["x"], moved["y"])
        own = moved.get("own")
    back = moved["back"]
    back[last - 1] = move(grads[last - 1], 1 - last, 0)
    parts[last] = whole(*near[last]) + tuple((f, 0, half) for f in moved["far"])
    parts[0] = whole(*near[0]) + tuple((f, half, half) for f in moved["far"])
    add_chunks(last, 0)
    back[last] = move(grads[last], -last, 0)
    back[0] = grads[0]
    back = [back[j] for j in range(length)]
    pieces = tuple((k, 0) if c == 0 else (length + c - 1, k) for k in range(length) for c in range(4))
    w_slots = order_slots(w_arrays + w_flipped, pieces)
    d_rows = [d_rows[j] for j in range(length)]

    def outer_perm(steps):
        return [(i, (i + steps) % outer_size) for i in range(outer_size)]

    owners = (outer_at + jnp.arange(outer_size, dtype=jnp.int32)) % outer_size
    partials = []
    for start, stop in ((0, experts // 2), (experts // 2, experts)):
        if start:
            d_rows, back = tie((d_rows, back))
        mine, *sent = partial_rows(owners, w_slots, d_rows, start, stop)
        partials.append(
            [mine]
            + [lax.ppermute(part, "outer", outer_perm(r)) for r, part in enumerate(sent, 1)]
        )
    partials, leaving = tie((partials, regroup(back)))
    flipped = flips(leaving)

    at = outer_at.astype(jnp.int32)[None]
    total_rows = secondary.size // LANES
    blocks = rows // 16
    cuts = [0, blocks // 2, blocks]
    outs, copies = [], []
    for start, stop in zip(cuts[:-1], cuts[1:]):
        if start:
            partials, flipped = tie((partials, flipped))
        *outs, copy = adam_rows(
            at, partials, *state, total_rows, outs, start, stop - start
        )
        copies.append(copy)
    sent = [
        [lax.ppermute(copy, "outer", outer_perm(r)) for r in range(1, outer_size)]
        for copy in copies
    ]
    new_weight, new_moment1, new_moment2, full = outs
    for r in range(1, outer_size):
        owner = (outer_at + outer_size - r) % outer_size
        full = place_rows(
            owner.astype(jnp.int32)[None], sent[0][r - 1], sent[1][r - 1], full
        )

    d_hidden, d_probs = finish(
        *columns, hidden.reshape(choices, hidden_width), back + flipped, pieces
    )
    return (
        d_hidden.reshape(hidden.shape),
        d_probs[0].reshape(probs.shape),
        lane_unview(new_weight, weight.shape),
        lane_unview(new_moment1, weight.shape),
        lane_unview(new_moment2, weight.shape),
        lane_unview(full, secondary.shape),
    )


def solution(mesh):
    in_specs = (
        P(("outer", "inner"), None),
        P(("outer", "inner"), None, None),
        P(("outer", "inner"), None),
        P(("outer", "inner"), None),
        P(None, "inner", None),
        P("outer", "inner", None),
        P("outer", "inner", None),
        P("outer", "inner", None),
    )
    out_specs = (
        P(("outer", "inner"), None, None),
        P(("outer", "inner"), None),
        P("outer", "inner", None),
        P("outer", "inner", None),
        P("outer", "inner", None),
        P(None, "inner", None),
    )
    return jax.shard_map(local, mesh=mesh, in_specs=in_specs, out_specs=out_specs, check_vma=False)
```

```python
import functools
import math

import jax
import jax.numpy as jnp
from jax import lax
from jax.experimental import pallas as pl
from jax.experimental.pallas import tpu as pltpu
from jax.sharding import PartitionSpec as P

EXPERTS = 64
CAP = 24
TOP = 8
LANES = 128
MIB = 1 << 20


beta_one = 0.9
beta_two = 0.95
adam_epsilon = 1e-08
learn_rate = 0.003
decay_rate = 0.1
bias_one = 1.0 - 0.9**20
bias_two = 1.0 - 0.95**20

HBM = pl.BlockSpec(memory_space=pltpu.HBM)
INSIDE = pl.BlockSpec(memory_space=pltpu.VMEM)


def slot_targets(flat_ids):
    count = flat_ids.shape[0]
    block = 128
    blocks = count // block
    onehot = (jnp.arange(EXPERTS, dtype=jnp.int32)[:, None] == flat_ids[None, :]).astype(
        jnp.bfloat16
    )
    tiles = onehot.reshape(EXPERTS, blocks, block)
    lower = (jnp.arange(block)[:, None] < jnp.arange(block)[None, :]).astype(jnp.bfloat16)
    within = jnp.einsum("ebk,kj->ebj", tiles, lower, preferred_element_type=jnp.float32)
    totals = jnp.sum(tiles.astype(jnp.float32), axis=2)
    small = (jnp.arange(blocks)[:, None] < jnp.arange(blocks)[None, :]).astype(jnp.float32)
    before = jnp.dot(totals, small, precision=lax.Precision.HIGHEST)
    ranking = (within + before[..., None]).reshape(EXPERTS, count)
    position = jnp.sum(ranking * onehot.astype(jnp.float32), axis=0).astype(jnp.int32)
    return flat_ids * CAP + position


def line_ring(length):
    return [0] + list(range(1, length, 2)) + list(range(2, length, 2))[::-1]


def ring_place(plane, length):
    return jnp.where(plane % 2 == 1, (plane + 1) // 2, (length - plane // 2) % length)


def ring_plane(place, length):
    up = 2 * place - 1
    down = 2 * (length - place)
    return jnp.where(place == 0, 0, jnp.where(up < length, up, down))


def step_perm(size, steps, flip):
    ring = line_ring(size // 4)
    after = {at: ring[(i + steps) % len(ring)] for i, at in enumerate(ring)}
    return [(i, after[i // 4] * 4 + (i % 4 ^ flip)) for i in range(size)]


def source_order(size):
    me = lax.axis_index("inner")
    length = size // 4
    steps = jnp.arange(length, dtype=jnp.int32)
    flips = jnp.arange(4, dtype=jnp.int32)
    at = ring_plane((ring_place(me // 4, length) - steps) % length, length)
    return (at[:, None] * 4 + (me % 4 ^ flips)[None, :]).reshape(size)


def grads_kernel(spans, first, *refs):
    chunks = len(spans)
    parts = [
        [ref.at[pl.ds(*span)] for ref, span in zip(refs[5 * j :], spans[j])]
        for j in range(chunks)
    ]
    by_expert, outs = refs[5 * chunks], refs[5 * chunks + 1 : 7 * chunks + 1]
    all_rows, match, all_d_rows, all_grads, weights, sems, weight_sems = refs[-7:]
    experts, width, features = by_expert.shape
    tokens = all_rows.shape[1] // 4
    slots = experts * CAP
    loads = []
    for j, pieces in enumerate(parts):
        at = 0
        loads.append([])
        for i, piece in enumerate(pieces):
            place = all_rows.at[j, pl.ds(at, piece.shape[0])]
            loads[j].append(pltpu.make_async_copy(piece, place, sems.at[j, i]))
            loads[j][i].start()
            at += piece.shape[0]
    weight_loads = [
        pltpu.make_async_copy(by_expert.at[e], weights.at[e], weight_sems.at[e])
        for e in range(experts)
    ]

    slot = lax.broadcasted_iota(jnp.int32, (slots, tokens), 0)
    expert = (first[0] + slot // CAP).astype(jnp.float32)
    place = (slot % CAP).astype(jnp.float32)
    earlier = lax.broadcasted_iota(jnp.int32, (tokens, tokens), 0)
    earlier = earlier < lax.broadcasted_iota(jnp.int32, (tokens, tokens), 1)
    earlier = jnp.where(earlier, 1.0, 0.0).astype(jnp.bfloat16)
    stores = []
    for j in range(chunks):
        rows, d_rows, grads = all_rows.at[j], all_d_rows.at[j], all_grads.at[j]
        for load in loads[j]:
            load.wait()
        if j == 0:
            for load in weight_loads:
                load.start()
        hits = []
        for c in range(4):
            ids = rows[c * tokens : (c + 1) * tokens, features:].astype(jnp.float32).T
            named = jnp.zeros((slots, tokens), jnp.float32)
            for k in range(TOP):
                named = jnp.where(expert == ids[k : k + 1], 1.0, named)
            rank = jnp.dot(
                named.astype(jnp.bfloat16), earlier, preferred_element_type=jnp.float32
            )
            hits.append(jnp.where(rank == place, named, 0.0))
        blank = jnp.zeros((CAP, tokens), jnp.float32)
        lines = []
        for e in range(experts):
            for c in range(4):
                line = [blank] * 4
                line[c] = hits[c][e * CAP : (e + 1) * CAP]
                lines.append(jnp.concatenate(line, axis=1))
        match[...] = jnp.concatenate(lines, axis=0).astype(jnp.bfloat16)

        step = min(512, features)
        for at in range(0, features, step):
            d_rows[:, at : at + step] = jnp.dot(
                match[...], rows[:, at : at + step], preferred_element_type=jnp.float32
            ).astype(jnp.bfloat16)
        stores.append(pltpu.make_async_copy(d_rows, outs[2 * j], sems.at[j, 5]))
        stores[-1].start()
        count = 4 * CAP
        found = []
        for e in range(experts):
            if j == 0:
                weight_loads[e].wait()
            found.append(
                lax.dot_general(
                    d_rows[e * count : (e + 1) * count, :],
                    weights[e],
                    (((1,), (1,)), ((), ())),
                    preferred_element_type=jnp.float32,
                )
            )
        for c in range(4):
            mine = [f[c * CAP : (c + 1) * CAP] for f in found]
            grads[c] = jnp.concatenate(mine, axis=0).astype(jnp.bfloat16)
        stores.append(pltpu.make_async_copy(grads, outs[2 * j + 1], sems.at[j, 6]))
        stores[-1].start()
    for store in stores:
        store.wait()


def chunk_grads(first, parts, by_expert, vmem):
    experts, width, features = by_expert.shape
    tokens, columns = parts[0][0][0].shape
    spans = tuple(tuple(piece[1:] for piece in part) for part in parts)
    slots = experts * CAP
    chunks = len(parts)
    found = pl.pallas_call(
        functools.partial(grads_kernel, spans),
        out_shape=[
            jax.ShapeDtypeStruct((4 * slots, features), jnp.bfloat16),
            jax.ShapeDtypeStruct((4, slots, width), jnp.bfloat16),
        ]
        * chunks,
        in_specs=[pl.BlockSpec(memory_space=pltpu.SMEM)] + [HBM] * (5 * chunks + 1),
        out_specs=[HBM] * (2 * chunks),
        scratch_shapes=[
            pltpu.VMEM((chunks, 4 * tokens, columns), jnp.bfloat16),
            pltpu.VMEM((4 * slots, 4 * tokens), jnp.bfloat16),
            pltpu.VMEM((chunks, 4 * slots, features), jnp.bfloat16),
            pltpu.VMEM((chunks, 4, slots, width), jnp.bfloat16),
            pltpu.VMEM(by_expert.shape, jnp.bfloat16),
            pltpu.SemaphoreType.DMA((chunks, 7)),
            pltpu.SemaphoreType.DMA((experts,)),
        ],
        compiler_params=pltpu.CompilerParams(vmem_limit_bytes=vmem * MIB),
        cost_estimate=pl.CostEstimate(
            flops=8 * chunks * slots * features * (4 * tokens + width),
            bytes_accessed=8 * chunks * (slots + tokens) * features,
            transcendentals=0,
        ),
    )(first, *(piece[0] for part in parts for piece in part), by_expert)
    return found[::2], found[1::2]


def order_kernel(pieces, *refs):
    arrays, (out, rows, wide, turned, sems) = refs[:-5], refs[-5:]
    size, slots, width = rows.shape
    experts = slots // CAP
    loads = [
        pltpu.make_async_copy(arrays[a].at[i], rows.at[n], sems.at[n])
        for n, (a, i) in enumerate(pieces)
    ]
    for load in loads:
        load.start()
    for n, load in enumerate(loads):
        load.wait()
        wide[n] = rows[n].astype(jnp.float32)
    for e in range(experts):
        mine = [wide[n, e * CAP : (e + 1) * CAP] for n in range(size)]
        turned[e] = jnp.concatenate(mine, axis=0).T.astype(jnp.bfloat16)
    store = pltpu.make_async_copy(turned, out, sems.at[size])
    store.start()
    store.wait()


def order_slots(arrays, pieces):
    slots, width = arrays[0].shape[1:]
    size = len(pieces)
    shape = (slots // CAP, width, size * CAP)
    return pl.pallas_call(
        functools.partial(order_kernel, pieces),
        out_shape=jax.ShapeDtypeStruct(shape, jnp.bfloat16),
        in_specs=[HBM] * len(arrays),
        out_specs=HBM,
        scratch_shapes=[
            pltpu.VMEM((size, slots, width), jnp.bfloat16),
            pltpu.VMEM((size, slots, width), jnp.float32),
            pltpu.VMEM(shape, jnp.bfloat16),
            pltpu.SemaphoreType.DMA((size + 1,)),
        ],
        compiler_params=pltpu.CompilerParams(vmem_limit_bytes=8 * MIB),
        cost_estimate=pl.CostEstimate(
            flops=0, bytes_accessed=8 * size * slots * width, transcendentals=0
        ),
    )(*arrays)


def regroup_kernel(*refs):
    count = len(refs) - 5
    arrays, outs, (held, sems) = refs[:count], refs[count:-2], refs[-2:]
    loads = [
        pltpu.make_async_copy(a.at[pl.ds(1, 3)], held.at[k], sems.at[k])
        for k, a in enumerate(arrays)
    ]
    for load in loads:
        load.start()
    for load in loads:
        load.wait()
    stores = [
        pltpu.make_async_copy(held.at[:, c], out, sems.at[count + c])
        for c, out in enumerate(outs)
    ]
    for store in stores:
        store.start()
    for store in stores:
        store.wait()


def regroup(arrays):
    _, slots, width = arrays[0].shape
    count = len(arrays)
    return pl.pallas_call(
        regroup_kernel,
        out_shape=[jax.ShapeDtypeStruct((count, slots, width), jnp.bfloat16)] * 3,
        in_specs=[HBM] * count,
        out_specs=[HBM] * 3,
        scratch_shapes=[
            pltpu.VMEM((count, 3, slots, width), jnp.bfloat16),
            pltpu.SemaphoreType.DMA((count + 3,)),
        ],
        compiler_params=pltpu.CompilerParams(vmem_limit_bytes=3 * MIB),
        cost_estimate=pl.CostEstimate(
            flops=0, bytes_accessed=12 * count * slots * width, transcendentals=0
        ),
    )(*arrays)


def partial_kernel(start, total, owners, weighted, *refs):
    count = owners.shape[0]
    blocks, outs = refs[: -4 - count], refs[-4 - count : -4]
    w_in, rows, sums, sems = refs[-4:]
    experts, width, features = sums.shape
    share = width // count
    slots = blocks[0].shape[0] // total
    loads = []
    for e in range(experts):
        mine = [(weighted.at[start + e], w_in.at[e])] + [
            (block.at[pl.ds((start + e) * slots, slots)], rows.at[e, pl.ds(k * slots, slots)])
            for k, block in enumerate(blocks)
        ]
        loads.append(
            [
                pltpu.make_async_copy(source, place, sems.at[e, i])
                for i, (source, place) in enumerate(mine)
            ]
        )
    stores = []
    step = min(1024, features)
    for load in loads[0]:
        load.start()
    for e in range(experts):
        if e + 1 < experts:
            for load in loads[e + 1]:
                load.start()
        for load in loads[e]:
            load.wait()
        for at in range(0, features, step):
            sums[e, :, at : at + step] = jnp.dot(
                w_in[e], rows[e, :, at : at + step], preferred_element_type=jnp.float32
            ).astype(jnp.bfloat16)
        for r, out in enumerate(outs):
            at = pl.multiple_of(owners[r] * share, share)
            store = pltpu.make_async_copy(
                sums.at[e, pl.ds(at, share)], out.at[e], sems.at[e, len(blocks) + 1 + r]
            )
            store.start()
            stores.append(store)
    for store in stores:
        store.wait()


def partial_rows(owners, weighted, blocks, start, stop):
    total, width, slots = weighted.shape
    experts = stop - start
    features = blocks[0].shape[1]
    count = owners.shape[0]
    return pl.pallas_call(
        functools.partial(partial_kernel, start, total),
        out_shape=[jax.ShapeDtypeStruct((experts, width // count, features), jnp.bfloat16)]
        * count,
        in_specs=[pl.BlockSpec(memory_space=pltpu.SMEM)] + [HBM] * (1 + len(blocks)),
        out_specs=[HBM] * count,
        scratch_shapes=[
            pltpu.VMEM((experts, width, slots), jnp.bfloat16),
            pltpu.VMEM((experts, slots, features), jnp.bfloat16),
            pltpu.VMEM((experts, width, features), jnp.bfloat16),
            pltpu.SemaphoreType.DMA((experts, 1 + len(blocks) + count)),
        ],
        compiler_params=pltpu.CompilerParams(vmem_limit_bytes=9 * MIB),
        cost_estimate=pl.CostEstimate(
            flops=2 * experts * width * slots * features,
            bytes_accessed=2 * experts * (width + slots) * features,
            transcendentals=0,
        ),
    )(owners, weighted, *blocks)


def root_of(x):
    inverse = lax.rsqrt(x)
    root = x * inverse
    return root + 0.5 * inverse * (x - root * root)


def reciprocal(x):
    estimate = pl.reciprocal(x, approx=True)
    return estimate * (2.0 - x * estimate)


def adam_kernel(count, owners, kept, first, at, *refs):
    del at
    partials, (w, m1, m2) = refs[:count], refs[count : count + 3]
    partials = [partials[i : i + owners] for i in range(0, count, owners)]
    new_w, new_m1, new_m2, full, copy, grad = refs[count + 3 + kept :]
    _, rows, features = partials[0][0].shape
    tiles = features // LANES
    places = [(span, e) for span in partials for e in range(span[0].shape[0])]
    experts = len(places)
    unit = tiles * experts
    stride = unit + 1
    for e, (span, at) in enumerate(places):
        total = span[0][at].astype(jnp.float32)
        for part in span[1:]:
            total = total + part[at].astype(jnp.float32)
        for t in range(tiles):
            grad[pl.ds(t * experts + e, rows, stride=stride), :] = total[
                :, t * LANES : (t + 1) * LANES
            ]
    block = rows * unit
    base = pl.multiple_of((first + pl.program_id(0)) * block, block)
    for h in range(rows):
        here = slice(h * unit, (h + 1) * unit)
        there = pl.ds(base + h * unit, unit)
        g = grad[h * stride : h * stride + unit]
        one = beta_one * m1[there] + (1.0 - beta_one) * g
        two = beta_two * m2[there] + (1.0 - beta_two) * g * g
        new_m1[here] = one
        new_m2[here] = two
        old = w[there]
        root = reciprocal(root_of(two * (1.0 / bias_two)) + adam_epsilon)
        new = old - learn_rate * (one * (1.0 / bias_one) * root + decay_rate * old)
        new_w[here] = new
        copy[here] = new.astype(jnp.bfloat16)
        full[here] = new.astype(jnp.bfloat16)


def adam_rows(at, partials, w, m1, m2, total_rows, before, first, steps):
    owners = len(partials[0])
    partials = [part for span in partials for part in span]
    _, rows, features = partials[0].shape
    experts = sum(part.shape[0] for part in partials) // owners
    block = 16
    flat = block * experts * features // LANES
    count, kept = len(partials), len(before)
    whole = rows // block
    parts = [
        pl.BlockSpec((part.shape[0], block, features), lambda i, at: (0, first + i, 0))
        for part in partials
    ]
    line = pl.BlockSpec((flat, LANES), lambda i, at: (first + i, 0))
    placed = pl.BlockSpec((flat, LANES), lambda i, at: (at[0] * whole + first + i, 0))
    return pl.pallas_call(
        functools.partial(adam_kernel, count, owners, kept, first),
        grid_spec=pltpu.PrefetchScalarGridSpec(
            num_scalar_prefetch=1,
            grid=(steps,),
            in_specs=parts + [INSIDE] * 3 + [HBM] * kept,
            out_specs=[line] * 3 + [placed, pl.BlockSpec((flat, LANES), lambda i, at: (i, 0))],
            scratch_shapes=[pltpu.VMEM((flat + block, LANES), jnp.float32)],
        ),
        out_shape=[jax.ShapeDtypeStruct(w.shape, jnp.float32)] * 3
        + [
            jax.ShapeDtypeStruct((total_rows, LANES), jnp.bfloat16),
            jax.ShapeDtypeStruct((steps * flat, LANES), jnp.bfloat16),
        ],
        input_output_aliases={4 + count + i: i for i in range(kept)},
        compiler_params=pltpu.CompilerParams(vmem_limit_bytes=10 * MIB),
        cost_estimate=pl.CostEstimate(
            flops=20 * steps * flat * LANES,
            bytes_accessed=20 * steps * flat * LANES,
            transcendentals=0,
        ),
    )(at, *partials, w, m1, m2, *before)


def place_kernel(cut, at, low, high, full, out):
    del at, full
    here = pl.program_id(0)

    @pl.when(here < cut)
    def _():
        out[...] = low[...]

    @pl.when(here >= cut)
    def _():
        out[...] = high[...]


def place_rows(owner, low, high, full):
    block = math.gcd(low.shape[0], high.shape[0])
    block = block // 3 if block % 3 == 0 else block
    cut = low.shape[0] // block
    steps = cut + high.shape[0] // block
    shape = (block, LANES)
    return pl.pallas_call(
        functools.partial(place_kernel, cut),
        grid_spec=pltpu.PrefetchScalarGridSpec(
            num_scalar_prefetch=1,
            grid=(steps,),
            in_specs=[
                pl.BlockSpec(shape, lambda i, at: (jnp.minimum(i, cut - 1), 0)),
                pl.BlockSpec(shape, lambda i, at: (jnp.maximum(i - cut, 0), 0)),
                HBM,
            ],
            out_specs=pl.BlockSpec(shape, lambda i, at: (at[0] * steps + i, 0)),
        ),
        out_shape=jax.ShapeDtypeStruct(full.shape, full.dtype),
        input_output_aliases={3: 0},
        compiler_params=pltpu.CompilerParams(vmem_limit_bytes=12 * MIB),
        cost_estimate=pl.CostEstimate(
            flops=0, bytes_accessed=4 * (low.size + high.size), transcendentals=0
        ),
    )(owner, low, high, full)


def finish_kernel(pieces, target, probs, hidden, *refs):
    back, (d_hidden, d_probs, rows, states, outs, sums, sems) = refs[:-7], refs[-7:]
    count = back[0].shape[1]
    choices, width = hidden.shape
    slots = rows.shape[0]
    loads = [
        pltpu.make_async_copy(back[a].at[i], rows.at[pl.ds(n * count, count)], sems.at[n])
        for n, (a, i) in enumerate(pieces)
    ]
    loads.append(pltpu.make_async_copy(hidden, states, sems.at[len(pieces)]))
    for load in loads:
        load.start()
    targets, scales = target[...].T, probs[...].T
    for load in loads:
        load.wait()
    ones = jnp.ones((8, width), jnp.bfloat16)
    across = (((1,), (1,)), ((), ()))
    step = 2 * LANES
    stores = []
    for n, at in enumerate(range(0, choices, step)):
        here = slice(at, at + step)

        def column(table):
            return jnp.concatenate([table[:, 2 * n : 2 * n + 1], table[:, 2 * n + 1 : 2 * n + 2]])

        places = lax.broadcasted_iota(jnp.int32, (step, slots), 1)
        onehot = jnp.where(places == column(targets).astype(jnp.int32), 1.0, 0.0)
        g = jnp.dot(onehot.astype(jnp.bfloat16), rows[...], preferred_element_type=jnp.float32)
        outs[here] = (column(scales) * g).astype(jnp.bfloat16)
        stores.append(
            pltpu.make_async_copy(outs.at[here], d_hidden.at[here], sems.at[len(loads) + n])
        )
        stores[n].start()
        product = states[here].astype(jnp.float32) * g
        high = product.astype(jnp.bfloat16)
        low = (product - high.astype(jnp.float32)).astype(jnp.bfloat16)
        sums[:, here] = lax.dot_general(
            ones, high, across, preferred_element_type=jnp.float32
        ) + lax.dot_general(ones, low, across, preferred_element_type=jnp.float32)
    d_probs[...] = sums[...]
    for store in stores:
        store.wait()


def finish(target, probs, hidden, back, pieces):
    choices, width = hidden.shape
    slots = len(pieces) * back[0].shape[1]
    steps = choices // (2 * LANES)
    return pl.pallas_call(
        functools.partial(finish_kernel, pieces),
        out_shape=(
            jax.ShapeDtypeStruct((choices, width), jnp.bfloat16),
            jax.ShapeDtypeStruct((8, choices), jnp.float32),
        ),
        in_specs=[INSIDE, INSIDE] + [HBM] * (1 + len(back)),
        out_specs=(HBM, INSIDE),
        scratch_shapes=[
            pltpu.VMEM((slots, width), jnp.bfloat16),
            pltpu.VMEM((choices, width), jnp.bfloat16),
            pltpu.VMEM((choices, width), jnp.bfloat16),
            pltpu.VMEM((8, choices), jnp.float32),
            pltpu.SemaphoreType.DMA((len(pieces) + 1 + steps,)),
        ],
        compiler_params=pltpu.CompilerParams(vmem_limit_bytes=56 * MIB),
        cost_estimate=pl.CostEstimate(
            flops=2 * choices * slots * width, bytes_accessed=8 * hidden.size, transcendentals=0
        ),
    )(target, probs, hidden, *back)


def lane_view(array):
    h, e, d = array.shape
    return array.reshape(h, e, d // LANES, LANES).transpose(0, 2, 1, 3).reshape(-1, LANES)


def lane_unview(rows, shape):
    h, e, d = shape
    return rows.reshape(h, d // LANES, e, LANES).transpose(0, 2, 1, 3).reshape(shape)


def local(cotangent, hidden, probs, expert_ids, secondary, weight, moment1, moment2):
    token_count = cotangent.shape[0]
    top_k = expert_ids.shape[1]
    hidden_width = hidden.shape[2]
    experts = secondary.shape[1]
    size = lax.axis_size("inner")
    length = size // 4
    outer_size = lax.axis_size("outer")
    outer_at = lax.axis_index("outer")
    me = lax.axis_index("inner")
    choices = token_count * top_k
    slots = experts * CAP
    rows = weight.shape[0]

    flat_ids = expert_ids.reshape(choices)
    target = slot_targets(flat_ids)
    device = flat_ids // experts
    ring_steps = (ring_place(device // 4, length) - ring_place(me // 4, length)) % length
    relative = ring_steps * 4 + (device % 4 ^ me % 4)
    target = (relative - device) * slots + target
    all_slots = jnp.arange(size * slots, dtype=jnp.int32)
    matches = (all_slots[:, None] == target[None, :]).astype(jnp.bfloat16)
    weighted = (
        (probs[..., None] * hidden.astype(jnp.float32))
        .astype(jnp.bfloat16)
        .reshape(choices, hidden_width)
    )
    w_send = jnp.dot(matches, weighted, preferred_element_type=jnp.float32).astype(jnp.bfloat16)
    w_send = w_send.reshape(length, 4, slots, hidden_width)
    columns = tuple(
        v.astype(jnp.float32).reshape(choices // LANES, LANES) for v in (target, probs)
    )
    state = tuple(lane_view(a) for a in (weight, moment1, moment2))

    def move(block, steps, flip):
        return lax.ppermute(block, "inner", step_perm(size, steps, flip))

    tie = lax.optimization_barrier
    last = length - 1
    half = token_count // 2
    first = (me * experts).astype(jnp.int32)[None]
    tags = jnp.pad(expert_ids.astype(jnp.bfloat16), ((0, 0), (0, LANES - top_k)))
    own = jnp.concatenate([cotangent, tags], axis=1)
    by_expert = jnp.transpose(secondary, (1, 0, 2))
    near, parts, w_parts = {}, {}, {}
    d_rows, grads, back = {}, {}, {}

    def add_chunks(*chunks, vmem=56):
        found = chunk_grads(first, [parts[j] for j in chunks], by_expert, vmem)
        for j, d_chunk, g_chunk in zip(chunks, *found):
            d_rows[j], grads[j] = d_chunk, g_chunk

    def flips(arrays):
        return [move(a, 0, c) for c, a in enumerate(arrays, 1)]

    def whole(*arrays):
        return tuple((a, 0, a.shape[0]) for a in arrays)

    def halves(j):
        _, by_x, by_y = near[j]
        return (by_x[:half], by_y[half:])

    def far(low, high):
        return (move(low, 0, 2), move(high, 0, 1))

    for k in range(length + 1):
        moving = {}
        if k < last:
            moving["own"] = move(own, 1, 0)
        if k < length:
            moving["x"] = move(own, 0, 1)
            moving["y"] = move(own, 0, 2)
        if 1 < k < length:
            moving["far"] = far(*halves(k - 1))
        if k == length:
            both = zip(halves(last), first_cut)
            moving["far"] = far(*(jnp.concatenate(pair) for pair in both))
            for j in range(1, last - 1):
                back[j] = move(grads[j], -j, 0)
            moving["back"] = back
        if k > 2:
            add_chunks(k - 2)
        if k == 0:
            moving["columns"] = columns
        if k == 1:
            moving["cut"] = halves(0)
            moving["send"] = [w_send[j] for j in range(length)]
        if k == last - 1:
            moving["weights"] = by_expert
            w_parts[1] = move(w_send[1], 1, 0)
        if k == last:
            for j in range(last, 1, -1):
                w_parts[j] = move(w_send[j], j, 0)
        if k != 1:
            moving["send"] = w_send
        moving["done"] = (d_rows, grads, w_parts)
        moved = tie(moving)
        d_rows, grads, w_parts = moved["done"]
        w_send = moved["send"]
        if k == 0:
            columns = moved["columns"]
        if k == 1:
            first_cut = moved["cut"]
        if k == last - 1:
            by_expert = moved["weights"]
        if k == last:
            w_parts[0] = w_send[0]
            w_arrays = [w_parts[j] for j in range(length)]
            w_flipped = flips(regroup(w_arrays))
        if 1 < k < length:
            parts[k - 1] = whole(*near[k - 1]) + whole(*moved["far"])
        if k < length:
            near[k] = (own, moved["x"], moved["y"])
        own = moved.get("own")
    back = moved["back"]
    back[last - 1] = move(grads[last - 1], 1 - last, 0)
    parts[last] = whole(*near[last]) + tuple((f, 0, half) for f in moved["far"])
    parts[0] = whole(*near[0]) + tuple((f, half, half) for f in moved["far"])
    add_chunks(last, 0, vmem=24)
    back[last] = move(grads[last], -last, 0)
    back[0] = grads[0]
    back = [back[j] for j in range(length)]
    pieces = tuple((k, 0) if c == 0 else (length + c - 1, k) for k in range(length) for c in range(4))
    w_slots = order_slots(w_arrays + w_flipped, pieces)
    d_rows = [d_rows[j] for j in range(length)]

    def outer_perm(steps):
        return [(i, (i + steps) % outer_size) for i in range(outer_size)]

    owners = (outer_at + jnp.arange(outer_size, dtype=jnp.int32)) % outer_size
    partials = []
    for start, stop in ((0, experts // 2), (experts // 2, experts)):
        if start:
            d_rows, back = tie((d_rows, back))
        mine, *sent = partial_rows(owners, w_slots, d_rows, start, stop)
        partials.append(
            [mine]
            + [lax.ppermute(part, "outer", outer_perm(r)) for r, part in enumerate(sent, 1)]
        )
    partials, leaving = tie((partials, regroup(back)))
    flipped = flips(leaving)

    at = outer_at.astype(jnp.int32)[None]
    total_rows = secondary.size // LANES
    blocks = rows // 16
    cuts = [0, blocks // 2, blocks]
    outs, copies = [], []
    for start, stop in zip(cuts[:-1], cuts[1:]):
        if start:
            partials, flipped = tie((partials, flipped))
        *outs, copy = adam_rows(
            at, partials, *state, total_rows, outs, start, stop - start
        )
        copies.append(copy)
    sent = [
        [lax.ppermute(copy, "outer", outer_perm(r)) for r in range(1, outer_size)]
        for copy in copies
    ]
    new_weight, new_moment1, new_moment2, full = outs
    for r in range(1, outer_size):
        owner = (outer_at + outer_size - r) % outer_size
        full = place_rows(
            owner.astype(jnp.int32)[None], sent[0][r - 1], sent[1][r - 1], full
        )

    d_hidden, d_probs = finish(
        *columns, hidden.reshape(choices, hidden_width), back + flipped, pieces
    )
    return (
        d_hidden.reshape(hidden.shape),
        d_probs[0].reshape(probs.shape),
        lane_unview(new_weight, weight.shape),
        lane_unview(new_moment1, weight.shape),
        lane_unview(new_moment2, weight.shape),
        lane_unview(full, secondary.shape),
    )


def solution(mesh):
    in_specs = (
        P(("outer", "inner"), None),
        P(("outer", "inner"), None, None),
        P(("outer", "inner"), None),
        P(("outer", "inner"), None),
        P(None, "inner", None),
        P("outer", "inner", None),
        P("outer", "inner", None),
        P("outer", "inner", None),
    )
    out_specs = (
        P(("outer", "inner"), None, None),
        P(("outer", "inner"), None),
        P("outer", "inner", None),
        P("outer", "inner", None),
        P("outer", "inner", None),
        P(None, "inner", None),
    )
    return jax.shard_map(local, mesh=mesh, in_specs=in_specs, out_specs=out_specs, check_vma=False)
```

```python
import functools

import jax
import jax.numpy as jnp
from jax import lax
from jax.experimental import pallas as pl
from jax.experimental.pallas import tpu as pltpu
from jax.sharding import PartitionSpec as P

EXPERTS = 64
CAP = 24
TOP = 8
LANES = 128
MIB = 1 << 20
SMALL = pl.CostEstimate(flops=0, bytes_accessed=1 << 16, transcendentals=0)


beta_one = 0.9
beta_two = 0.95
adam_epsilon = 1e-08
learn_rate = 0.003
decay_rate = 0.1
bias_one = 1.0 - 0.9**20
bias_two = 1.0 - 0.95**20

HBM = pl.BlockSpec(memory_space=pltpu.HBM)
INSIDE = pl.BlockSpec(memory_space=pltpu.VMEM)


def slot_targets(flat_ids):
    count = flat_ids.shape[0]
    block = 128
    blocks = count // block
    onehot = (jnp.arange(EXPERTS, dtype=jnp.int32)[:, None] == flat_ids[None, :]).astype(
        jnp.bfloat16
    )
    tiles = onehot.reshape(EXPERTS, blocks, block)
    lower = (jnp.arange(block)[:, None] < jnp.arange(block)[None, :]).astype(jnp.bfloat16)
    within = jnp.einsum("ebk,kj->ebj", tiles, lower, preferred_element_type=jnp.float32)
    totals = jnp.sum(tiles.astype(jnp.float32), axis=2)
    small = (jnp.arange(blocks)[:, None] < jnp.arange(blocks)[None, :]).astype(jnp.float32)
    before = jnp.dot(totals, small, precision=lax.Precision.HIGHEST)
    ranking = (within + before[..., None]).reshape(EXPERTS, count)
    position = jnp.sum(ranking * onehot.astype(jnp.float32), axis=0).astype(jnp.int32)
    return flat_ids * CAP + position


def line_ring(length):
    return [0] + list(range(1, length, 2)) + list(range(2, length, 2))[::-1]


def ring_place(plane, length):
    return jnp.where(plane % 2 == 1, (plane + 1) // 2, (length - plane // 2) % length)


def ring_plane(place, length):
    up = 2 * place - 1
    down = 2 * (length - place)
    return jnp.where(place == 0, 0, jnp.where(up < length, up, down))


def step_perm(size, steps, flip):
    ring = line_ring(size // 4)
    after = {at: ring[(i + steps) % len(ring)] for i, at in enumerate(ring)}
    return [(i, after[i // 4] * 4 + (i % 4 ^ flip)) for i in range(size)]


def source_order(size):
    me = lax.axis_index("inner")
    length = size // 4
    steps = jnp.arange(length, dtype=jnp.int32)
    flips = jnp.arange(4, dtype=jnp.int32)
    at = ring_plane((ring_place(me // 4, length) - steps) % length, length)
    return (at[:, None] * 4 + (me % 4 ^ flips)[None, :]).reshape(size)


def grads_kernel(spans, first, *refs):
    chunks = len(spans)
    parts = [
        [ref.at[pl.ds(*span)] for ref, span in zip(refs[5 * j :], spans[j])]
        for j in range(chunks)
    ]
    by_expert, outs = refs[5 * chunks], refs[5 * chunks + 1 : 7 * chunks + 1]
    all_rows, match, all_d_rows, all_grads, weights, sems, weight_sems = refs[-7:]
    experts, width, features = by_expert.shape
    tokens = all_rows.shape[1] // 4
    slots = experts * CAP
    loads = []
    for j, pieces in enumerate(parts):
        at = 0
        loads.append([])
        for i, piece in enumerate(pieces):
            place = all_rows.at[j, pl.ds(at, piece.shape[0])]
            loads[j].append(pltpu.make_async_copy(piece, place, sems.at[j, i]))
            loads[j][i].start()
            at += piece.shape[0]
    weight_loads = [
        pltpu.make_async_copy(by_expert.at[e], weights.at[e], weight_sems.at[e])
        for e in range(experts)
    ]

    slot = lax.broadcasted_iota(jnp.int32, (slots, tokens), 0)
    expert = (first[0] + slot // CAP).astype(jnp.float32)
    place = (slot % CAP).astype(jnp.float32)
    earlier = lax.broadcasted_iota(jnp.int32, (tokens, tokens), 0)
    earlier = earlier < lax.broadcasted_iota(jnp.int32, (tokens, tokens), 1)
    earlier = jnp.where(earlier, 1.0, 0.0).astype(jnp.bfloat16)
    stores = []
    for j in range(chunks):
        rows, d_rows, grads = all_rows.at[j], all_d_rows.at[j], all_grads.at[j]
        for load in loads[j]:
            load.wait()
        if j == 0:
            for load in weight_loads:
                load.start()
        hits = []
        for c in range(4):
            ids = rows[c * tokens : (c + 1) * tokens, features:].astype(jnp.float32).T
            named = jnp.zeros((slots, tokens), jnp.float32)
            for k in range(TOP):
                named = jnp.where(expert == ids[k : k + 1], 1.0, named)
            rank = jnp.dot(
                named.astype(jnp.bfloat16), earlier, preferred_element_type=jnp.float32
            )
            hits.append(jnp.where(rank == place, named, 0.0))
        blank = jnp.zeros((CAP, tokens), jnp.float32)
        lines = []
        for e in range(experts):
            for c in range(4):
                line = [blank] * 4
                line[c] = hits[c][e * CAP : (e + 1) * CAP]
                lines.append(jnp.concatenate(line, axis=1))
        match[...] = jnp.concatenate(lines, axis=0).astype(jnp.bfloat16)

        step = min(512, features)
        for at in range(0, features, step):
            d_rows[:, at : at + step] = jnp.dot(
                match[...], rows[:, at : at + step], preferred_element_type=jnp.float32
            ).astype(jnp.bfloat16)
        stores.append(pltpu.make_async_copy(d_rows, outs[2 * j], sems.at[j, 5]))
        stores[-1].start()
        count = 4 * CAP
        found = []
        for e in range(experts):
            if j == 0:
                weight_loads[e].wait()
            found.append(
                lax.dot_general(
                    d_rows[e * count : (e + 1) * count, :],
                    weights[e],
                    (((1,), (1,)), ((), ())),
                    preferred_element_type=jnp.float32,
                )
            )
        for c in range(4):
            mine = [f[c * CAP : (c + 1) * CAP] for f in found]
            grads[c] = jnp.concatenate(mine, axis=0).astype(jnp.bfloat16)
        stores.append(pltpu.make_async_copy(grads, outs[2 * j + 1], sems.at[j, 6]))
        stores[-1].start()
    for store in stores:
        store.wait()


def chunk_grads(first, parts, by_expert, vmem):
    experts, width, features = by_expert.shape
    tokens, columns = parts[0][0][0].shape
    spans = tuple(tuple(piece[1:] for piece in part) for part in parts)
    slots = experts * CAP
    chunks = len(parts)
    found = pl.pallas_call(
        functools.partial(grads_kernel, spans),
        out_shape=[
            jax.ShapeDtypeStruct((4 * slots, features), jnp.bfloat16),
            jax.ShapeDtypeStruct((4, slots, width), jnp.bfloat16),
        ]
        * chunks,
        in_specs=[pl.BlockSpec(memory_space=pltpu.SMEM)] + [HBM] * (5 * chunks + 1),
        out_specs=[HBM] * (2 * chunks),
        scratch_shapes=[
            pltpu.VMEM((chunks, 4 * tokens, columns), jnp.bfloat16),
            pltpu.VMEM((4 * slots, 4 * tokens), jnp.bfloat16),
            pltpu.VMEM((chunks, 4 * slots, features), jnp.bfloat16),
            pltpu.VMEM((chunks, 4, slots, width), jnp.bfloat16),
            pltpu.VMEM(by_expert.shape, jnp.bfloat16),
            pltpu.SemaphoreType.DMA((chunks, 7)),
            pltpu.SemaphoreType.DMA((experts,)),
        ],
        compiler_params=pltpu.CompilerParams(vmem_limit_bytes=vmem * MIB),
        cost_estimate=pl.CostEstimate(
            flops=8 * chunks * slots * features * (4 * tokens + width),
            bytes_accessed=8 * chunks * (slots + tokens) * features,
            transcendentals=0,
        ),
    )(first, *(piece[0] for part in parts for piece in part), by_expert)
    return found[::2], found[1::2]


def order_kernel(pieces, *refs):
    arrays, (out, rows, wide, turned, sems) = refs[:-5], refs[-5:]
    size, slots, width = rows.shape
    experts = slots // CAP
    loads = [
        pltpu.make_async_copy(arrays[a].at[i], rows.at[n], sems.at[n])
        for n, (a, i) in enumerate(pieces)
    ]
    for load in loads:
        load.start()
    for n, load in enumerate(loads):
        load.wait()
        wide[n] = rows[n].astype(jnp.float32)
    for e in range(experts):
        mine = [wide[n, e * CAP : (e + 1) * CAP] for n in range(size)]
        turned[e] = jnp.concatenate(mine, axis=0).T.astype(jnp.bfloat16)
    store = pltpu.make_async_copy(turned, out, sems.at[size])
    store.start()
    store.wait()


def order_slots(arrays, pieces):
    slots, width = arrays[0].shape[1:]
    size = len(pieces)
    shape = (slots // CAP, width, size * CAP)
    return pl.pallas_call(
        functools.partial(order_kernel, pieces),
        out_shape=jax.ShapeDtypeStruct(shape, jnp.bfloat16),
        in_specs=[HBM] * len(arrays),
        out_specs=HBM,
        scratch_shapes=[
            pltpu.VMEM((size, slots, width), jnp.bfloat16),
            pltpu.VMEM((size, slots, width), jnp.float32),
            pltpu.VMEM(shape, jnp.bfloat16),
            pltpu.SemaphoreType.DMA((size + 1,)),
        ],
        compiler_params=pltpu.CompilerParams(vmem_limit_bytes=10 * MIB),
        cost_estimate=pl.CostEstimate(
            flops=0, bytes_accessed=8 * size * slots * width, transcendentals=0
        ),
    )(*arrays)


def regroup_kernel(*refs):
    count = len(refs) - 5
    arrays, outs, (held, sems) = refs[:count], refs[count:-2], refs[-2:]
    loads = [
        pltpu.make_async_copy(a.at[pl.ds(1, 3)], held.at[k], sems.at[k])
        for k, a in enumerate(arrays)
    ]
    for load in loads:
        load.start()
    for load in loads:
        load.wait()
    stores = [
        pltpu.make_async_copy(held.at[:, c], out, sems.at[count + c])
        for c, out in enumerate(outs)
    ]
    for store in stores:
        store.start()
    for store in stores:
        store.wait()


def regroup(arrays):
    _, slots, width = arrays[0].shape
    count = len(arrays)
    return pl.pallas_call(
        regroup_kernel,
        out_shape=[jax.ShapeDtypeStruct((count, slots, width), jnp.bfloat16)] * 3,
        in_specs=[HBM] * count,
        out_specs=[HBM] * 3,
        scratch_shapes=[
            pltpu.VMEM((count, 3, slots, width), jnp.bfloat16),
            pltpu.SemaphoreType.DMA((count + 3,)),
        ],
        compiler_params=pltpu.CompilerParams(vmem_limit_bytes=10 * MIB),
        cost_estimate=pl.CostEstimate(
            flops=0, bytes_accessed=12 * count * slots * width, transcendentals=0
        ),
    )(*arrays)


def partial_kernel(start, total, owners, weighted, *refs):
    count = owners.shape[0]
    blocks, outs = refs[: -4 - count], refs[-4 - count : -4]
    w_in, rows, sums, sems = refs[-4:]
    experts, width, features = sums.shape
    share = width // count
    slots = blocks[0].shape[0] // total
    loads = []
    for e in range(experts):
        mine = [(weighted.at[start + e], w_in.at[e])] + [
            (block.at[pl.ds((start + e) * slots, slots)], rows.at[e, pl.ds(k * slots, slots)])
            for k, block in enumerate(blocks)
        ]
        loads.append(
            [
                pltpu.make_async_copy(source, place, sems.at[e, i])
                for i, (source, place) in enumerate(mine)
            ]
        )
    stores = []
    step = min(1024, features)
    for load in loads[0]:
        load.start()
    for e in range(experts):
        if e + 1 < experts:
            for load in loads[e + 1]:
                load.start()
        for load in loads[e]:
            load.wait()
        for at in range(0, features, step):
            sums[e, :, at : at + step] = jnp.dot(
                w_in[e], rows[e, :, at : at + step], preferred_element_type=jnp.float32
            ).astype(jnp.bfloat16)
        for r, out in enumerate(outs):
            at = pl.multiple_of(owners[r] * share, share)
            store = pltpu.make_async_copy(
                sums.at[e, pl.ds(at, share)], out.at[e], sems.at[e, len(blocks) + 1 + r]
            )
            store.start()
            stores.append(store)
    for store in stores:
        store.wait()


def partial_rows(owners, weighted, blocks, start, stop):
    total, width, slots = weighted.shape
    experts = stop - start
    features = blocks[0].shape[1]
    count = owners.shape[0]
    return pl.pallas_call(
        functools.partial(partial_kernel, start, total),
        out_shape=[jax.ShapeDtypeStruct((experts, width // count, features), jnp.bfloat16)]
        * count,
        in_specs=[pl.BlockSpec(memory_space=pltpu.SMEM)] + [HBM] * (1 + len(blocks)),
        out_specs=[HBM] * count,
        scratch_shapes=[
            pltpu.VMEM((experts, width, slots), jnp.bfloat16),
            pltpu.VMEM((experts, slots, features), jnp.bfloat16),
            pltpu.VMEM((experts, width, features), jnp.bfloat16),
            pltpu.SemaphoreType.DMA((experts, 1 + len(blocks) + count)),
        ],
        compiler_params=pltpu.CompilerParams(vmem_limit_bytes=16 * MIB),
        cost_estimate=pl.CostEstimate(
            flops=2 * experts * width * slots * features,
            bytes_accessed=2 * experts * (width + slots) * features,
            transcendentals=0,
        ),
    )(owners, weighted, *blocks)


def root_of(x):
    inverse = lax.rsqrt(x)
    root = x * inverse
    return root + 0.5 * inverse * (x - root * root)


def reciprocal(x):
    estimate = pl.reciprocal(x, approx=True)
    return estimate * (2.0 - x * estimate)


def adam_kernel(count, owners, kept, first, at, *refs):
    del at
    partials, (w, m1, m2) = refs[:count], refs[count : count + 3]
    partials = [partials[i : i + owners] for i in range(0, count, owners)]
    new_w, new_m1, new_m2, full, copy, grad = refs[count + 3 + kept :]
    _, rows, features = partials[0][0].shape
    tiles = features // LANES
    places = [(span, e) for span in partials for e in range(span[0].shape[0])]
    experts = len(places)
    unit = tiles * experts
    stride = unit + 1
    for e, (span, at) in enumerate(places):
        total = span[0][at].astype(jnp.float32)
        for part in span[1:]:
            total = total + part[at].astype(jnp.float32)
        for t in range(tiles):
            grad[pl.ds(t * experts + e, rows, stride=stride), :] = total[
                :, t * LANES : (t + 1) * LANES
            ]
    block = rows * unit
    base = pl.multiple_of((first + pl.program_id(0)) * block, block)
    for h in range(rows):
        here = slice(h * unit, (h + 1) * unit)
        there = pl.ds(base + h * unit, unit)
        g = grad[h * stride : h * stride + unit]
        one = beta_one * m1[there] + (1.0 - beta_one) * g
        two = beta_two * m2[there] + (1.0 - beta_two) * g * g
        new_m1[here] = one
        new_m2[here] = two
        old = w[there]
        root = reciprocal(root_of(two * (1.0 / bias_two)) + adam_epsilon)
        new = old - learn_rate * (one * (1.0 / bias_one) * root + decay_rate * old)
        new_w[here] = new
        copy[here] = new.astype(jnp.bfloat16)
        full[here] = new.astype(jnp.bfloat16)


def adam_rows(at, partials, w, m1, m2, total_rows, before, first, steps):
    owners = len(partials[0])
    partials = [part for span in partials for part in span]
    _, rows, features = partials[0].shape
    experts = sum(part.shape[0] for part in partials) // owners
    block = 16
    flat = block * experts * features // LANES
    count, kept = len(partials), len(before)
    whole = rows // block
    parts = [
        pl.BlockSpec((part.shape[0], block, features), lambda i, at: (0, first + i, 0))
        for part in partials
    ]
    line = pl.BlockSpec((flat, LANES), lambda i, at: (first + i, 0))
    placed = pl.BlockSpec((flat, LANES), lambda i, at: (at[0] * whole + first + i, 0))
    return pl.pallas_call(
        functools.partial(adam_kernel, count, owners, kept, first),
        grid_spec=pltpu.PrefetchScalarGridSpec(
            num_scalar_prefetch=1,
            grid=(steps,),
            in_specs=parts + [INSIDE] * 3 + [HBM] * kept,
            out_specs=[line] * 3 + [placed, line],
            scratch_shapes=[pltpu.VMEM((flat + block, LANES), jnp.float32)],
        ),
        out_shape=[jax.ShapeDtypeStruct(w.shape, jnp.float32)] * 3
        + [
            jax.ShapeDtypeStruct((total_rows, LANES), jnp.bfloat16),
            jax.ShapeDtypeStruct(w.shape, jnp.bfloat16),
        ],
        input_output_aliases={4 + count + i: i for i in range(kept)},
        compiler_params=pltpu.CompilerParams(vmem_limit_bytes=10 * MIB),
        cost_estimate=SMALL,
    )(at, *partials, w, m1, m2, *before)


def place_kernel(at, got, full, out):
    del at, full
    out[...] = got[...]


def place_rows(owner, got, full):
    steps = 6
    block = got.shape[0] // steps
    return pl.pallas_call(
        place_kernel,
        grid_spec=pltpu.PrefetchScalarGridSpec(
            num_scalar_prefetch=1,
            grid=(steps,),
            in_specs=[pl.BlockSpec((block, LANES), lambda i, at: (i, 0)), HBM],
            out_specs=pl.BlockSpec((block, LANES), lambda i, at: (at[0] * steps + i, 0)),
        ),
        out_shape=jax.ShapeDtypeStruct(full.shape, full.dtype),
        input_output_aliases={2: 0},
        compiler_params=pltpu.CompilerParams(vmem_limit_bytes=14 * MIB),
        cost_estimate=pl.CostEstimate(flops=0, bytes_accessed=4 * got.size, transcendentals=0),
    )(owner, got, full)


def finish_kernel(pieces, target, probs, hidden, *refs):
    back, (d_hidden, d_probs, rows, states, outs, sums, sems) = refs[:-7], refs[-7:]
    count = back[0].shape[1]
    choices, width = hidden.shape
    slots = rows.shape[0]
    loads = [
        pltpu.make_async_copy(back[a].at[i], rows.at[pl.ds(n * count, count)], sems.at[n])
        for n, (a, i) in enumerate(pieces)
    ]
    loads.append(pltpu.make_async_copy(hidden, states, sems.at[len(pieces)]))
    for load in loads:
        load.start()
    targets, scales = target[...].T, probs[...].T
    for load in loads:
        load.wait()
    ones = jnp.ones((8, width), jnp.bfloat16)
    across = (((1,), (1,)), ((), ()))
    step = 2 * LANES
    stores = []
    for n, at in enumerate(range(0, choices, step)):
        here = slice(at, at + step)

        def column(table):
            return jnp.concatenate([table[:, 2 * n : 2 * n + 1], table[:, 2 * n + 1 : 2 * n + 2]])

        places = lax.broadcasted_iota(jnp.int32, (step, slots), 1)
        onehot = jnp.where(places == column(targets).astype(jnp.int32), 1.0, 0.0)
        g = jnp.dot(onehot.astype(jnp.bfloat16), rows[...], preferred_element_type=jnp.float32)
        outs[here] = (column(scales) * g).astype(jnp.bfloat16)
        stores.append(
            pltpu.make_async_copy(outs.at[here], d_hidden.at[here], sems.at[len(loads) + n])
        )
        stores[n].start()
        product = states[here].astype(jnp.float32) * g
        high = product.astype(jnp.bfloat16)
        low = (product - high.astype(jnp.float32)).astype(jnp.bfloat16)
        sums[:, here] = lax.dot_general(
            ones, high, across, preferred_element_type=jnp.float32
        ) + lax.dot_general(ones, low, across, preferred_element_type=jnp.float32)
    d_probs[...] = sums[...]
    for store in stores:
        store.wait()


def finish(target, probs, hidden, back, pieces):
    choices, width = hidden.shape
    slots = len(pieces) * back[0].shape[1]
    steps = choices // (2 * LANES)
    return pl.pallas_call(
        functools.partial(finish_kernel, pieces),
        out_shape=(
            jax.ShapeDtypeStruct((choices, width), jnp.bfloat16),
            jax.ShapeDtypeStruct((8, choices), jnp.float32),
        ),
        in_specs=[INSIDE, INSIDE] + [HBM] * (1 + len(back)),
        out_specs=(HBM, INSIDE),
        scratch_shapes=[
            pltpu.VMEM((slots, width), jnp.bfloat16),
            pltpu.VMEM((choices, width), jnp.bfloat16),
            pltpu.VMEM((choices, width), jnp.bfloat16),
            pltpu.VMEM((8, choices), jnp.float32),
            pltpu.SemaphoreType.DMA((len(pieces) + 1 + steps,)),
        ],
        compiler_params=pltpu.CompilerParams(vmem_limit_bytes=56 * MIB),
        cost_estimate=pl.CostEstimate(
            flops=2 * choices * slots * width, bytes_accessed=8 * hidden.size, transcendentals=0
        ),
    )(target, probs, hidden, *back)


def lane_view(array):
    h, e, d = array.shape
    return array.reshape(h, e, d // LANES, LANES).transpose(0, 2, 1, 3).reshape(-1, LANES)


def lane_unview(rows, shape):
    h, e, d = shape
    return rows.reshape(h, d // LANES, e, LANES).transpose(0, 2, 1, 3).reshape(shape)


def local(cotangent, hidden, probs, expert_ids, secondary, weight, moment1, moment2):
    token_count = cotangent.shape[0]
    top_k = expert_ids.shape[1]
    hidden_width = hidden.shape[2]
    experts = secondary.shape[1]
    size = lax.axis_size("inner")
    length = size // 4
    outer_size = lax.axis_size("outer")
    outer_at = lax.axis_index("outer")
    me = lax.axis_index("inner")
    choices = token_count * top_k
    slots = experts * CAP
    rows = weight.shape[0]

    flat_ids = expert_ids.reshape(choices)
    target = slot_targets(flat_ids)
    device = flat_ids // experts
    ring_steps = (ring_place(device // 4, length) - ring_place(me // 4, length)) % length
    relative = ring_steps * 4 + (device % 4 ^ me % 4)
    target = (relative - device) * slots + target
    all_slots = jnp.arange(size * slots, dtype=jnp.int32)
    matches = (all_slots[:, None] == target[None, :]).astype(jnp.bfloat16)
    weighted = (
        (probs[..., None] * hidden.astype(jnp.float32))
        .astype(jnp.bfloat16)
        .reshape(choices, hidden_width)
    )
    w_send = jnp.dot(matches, weighted, preferred_element_type=jnp.float32).astype(jnp.bfloat16)
    w_send = w_send.reshape(length, 4, slots, hidden_width)
    columns = tuple(
        v.astype(jnp.float32).reshape(choices // LANES, LANES) for v in (target, probs)
    )
    state = tuple(lane_view(a) for a in (weight, moment1, moment2))

    def move(block, steps, flip):
        return lax.ppermute(block, "inner", step_perm(size, steps, flip))

    tie = lax.optimization_barrier
    last = length - 1
    half = token_count // 2
    first = (me * experts).astype(jnp.int32)[None]
    tags = jnp.pad(expert_ids.astype(jnp.bfloat16), ((0, 0), (0, LANES - top_k)))
    own = jnp.concatenate([cotangent, tags], axis=1)
    by_expert = jnp.transpose(secondary, (1, 0, 2))
    near, parts, w_parts = {}, {}, {}
    d_rows, grads, back = {}, {}, {}

    def add_chunks(*chunks, vmem=56):
        found = chunk_grads(first, [parts[j] for j in chunks], by_expert, vmem)
        for j, d_chunk, g_chunk in zip(chunks, *found):
            d_rows[j], grads[j] = d_chunk, g_chunk

    def flips(arrays):
        return [move(a, 0, c) for c, a in enumerate(arrays, 1)]

    def whole(*arrays):
        return tuple((a, 0, a.shape[0]) for a in arrays)

    def halves(j):
        _, by_x, by_y = near[j]
        return (by_x[:half], by_y[half:])

    def far(low, high):
        return (move(low, 0, 2), move(high, 0, 1))

    for k in range(length + 1):
        moving = {}
        if k < last:
            moving["own"] = move(own, 1, 0)
        if k < length:
            moving["x"] = move(own, 0, 1)
            moving["y"] = move(own, 0, 2)
        if 1 < k < length:
            moving["far"] = far(*halves(k - 1))
        if k == length:
            both = zip(halves(last), first_cut)
            moving["far"] = far(*(jnp.concatenate(pair) for pair in both))
            for j in range(1, last - 1):
                back[j] = move(grads[j], -j, 0)
            moving["back"] = back
        if k > 2:
            add_chunks(k - 2)
        if k == 0:
            moving["columns"] = columns
        if k == 1:
            moving["cut"] = halves(0)
            moving["send"] = [w_send[j] for j in range(length)]
        if k == last - 1:
            moving["weights"] = by_expert
            w_parts[1] = move(w_send[1], 1, 0)
        if k == last:
            for j in range(last, 1, -1):
                w_parts[j] = move(w_send[j], j, 0)
        if k != 1:
            moving["send"] = w_send
        moving["done"] = (d_rows, grads, w_parts)
        moved = tie(moving)
        d_rows, grads, w_parts = moved["done"]
        w_send = moved["send"]
        if k == 0:
            columns = moved["columns"]
        if k == 1:
            first_cut = moved["cut"]
        if k == last - 1:
            by_expert = moved["weights"]
        if k == last:
            w_parts[0] = w_send[0]
            w_arrays = [w_parts[j] for j in range(length)]
            w_flipped = flips(regroup(w_arrays))
        if 1 < k < length:
            parts[k - 1] = whole(*near[k - 1]) + whole(*moved["far"])
        if k < length:
            near[k] = (own, moved["x"], moved["y"])
        own = moved.get("own")
    back = moved["back"]
    back[last - 1] = move(grads[last - 1], 1 - last, 0)
    parts[last] = whole(*near[last]) + tuple((f, 0, half) for f in moved["far"])
    parts[0] = whole(*near[0]) + tuple((f, half, half) for f in moved["far"])
    add_chunks(last, 0, vmem=56)
    back[last] = move(grads[last], -last, 0)
    back[0] = grads[0]
    back = [back[j] for j in range(length)]
    pieces = tuple((k, 0) if c == 0 else (length + c - 1, k) for k in range(length) for c in range(4))
    w_slots = order_slots(w_arrays + w_flipped, pieces)
    d_rows = [d_rows[j] for j in range(length)]

    def outer_perm(steps):
        return [(i, (i + steps) % outer_size) for i in range(outer_size)]

    owners = (outer_at + jnp.arange(outer_size, dtype=jnp.int32)) % outer_size
    partials = []
    for start, stop in ((0, experts // 2), (experts // 2, experts)):
        if start:
            d_rows, back = tie((d_rows, back))
        mine, *sent = partial_rows(owners, w_slots, d_rows, start, stop)
        partials.append(
            [mine]
            + [lax.ppermute(part, "outer", outer_perm(r)) for r, part in enumerate(sent, 1)]
        )
    partials, leaving = tie((partials, regroup(back)))
    flipped = flips(leaving)

    at = outer_at.astype(jnp.int32)[None]
    total_rows = secondary.size // LANES
    blocks = rows // 16
    cuts = [0, blocks - blocks // 3, blocks]
    outs = []
    for start, stop in zip(cuts[:-1], cuts[1:]):
        if stop == blocks:
            partials, flipped = tie((partials, flipped))
        outs = adam_rows(
            at, partials, *state, total_rows, outs, start, stop - start
        )
    new_weight, new_moment1, new_moment2, full, copy = outs
    for r in range(1, outer_size):
        got = lax.ppermute(copy, "outer", outer_perm(r))
        owner = (outer_at + outer_size - r) % outer_size
        full = place_rows(owner.astype(jnp.int32)[None], got, full)

    d_hidden, d_probs = finish(
        *columns, hidden.reshape(choices, hidden_width), back + flipped, pieces
    )
    return (
        d_hidden.reshape(hidden.shape),
        d_probs[0].reshape(probs.shape),
        lane_unview(new_weight, weight.shape),
        lane_unview(new_moment1, weight.shape),
        lane_unview(new_moment2, weight.shape),
        lane_unview(full, secondary.shape),
    )


def solution(mesh):
    in_specs = (
        P(("outer", "inner"), None),
        P(("outer", "inner"), None, None),
        P(("outer", "inner"), None),
        P(("outer", "inner"), None),
        P(None, "inner", None),
        P("outer", "inner", None),
        P("outer", "inner", None),
        P("outer", "inner", None),
    )
    out_specs = (
        P(("outer", "inner"), None, None),
        P(("outer", "inner"), None),
        P("outer", "inner", None),
        P("outer", "inner", None),
        P("outer", "inner", None),
        P(None, "inner", None),
    )
    return jax.shard_map(local, mesh=mesh, in_specs=in_specs, out_specs=out_specs, check_vma=False)
```

```python
import functools

import jax
import jax.numpy as jnp
from jax import lax
from jax.experimental import pallas as pl
from jax.experimental.pallas import tpu as pltpu
from jax.sharding import PartitionSpec as P

EXPERTS = 64
CAP = 24
TOP = 8
LANES = 128
MIB = 1 << 20
SMALL = pl.CostEstimate(flops=0, bytes_accessed=1 << 16, transcendentals=0)


beta_one = 0.9
beta_two = 0.95
adam_epsilon = 1e-08
learn_rate = 0.003
decay_rate = 0.1
bias_one = 1.0 - 0.9**20
bias_two = 1.0 - 0.95**20

HBM = pl.BlockSpec(memory_space=pltpu.HBM)
INSIDE = pl.BlockSpec(memory_space=pltpu.VMEM)


def slot_targets(flat_ids):
    count = flat_ids.shape[0]
    block = 128
    blocks = count // block
    onehot = (jnp.arange(EXPERTS, dtype=jnp.int32)[:, None] == flat_ids[None, :]).astype(
        jnp.bfloat16
    )
    tiles = onehot.reshape(EXPERTS, blocks, block)
    lower = (jnp.arange(block)[:, None] < jnp.arange(block)[None, :]).astype(jnp.bfloat16)
    within = jnp.einsum("ebk,kj->ebj", tiles, lower, preferred_element_type=jnp.float32)
    totals = jnp.sum(tiles.astype(jnp.float32), axis=2)
    small = (jnp.arange(blocks)[:, None] < jnp.arange(blocks)[None, :]).astype(jnp.float32)
    before = jnp.dot(totals, small, precision=lax.Precision.HIGHEST)
    ranking = (within + before[..., None]).reshape(EXPERTS, count)
    position = jnp.sum(ranking * onehot.astype(jnp.float32), axis=0).astype(jnp.int32)
    return flat_ids * CAP + position


def line_ring(length):
    return [0] + list(range(1, length, 2)) + list(range(2, length, 2))[::-1]


def ring_place(plane, length):
    return jnp.where(plane % 2 == 1, (plane + 1) // 2, (length - plane // 2) % length)


def ring_plane(place, length):
    up = 2 * place - 1
    down = 2 * (length - place)
    return jnp.where(place == 0, 0, jnp.where(up < length, up, down))


def step_perm(size, steps, flip):
    ring = line_ring(size // 4)
    after = {at: ring[(i + steps) % len(ring)] for i, at in enumerate(ring)}
    return [(i, after[i // 4] * 4 + (i % 4 ^ flip)) for i in range(size)]


def source_order(size):
    me = lax.axis_index("inner")
    length = size // 4
    steps = jnp.arange(length, dtype=jnp.int32)
    flips = jnp.arange(4, dtype=jnp.int32)
    at = ring_plane((ring_place(me // 4, length) - steps) % length, length)
    return (at[:, None] * 4 + (me % 4 ^ flips)[None, :]).reshape(size)


def grads_kernel(spans, keep, first, *refs):
    chunks = len(spans)
    parts = [
        [ref.at[pl.ds(*span)] for ref, span in zip(refs[5 * j :], spans[j])]
        for j in range(chunks)
    ]
    by_expert, outs = refs[5 * chunks], refs[5 * chunks + 1 : 7 * chunks + 1]
    all_rows, match, all_grads, weights, sems, weight_sems, *all_d_rows = refs[7 * chunks + 1 :]
    experts, width, features = by_expert.shape
    tokens = all_rows.shape[1] // 4
    slots = experts * CAP
    loads = []
    for j, pieces in enumerate(parts):
        at = 0
        loads.append([])
        for i, piece in enumerate(pieces):
            place = all_rows.at[j, pl.ds(at, piece.shape[0])]
            loads[j].append(pltpu.make_async_copy(piece, place, sems.at[j, i]))
            loads[j][i].start()
            at += piece.shape[0]
    weight_loads = [
        pltpu.make_async_copy(by_expert.at[e], weights.at[e], weight_sems.at[e])
        for e in range(experts)
    ]

    slot = lax.broadcasted_iota(jnp.int32, (slots, tokens), 0)
    expert = (first[0] + slot // CAP).astype(jnp.float32)
    place = (slot % CAP).astype(jnp.float32)
    earlier = lax.broadcasted_iota(jnp.int32, (tokens, tokens), 0)
    earlier = earlier < lax.broadcasted_iota(jnp.int32, (tokens, tokens), 1)
    earlier = jnp.where(earlier, 1.0, 0.0).astype(jnp.bfloat16)
    stores = []
    for j in range(chunks):
        rows, grads = all_rows.at[j], all_grads.at[j]
        d_rows = outs[2 * j] if keep else all_d_rows[0].at[j]
        for load in loads[j]:
            load.wait()
        if j == 0:
            for load in weight_loads:
                load.start()
        hits = []
        for c in range(4):
            ids = rows[c * tokens : (c + 1) * tokens, features:].astype(jnp.float32).T
            named = jnp.zeros((slots, tokens), jnp.float32)
            for k in range(TOP):
                named = jnp.where(expert == ids[k : k + 1], 1.0, named)
            rank = jnp.dot(
                named.astype(jnp.bfloat16), earlier, preferred_element_type=jnp.float32
            )
            hits.append(jnp.where(rank == place, named, 0.0))
        blank = jnp.zeros((CAP, tokens), jnp.float32)
        lines = []
        for e in range(experts):
            for c in range(4):
                line = [blank] * 4
                line[c] = hits[c][e * CAP : (e + 1) * CAP]
                lines.append(jnp.concatenate(line, axis=1))
        match[...] = jnp.concatenate(lines, axis=0).astype(jnp.bfloat16)

        step = min(512, features)
        for at in range(0, features, step):
            d_rows[:, at : at + step] = jnp.dot(
                match[...], rows[:, at : at + step], preferred_element_type=jnp.float32
            ).astype(jnp.bfloat16)
        if not keep:
            stores.append(pltpu.make_async_copy(d_rows, outs[2 * j], sems.at[j, 5]))
            stores[-1].start()
        count = 4 * CAP
        found = []
        for e in range(experts):
            if j == 0:
                weight_loads[e].wait()
            found.append(
                lax.dot_general(
                    d_rows[e * count : (e + 1) * count, :],
                    weights[e],
                    (((1,), (1,)), ((), ())),
                    preferred_element_type=jnp.float32,
                )
            )
        for c in range(4):
            mine = [f[c * CAP : (c + 1) * CAP] for f in found]
            grads[c] = jnp.concatenate(mine, axis=0).astype(jnp.bfloat16)
        stores.append(pltpu.make_async_copy(grads, outs[2 * j + 1], sems.at[j, 6]))
        stores[-1].start()
    for store in stores:
        store.wait()


def chunk_grads(first, parts, by_expert, keep):
    experts, width, features = by_expert.shape
    tokens, columns = parts[0][0][0].shape
    spans = tuple(tuple(piece[1:] for piece in part) for part in parts)
    slots = experts * CAP
    chunks = len(parts)
    found = pl.pallas_call(
        functools.partial(grads_kernel, spans, keep),
        out_shape=[
            jax.ShapeDtypeStruct((4 * slots, features), jnp.bfloat16),
            jax.ShapeDtypeStruct((4, slots, width), jnp.bfloat16),
        ]
        * chunks,
        in_specs=[pl.BlockSpec(memory_space=pltpu.SMEM)] + [HBM] * (5 * chunks + 1),
        out_specs=[INSIDE if keep else HBM, HBM] * chunks,
        scratch_shapes=[
            pltpu.VMEM((chunks, 4 * tokens, columns), jnp.bfloat16),
            pltpu.VMEM((4 * slots, 4 * tokens), jnp.bfloat16),
            pltpu.VMEM((chunks, 4, slots, width), jnp.bfloat16),
            pltpu.VMEM(by_expert.shape, jnp.bfloat16),
            pltpu.SemaphoreType.DMA((chunks, 7)),
            pltpu.SemaphoreType.DMA((experts,)),
        ]
        + ([] if keep else [pltpu.VMEM((chunks, 4 * slots, features), jnp.bfloat16)]),
        compiler_params=pltpu.CompilerParams(vmem_limit_bytes=(52 if keep else 56) * MIB),
        cost_estimate=pl.CostEstimate(
            flops=8 * chunks * slots * features * (4 * tokens + width),
            bytes_accessed=8 * chunks * (slots + tokens) * features,
            transcendentals=0,
        ),
    )(first, *(piece[0] for part in parts for piece in part), by_expert)
    return found[::2], found[1::2]


def order_kernel(pieces, *refs):
    arrays, (out, rows, wide, turned, sems) = refs[:-5], refs[-5:]
    size, slots, width = rows.shape
    experts = slots // CAP
    loads = [
        pltpu.make_async_copy(arrays[a].at[i], rows.at[n], sems.at[n])
        for n, (a, i) in enumerate(pieces)
    ]
    for load in loads:
        load.start()
    for n, load in enumerate(loads):
        load.wait()
        wide[n] = rows[n].astype(jnp.float32)
    for e in range(experts):
        mine = [wide[n, e * CAP : (e + 1) * CAP] for n in range(size)]
        turned[e] = jnp.concatenate(mine, axis=0).T.astype(jnp.bfloat16)
    store = pltpu.make_async_copy(turned, out, sems.at[size])
    store.start()
    store.wait()


def order_slots(arrays, pieces):
    slots, width = arrays[0].shape[1:]
    size = len(pieces)
    shape = (slots // CAP, width, size * CAP)
    return pl.pallas_call(
        functools.partial(order_kernel, pieces),
        out_shape=jax.ShapeDtypeStruct(shape, jnp.bfloat16),
        in_specs=[HBM] * len(arrays),
        out_specs=HBM,
        scratch_shapes=[
            pltpu.VMEM((size, slots, width), jnp.bfloat16),
            pltpu.VMEM((size, slots, width), jnp.float32),
            pltpu.VMEM(shape, jnp.bfloat16),
            pltpu.SemaphoreType.DMA((size + 1,)),
        ],
        compiler_params=pltpu.CompilerParams(vmem_limit_bytes=10 * MIB),
        cost_estimate=pl.CostEstimate(
            flops=0, bytes_accessed=8 * size * slots * width, transcendentals=0
        ),
    )(*arrays)


def regroup_kernel(*refs):
    count = len(refs) - 5
    arrays, outs, (held, sems) = refs[:count], refs[count:-2], refs[-2:]
    loads = [
        pltpu.make_async_copy(a.at[pl.ds(1, 3)], held.at[k], sems.at[k])
        for k, a in enumerate(arrays)
    ]
    for load in loads:
        load.start()
    for load in loads:
        load.wait()
    stores = [
        pltpu.make_async_copy(held.at[:, c], out, sems.at[count + c])
        for c, out in enumerate(outs)
    ]
    for store in stores:
        store.start()
    for store in stores:
        store.wait()


def regroup(arrays):
    _, slots, width = arrays[0].shape
    count = len(arrays)
    return pl.pallas_call(
        regroup_kernel,
        out_shape=[jax.ShapeDtypeStruct((count, slots, width), jnp.bfloat16)] * 3,
        in_specs=[HBM] * count,
        out_specs=[HBM] * 3,
        scratch_shapes=[
            pltpu.VMEM((count, 3, slots, width), jnp.bfloat16),
            pltpu.SemaphoreType.DMA((count + 3,)),
        ],
        compiler_params=pltpu.CompilerParams(vmem_limit_bytes=10 * MIB),
        cost_estimate=pl.CostEstimate(
            flops=0, bytes_accessed=12 * count * slots * width, transcendentals=0
        ),
    )(*arrays)


def partial_kernel(start, total, owners, weighted, *refs):
    count = owners.shape[0]
    blocks, outs = refs[: -4 - count], refs[-4 - count : -4]
    w_in, rows, sums, sems = refs[-4:]
    experts, width, features = sums.shape
    share = width // count
    slots = blocks[0].shape[0] // total
    loads = []
    for e in range(experts):
        mine = [(weighted.at[start + e], w_in.at[e])] + [
            (block.at[pl.ds((start + e) * slots, slots)], rows.at[e, pl.ds(k * slots, slots)])
            for k, block in enumerate(blocks)
        ]
        loads.append(
            [
                pltpu.make_async_copy(source, place, sems.at[e, i])
                for i, (source, place) in enumerate(mine)
            ]
        )
    stores = []
    step = min(1024, features)
    for load in loads[0]:
        load.start()
    for e in range(experts):
        if e + 1 < experts:
            for load in loads[e + 1]:
                load.start()
        for load in loads[e]:
            load.wait()
        for at in range(0, features, step):
            sums[e, :, at : at + step] = jnp.dot(
                w_in[e], rows[e, :, at : at + step], preferred_element_type=jnp.float32
            ).astype(jnp.bfloat16)
        for r, out in enumerate(outs):
            at = pl.multiple_of(owners[r] * share, share)
            store = pltpu.make_async_copy(
                sums.at[e, pl.ds(at, share)], out.at[e], sems.at[e, len(blocks) + 1 + r]
            )
            store.start()
            stores.append(store)
    for store in stores:
        store.wait()


def partial_rows(owners, weighted, blocks, start, stop):
    total, width, slots = weighted.shape
    experts = stop - start
    features = blocks[0].shape[1]
    count = owners.shape[0]
    return pl.pallas_call(
        functools.partial(partial_kernel, start, total),
        out_shape=[jax.ShapeDtypeStruct((experts, width // count, features), jnp.bfloat16)]
        * count,
        in_specs=[pl.BlockSpec(memory_space=pltpu.SMEM)] + [HBM] * (1 + len(blocks)),
        out_specs=[HBM] * count,
        scratch_shapes=[
            pltpu.VMEM((experts, width, slots), jnp.bfloat16),
            pltpu.VMEM((experts, slots, features), jnp.bfloat16),
            pltpu.VMEM((experts, width, features), jnp.bfloat16),
            pltpu.SemaphoreType.DMA((experts, 1 + len(blocks) + count)),
        ],
        compiler_params=pltpu.CompilerParams(vmem_limit_bytes=16 * MIB),
        cost_estimate=pl.CostEstimate(
            flops=2 * experts * width * slots * features,
            bytes_accessed=2 * experts * (width + slots) * features,
            transcendentals=0,
        ),
    )(owners, weighted, *blocks)


def root_of(x):
    inverse = lax.rsqrt(x)
    root = x * inverse
    return root + 0.5 * inverse * (x - root * root)


def reciprocal(x):
    estimate = pl.reciprocal(x, approx=True)
    return estimate * (2.0 - x * estimate)


def adam_kernel(count, owners, kept, first, at, *refs):
    del at
    partials, (w, m1, m2) = refs[:count], refs[count : count + 3]
    partials = [partials[i : i + owners] for i in range(0, count, owners)]
    new_w, new_m1, new_m2, full, copy, grad = refs[count + 3 + kept :]
    _, rows, features = partials[0][0].shape
    tiles = features // LANES
    places = [(span, e) for span in partials for e in range(span[0].shape[0])]
    experts = len(places)
    unit = tiles * experts
    stride = unit + 1
    for e, (span, at) in enumerate(places):
        total = span[0][at].astype(jnp.float32)
        for part in span[1:]:
            total = total + part[at].astype(jnp.float32)
        for t in range(tiles):
            grad[pl.ds(t * experts + e, rows, stride=stride), :] = total[
                :, t * LANES : (t + 1) * LANES
            ]
    block = rows * unit
    base = pl.multiple_of((first + pl.program_id(0)) * block, block)
    for h in range(rows):
        here = slice(h * unit, (h + 1) * unit)
        there = pl.ds(base + h * unit, unit)
        g = grad[h * stride : h * stride + unit]
        one = beta_one * m1[there] + (1.0 - beta_one) * g
        two = beta_two * m2[there] + (1.0 - beta_two) * g * g
        new_m1[here] = one
        new_m2[here] = two
        old = w[there]
        root = reciprocal(root_of(two * (1.0 / bias_two)) + adam_epsilon)
        new = old - learn_rate * (one * (1.0 / bias_one) * root + decay_rate * old)
        new_w[here] = new
        copy[here] = new.astype(jnp.bfloat16)
        full[here] = new.astype(jnp.bfloat16)


def adam_rows(at, partials, w, m1, m2, total_rows, before, first, steps):
    owners = len(partials[0])
    partials = [part for span in partials for part in span]
    _, rows, features = partials[0].shape
    experts = sum(part.shape[0] for part in partials) // owners
    block = 16
    flat = block * experts * features // LANES
    count, kept = len(partials), len(before)
    whole = rows // block
    parts = [
        pl.BlockSpec((part.shape[0], block, features), lambda i, at: (0, first + i, 0))
        for part in partials
    ]
    line = pl.BlockSpec((flat, LANES), lambda i, at: (first + i, 0))
    placed = pl.BlockSpec((flat, LANES), lambda i, at: (at[0] * whole + first + i, 0))
    return pl.pallas_call(
        functools.partial(adam_kernel, count, owners, kept, first),
        grid_spec=pltpu.PrefetchScalarGridSpec(
            num_scalar_prefetch=1,
            grid=(steps,),
            in_specs=parts + [INSIDE] * 3 + [HBM] * kept,
            out_specs=[line] * 3 + [placed, line],
            scratch_shapes=[pltpu.VMEM((flat + block, LANES), jnp.float32)],
        ),
        out_shape=[jax.ShapeDtypeStruct(w.shape, jnp.float32)] * 3
        + [
            jax.ShapeDtypeStruct((total_rows, LANES), jnp.bfloat16),
            jax.ShapeDtypeStruct(w.shape, jnp.bfloat16),
        ],
        input_output_aliases={4 + count + i: i for i in range(kept)},
        compiler_params=pltpu.CompilerParams(vmem_limit_bytes=10 * MIB),
        cost_estimate=SMALL,
    )(at, *partials, w, m1, m2, *before)


def place_kernel(at, got, full, out):
    del at, full
    out[...] = got[...]


def place_rows(owner, got, full):
    steps = 6
    block = got.shape[0] // steps
    return pl.pallas_call(
        place_kernel,
        grid_spec=pltpu.PrefetchScalarGridSpec(
            num_scalar_prefetch=1,
            grid=(steps,),
            in_specs=[pl.BlockSpec((block, LANES), lambda i, at: (i, 0)), HBM],
            out_specs=pl.BlockSpec((block, LANES), lambda i, at: (at[0] * steps + i, 0)),
        ),
        out_shape=jax.ShapeDtypeStruct(full.shape, full.dtype),
        input_output_aliases={2: 0},
        compiler_params=pltpu.CompilerParams(vmem_limit_bytes=14 * MIB),
        cost_estimate=pl.CostEstimate(flops=0, bytes_accessed=4 * got.size, transcendentals=0),
    )(owner, got, full)


def finish_kernel(pieces, target, probs, hidden, *refs):
    back, (d_hidden, d_probs, rows, states, outs, sums, sems) = refs[:-7], refs[-7:]
    count = back[0].shape[1]
    choices, width = hidden.shape
    slots = rows.shape[0]
    loads = [
        pltpu.make_async_copy(back[a].at[i], rows.at[pl.ds(n * count, count)], sems.at[n])
        for n, (a, i) in enumerate(pieces)
    ]
    loads.append(pltpu.make_async_copy(hidden, states, sems.at[len(pieces)]))
    for load in loads:
        load.start()
    targets, scales = target[...].T, probs[...].T
    for load in loads[:-1]:
        load.wait()
    ones = jnp.ones((8, width), jnp.bfloat16)
    across = (((1,), (1,)), ((), ()))
    step = 2 * LANES
    stores = []
    for n, at in enumerate(range(0, choices, step)):
        here = slice(at, at + step)

        def column(table):
            return jnp.concatenate([table[:, 2 * n : 2 * n + 1], table[:, 2 * n + 1 : 2 * n + 2]])

        places = lax.broadcasted_iota(jnp.int32, (step, slots), 1)
        onehot = jnp.where(places == column(targets).astype(jnp.int32), 1.0, 0.0)
        g = jnp.dot(onehot.astype(jnp.bfloat16), rows[...], preferred_element_type=jnp.float32)
        outs[here] = (column(scales) * g).astype(jnp.bfloat16)
        stores.append(
            pltpu.make_async_copy(outs.at[here], d_hidden.at[here], sems.at[len(loads) + n])
        )
        stores[n].start()
        if n == 0:
            loads[-1].wait()
        product = states[here].astype(jnp.float32) * g
        high = product.astype(jnp.bfloat16)
        low = (product - high.astype(jnp.float32)).astype(jnp.bfloat16)
        sums[:, here] = lax.dot_general(
            ones, high, across, preferred_element_type=jnp.float32
        ) + lax.dot_general(ones, low, across, preferred_element_type=jnp.float32)
    d_probs[...] = sums[...]
    for store in stores:
        store.wait()


def finish(target, probs, hidden, back, pieces):
    choices, width = hidden.shape
    slots = len(pieces) * back[0].shape[1]
    steps = choices // (2 * LANES)
    return pl.pallas_call(
        functools.partial(finish_kernel, pieces),
        out_shape=(
            jax.ShapeDtypeStruct((choices, width), jnp.bfloat16),
            jax.ShapeDtypeStruct((8, choices), jnp.float32),
        ),
        in_specs=[INSIDE, INSIDE] + [HBM] * (1 + len(back)),
        out_specs=(HBM, INSIDE),
        scratch_shapes=[
            pltpu.VMEM((slots, width), jnp.bfloat16),
            pltpu.VMEM((choices, width), jnp.bfloat16),
            pltpu.VMEM((choices, width), jnp.bfloat16),
            pltpu.VMEM((8, choices), jnp.float32),
            pltpu.SemaphoreType.DMA((len(pieces) + 1 + steps,)),
        ],
        compiler_params=pltpu.CompilerParams(vmem_limit_bytes=56 * MIB),
        cost_estimate=pl.CostEstimate(
            flops=2 * choices * slots * width, bytes_accessed=8 * hidden.size, transcendentals=0
        ),
    )(target, probs, hidden, *back)


def lane_view(array):
    h, e, d = array.shape
    return array.reshape(h, e, d // LANES, LANES).transpose(0, 2, 1, 3).reshape(-1, LANES)


def lane_unview(rows, shape):
    h, e, d = shape
    return rows.reshape(h, d // LANES, e, LANES).transpose(0, 2, 1, 3).reshape(shape)


def local(cotangent, hidden, probs, expert_ids, secondary, weight, moment1, moment2):
    token_count = cotangent.shape[0]
    top_k = expert_ids.shape[1]
    hidden_width = hidden.shape[2]
    experts = secondary.shape[1]
    size = lax.axis_size("inner")
    length = size // 4
    outer_size = lax.axis_size("outer")
    outer_at = lax.axis_index("outer")
    me = lax.axis_index("inner")
    choices = token_count * top_k
    slots = experts * CAP
    rows = weight.shape[0]

    flat_ids = expert_ids.reshape(choices)
    target = slot_targets(flat_ids)
    device = flat_ids // experts
    ring_steps = (ring_place(device // 4, length) - ring_place(me // 4, length)) % length
    relative = ring_steps * 4 + (device % 4 ^ me % 4)
    target = (relative - device) * slots + target
    all_slots = jnp.arange(size * slots, dtype=jnp.int32)
    matches = (all_slots[:, None] == target[None, :]).astype(jnp.bfloat16)
    weighted = (
        (probs[..., None] * hidden.astype(jnp.float32))
        .astype(jnp.bfloat16)
        .reshape(choices, hidden_width)
    )
    w_send = jnp.dot(matches, weighted, preferred_element_type=jnp.float32).astype(jnp.bfloat16)
    w_send = w_send.reshape(length, 4, slots, hidden_width)
    columns = tuple(
        v.astype(jnp.float32).reshape(choices // LANES, LANES) for v in (target, probs)
    )
    state = tuple(lane_view(a) for a in (weight, moment1, moment2))

    def move(block, steps, flip):
        return lax.ppermute(block, "inner", step_perm(size, steps, flip))

    tie = lax.optimization_barrier
    last = length - 1
    half = token_count // 2
    first = (me * experts).astype(jnp.int32)[None]
    tags = jnp.pad(expert_ids.astype(jnp.bfloat16), ((0, 0), (0, LANES - top_k)))
    own = jnp.concatenate([cotangent, tags], axis=1)
    by_expert = jnp.transpose(secondary, (1, 0, 2))
    near, parts, w_parts = {}, {}, {}
    d_rows, grads, back = {}, {}, {}

    def add_chunks(*chunks, keep=False):
        found = chunk_grads(first, [parts[j] for j in chunks], by_expert, keep)
        for j, d_chunk, g_chunk in zip(chunks, *found):
            d_rows[j], grads[j] = d_chunk, g_chunk

    def flips(arrays):
        return [move(a, 0, c) for c, a in enumerate(arrays, 1)]

    def whole(*arrays):
        return tuple((a, 0, a.shape[0]) for a in arrays)

    def halves(j):
        _, by_x, by_y = near[j]
        return (by_x[:half], by_y[half:])

    def far(low, high):
        return (move(low, 0, 2), move(high, 0, 1))

    for k in range(length + 1):
        moving = {}
        if k < last:
            moving["own"] = move(own, 1, 0)
        if k < length:
            moving["x"] = move(own, 0, 1)
            moving["y"] = move(own, 0, 2)
        if 1 < k < length:
            moving["far"] = far(*halves(k - 1))
        if k == length:
            both = zip(halves(last), first_cut)
            moving["far"] = far(*(jnp.concatenate(pair) for pair in both))
            for j in range(1, last - 1):
                back[j] = move(grads[j], -j, 0)
            moving["back"] = back
        if k > 2:
            add_chunks(k - 2)
        if k == 0:
            moving["columns"] = columns
        if k == 1:
            moving["cut"] = halves(0)
            moving["send"] = [w_send[j] for j in range(length)]
        if k == last - 1:
            moving["weights"] = by_expert
            w_parts[1] = move(w_send[1], 1, 0)
        if k == last:
            for j in range(last, 1, -1):
                w_parts[j] = move(w_send[j], j, 0)
        if k != 1:
            moving["send"] = w_send
        moving["done"] = (d_rows, grads, w_parts)
        moved = tie(moving)
        d_rows, grads, w_parts = moved["done"]
        w_send = moved["send"]
        if k == 0:
            columns = moved["columns"]
        if k == 1:
            first_cut = moved["cut"]
        if k == last - 1:
            by_expert = moved["weights"]
        if k == last:
            w_parts[0] = w_send[0]
            w_arrays = [w_parts[j] for j in range(length)]
            w_flipped = flips(regroup(w_arrays))
        if 1 < k < length:
            parts[k - 1] = whole(*near[k - 1]) + whole(*moved["far"])
        if k < length:
            near[k] = (own, moved["x"], moved["y"])
        own = moved.get("own")
    back = moved["back"]
    back[last - 1] = move(grads[last - 1], 1 - last, 0)
    parts[last] = whole(*near[last]) + tuple((f, 0, half) for f in moved["far"])
    parts[0] = whole(*near[0]) + tuple((f, half, half) for f in moved["far"])
    add_chunks(last, 0)
    back[last] = move(grads[last], -last, 0)
    back[0] = grads[0]
    back = [back[j] for j in range(length)]
    pieces = tuple((k, 0) if c == 0 else (length + c - 1, k) for k in range(length) for c in range(4))
    w_slots = order_slots(w_arrays + w_flipped, pieces)
    d_rows = [d_rows[j] for j in range(length)]

    def outer_perm(steps):
        return [(i, (i + steps) % outer_size) for i in range(outer_size)]

    owners = (outer_at + jnp.arange(outer_size, dtype=jnp.int32)) % outer_size
    partials = []
    for start, stop in ((0, experts // 2), (experts // 2, experts)):
        if start:
            d_rows, back = tie((d_rows, back))
        mine, *sent = partial_rows(owners, w_slots, d_rows, start, stop)
        partials.append(
            [mine]
            + [lax.ppermute(part, "outer", outer_perm(r)) for r, part in enumerate(sent, 1)]
        )
    partials, leaving = tie((partials, regroup(back)))
    flipped = flips(leaving)

    at = outer_at.astype(jnp.int32)[None]
    total_rows = secondary.size // LANES
    blocks = rows // 16
    cuts = [0, blocks - max(1, blocks // 6), blocks]
    outs = []
    for start, stop in zip(cuts[:-1], cuts[1:]):
        if stop == blocks:
            partials, flipped = tie((partials, flipped))
        outs = adam_rows(
            at, partials, *state, total_rows, outs, start, stop - start
        )
    new_weight, new_moment1, new_moment2, full, copy = outs
    for r in range(1, outer_size):
        got = lax.ppermute(copy, "outer", outer_perm(r))
        owner = (outer_at + outer_size - r) % outer_size
        full = place_rows(owner.astype(jnp.int32)[None], got, full)

    d_hidden, d_probs = finish(
        *columns, hidden.reshape(choices, hidden_width), back + flipped, pieces
    )
    return (
        d_hidden.reshape(hidden.shape),
        d_probs[0].reshape(probs.shape),
        lane_unview(new_weight, weight.shape),
        lane_unview(new_moment1, weight.shape),
        lane_unview(new_moment2, weight.shape),
        lane_unview(full, secondary.shape),
    )


def solution(mesh):
    in_specs = (
        P(("outer", "inner"), None),
        P(("outer", "inner"), None, None),
        P(("outer", "inner"), None),
        P(("outer", "inner"), None),
        P(None, "inner", None),
        P("outer", "inner", None),
        P("outer", "inner", None),
        P("outer", "inner", None),
    )
    out_specs = (
        P(("outer", "inner"), None, None),
        P(("outer", "inner"), None),
        P("outer", "inner", None),
        P("outer", "inner", None),
        P("outer", "inner", None),
        P(None, "inner", None),
    )
    return jax.shard_map(local, mesh=mesh, in_specs=in_specs, out_specs=out_specs, check_vma=False)
```

```python
import functools

import jax
import jax.numpy as jnp
from jax import lax
from jax.experimental import pallas as pl
from jax.experimental.pallas import tpu as pltpu
from jax.sharding import PartitionSpec as P

EXPERTS = 64
CAP = 24
TOP = 8
LANES = 128
MIB = 1 << 20
SMALL = pl.CostEstimate(flops=0, bytes_accessed=1 << 16, transcendentals=0)


beta_one = 0.9
beta_two = 0.95
adam_epsilon = 1e-08
learn_rate = 0.003
decay_rate = 0.1
bias_one = 1.0 - 0.9**20
bias_two = 1.0 - 0.95**20

HBM = pl.BlockSpec(memory_space=pltpu.HBM)
INSIDE = pl.BlockSpec(memory_space=pltpu.VMEM)


def slot_targets(flat_ids):
    count = flat_ids.shape[0]
    block = 128
    blocks = count // block
    onehot = (jnp.arange(EXPERTS, dtype=jnp.int32)[:, None] == flat_ids[None, :]).astype(
        jnp.bfloat16
    )
    tiles = onehot.reshape(EXPERTS, blocks, block)
    lower = (jnp.arange(block)[:, None] < jnp.arange(block)[None, :]).astype(jnp.bfloat16)
    within = jnp.einsum("ebk,kj->ebj", tiles, lower, preferred_element_type=jnp.float32)
    totals = jnp.sum(tiles.astype(jnp.float32), axis=2)
    small = (jnp.arange(blocks)[:, None] < jnp.arange(blocks)[None, :]).astype(jnp.float32)
    before = jnp.dot(totals, small, precision=lax.Precision.HIGHEST)
    ranking = (within + before[..., None]).reshape(EXPERTS, count)
    position = jnp.sum(ranking * onehot.astype(jnp.float32), axis=0).astype(jnp.int32)
    return flat_ids * CAP + position


def line_ring(length):
    return [0] + list(range(1, length, 2)) + list(range(2, length, 2))[::-1]


def ring_place(plane, length):
    return jnp.where(plane % 2 == 1, (plane + 1) // 2, (length - plane // 2) % length)


def ring_plane(place, length):
    up = 2 * place - 1
    down = 2 * (length - place)
    return jnp.where(place == 0, 0, jnp.where(up < length, up, down))


def step_perm(size, steps, flip):
    ring = line_ring(size // 4)
    after = {at: ring[(i + steps) % len(ring)] for i, at in enumerate(ring)}
    return [(i, after[i // 4] * 4 + (i % 4 ^ flip)) for i in range(size)]


def source_order(size):
    me = lax.axis_index("inner")
    length = size // 4
    steps = jnp.arange(length, dtype=jnp.int32)
    flips = jnp.arange(4, dtype=jnp.int32)
    at = ring_plane((ring_place(me // 4, length) - steps) % length, length)
    return (at[:, None] * 4 + (me % 4 ^ flips)[None, :]).reshape(size)


def grads_kernel(spans, keep, first, *refs):
    chunks = len(spans)
    parts = [
        [ref.at[pl.ds(*span)] for ref, span in zip(refs[5 * j :], spans[j])]
        for j in range(chunks)
    ]
    by_expert, outs = refs[5 * chunks], refs[5 * chunks + 1 : 7 * chunks + 1]
    all_rows, match, all_grads, weights, sems, weight_sems, *all_d_rows = refs[7 * chunks + 1 :]
    experts, width, features = by_expert.shape
    tokens = all_rows.shape[1] // 4
    slots = experts * CAP
    loads = []
    for j, pieces in enumerate(parts):
        at = 0
        loads.append([])
        for i, piece in enumerate(pieces):
            place = all_rows.at[j, pl.ds(at, piece.shape[0])]
            loads[j].append(pltpu.make_async_copy(piece, place, sems.at[j, i]))
            loads[j][i].start()
            at += piece.shape[0]
    weight_loads = [
        pltpu.make_async_copy(by_expert.at[e], weights.at[e], weight_sems.at[e])
        for e in range(experts)
    ]

    slot = lax.broadcasted_iota(jnp.int32, (slots, tokens), 0)
    expert = (first[0] + slot // CAP).astype(jnp.float32)
    place = (slot % CAP).astype(jnp.float32)
    earlier = lax.broadcasted_iota(jnp.int32, (tokens, tokens), 0)
    earlier = earlier < lax.broadcasted_iota(jnp.int32, (tokens, tokens), 1)
    earlier = jnp.where(earlier, 1.0, 0.0).astype(jnp.bfloat16)
    stores = []
    for j in range(chunks):
        rows, grads = all_rows.at[j], all_grads.at[j]
        d_rows = outs[2 * j] if keep else all_d_rows[0].at[j]
        for load in loads[j]:
            load.wait()
        if j == 0:
            for load in weight_loads:
                load.start()
        hits = []
        for c in range(4):
            ids = rows[c * tokens : (c + 1) * tokens, features:].astype(jnp.float32).T
            named = jnp.zeros((slots, tokens), jnp.float32)
            for k in range(TOP):
                named = jnp.where(expert == ids[k : k + 1], 1.0, named)
            rank = jnp.dot(
                named.astype(jnp.bfloat16), earlier, preferred_element_type=jnp.float32
            )
            hits.append(jnp.where(rank == place, named, 0.0))
        blank = jnp.zeros((CAP, tokens), jnp.float32)
        lines = []
        for e in range(experts):
            for c in range(4):
                line = [blank] * 4
                line[c] = hits[c][e * CAP : (e + 1) * CAP]
                lines.append(jnp.concatenate(line, axis=1))
        match[...] = jnp.concatenate(lines, axis=0).astype(jnp.bfloat16)

        step = min(512, features)
        for at in range(0, features, step):
            d_rows[:, at : at + step] = jnp.dot(
                match[...], rows[:, at : at + step], preferred_element_type=jnp.float32
            ).astype(jnp.bfloat16)
        if not keep:
            stores.append(pltpu.make_async_copy(d_rows, outs[2 * j], sems.at[j, 5]))
            stores[-1].start()
        count = 4 * CAP
        found = []
        for e in range(experts):
            if j == 0:
                weight_loads[e].wait()
            found.append(
                lax.dot_general(
                    d_rows[e * count : (e + 1) * count, :],
                    weights[e],
                    (((1,), (1,)), ((), ())),
                    preferred_element_type=jnp.float32,
                )
            )
        for c in range(4):
            mine = [f[c * CAP : (c + 1) * CAP] for f in found]
            grads[c] = jnp.concatenate(mine, axis=0).astype(jnp.bfloat16)
        stores.append(pltpu.make_async_copy(grads, outs[2 * j + 1], sems.at[j, 6]))
        stores[-1].start()
    for store in stores:
        store.wait()


def chunk_grads(first, parts, by_expert, keep):
    experts, width, features = by_expert.shape
    tokens, columns = parts[0][0][0].shape
    spans = tuple(tuple(piece[1:] for piece in part) for part in parts)
    slots = experts * CAP
    chunks = len(parts)
    found = pl.pallas_call(
        functools.partial(grads_kernel, spans, keep),
        out_shape=[
            jax.ShapeDtypeStruct((4 * slots, features), jnp.bfloat16),
            jax.ShapeDtypeStruct((4, slots, width), jnp.bfloat16),
        ]
        * chunks,
        in_specs=[pl.BlockSpec(memory_space=pltpu.SMEM)] + [HBM] * (5 * chunks + 1),
        out_specs=[INSIDE if keep else HBM, HBM] * chunks,
        scratch_shapes=[
            pltpu.VMEM((chunks, 4 * tokens, columns), jnp.bfloat16),
            pltpu.VMEM((4 * slots, 4 * tokens), jnp.bfloat16),
            pltpu.VMEM((chunks, 4, slots, width), jnp.bfloat16),
            pltpu.VMEM(by_expert.shape, jnp.bfloat16),
            pltpu.SemaphoreType.DMA((chunks, 7)),
            pltpu.SemaphoreType.DMA((experts,)),
        ]
        + ([] if keep else [pltpu.VMEM((chunks, 4 * slots, features), jnp.bfloat16)]),
        compiler_params=pltpu.CompilerParams(vmem_limit_bytes=(52 if keep else 56) * MIB),
        cost_estimate=pl.CostEstimate(
            flops=8 * chunks * slots * features * (4 * tokens + width),
            bytes_accessed=8 * chunks * (slots + tokens) * features,
            transcendentals=0,
        ),
    )(first, *(piece[0] for part in parts for piece in part), by_expert)
    return found[::2], found[1::2]


def order_kernel(pieces, *refs):
    arrays, (out, rows, wide, turned, sems) = refs[:-5], refs[-5:]
    size, slots, width = rows.shape
    experts = slots // CAP
    loads = [
        pltpu.make_async_copy(arrays[a].at[i], rows.at[n], sems.at[n])
        for n, (a, i) in enumerate(pieces)
    ]
    for load in loads:
        load.start()
    for n, load in enumerate(loads):
        load.wait()
        wide[n] = rows[n].astype(jnp.float32)
    for e in range(experts):
        mine = [wide[n, e * CAP : (e + 1) * CAP] for n in range(size)]
        turned[e] = jnp.concatenate(mine, axis=0).T.astype(jnp.bfloat16)
    store = pltpu.make_async_copy(turned, out, sems.at[size])
    store.start()
    store.wait()


def order_slots(arrays, pieces):
    slots, width = arrays[0].shape[1:]
    size = len(pieces)
    shape = (slots // CAP, width, size * CAP)
    return pl.pallas_call(
        functools.partial(order_kernel, pieces),
        out_shape=jax.ShapeDtypeStruct(shape, jnp.bfloat16),
        in_specs=[HBM] * len(arrays),
        out_specs=HBM,
        scratch_shapes=[
            pltpu.VMEM((size, slots, width), jnp.bfloat16),
            pltpu.VMEM((size, slots, width), jnp.float32),
            pltpu.VMEM(shape, jnp.bfloat16),
            pltpu.SemaphoreType.DMA((size + 1,)),
        ],
        compiler_params=pltpu.CompilerParams(vmem_limit_bytes=10 * MIB),
        cost_estimate=pl.CostEstimate(
            flops=0, bytes_accessed=8 * size * slots * width, transcendentals=0
        ),
    )(*arrays)


def regroup_kernel(*refs):
    count = len(refs) - 5
    arrays, outs, (held, sems) = refs[:count], refs[count:-2], refs[-2:]
    loads = [
        pltpu.make_async_copy(a.at[pl.ds(1, 3)], held.at[k], sems.at[k])
        for k, a in enumerate(arrays)
    ]
    for load in loads:
        load.start()
    for load in loads:
        load.wait()
    stores = [
        pltpu.make_async_copy(held.at[:, c], out, sems.at[count + c])
        for c, out in enumerate(outs)
    ]
    for store in stores:
        store.start()
    for store in stores:
        store.wait()


def regroup(arrays):
    _, slots, width = arrays[0].shape
    count = len(arrays)
    return pl.pallas_call(
        regroup_kernel,
        out_shape=[jax.ShapeDtypeStruct((count, slots, width), jnp.bfloat16)] * 3,
        in_specs=[HBM] * count,
        out_specs=[HBM] * 3,
        scratch_shapes=[
            pltpu.VMEM((count, 3, slots, width), jnp.bfloat16),
            pltpu.SemaphoreType.DMA((count + 3,)),
        ],
        compiler_params=pltpu.CompilerParams(vmem_limit_bytes=10 * MIB),
        cost_estimate=pl.CostEstimate(
            flops=0, bytes_accessed=12 * count * slots * width, transcendentals=0
        ),
    )(*arrays)


def partial_kernel(start, total, owners, weighted, *refs):
    count = owners.shape[0]
    blocks, outs = refs[: -4 - count], refs[-4 - count : -4]
    w_in, rows, sums, sems = refs[-4:]
    experts, width, features = sums.shape
    share = width // count
    slots = blocks[0].shape[0] // total
    loads = []
    for e in range(experts):
        mine = [(weighted.at[start + e], w_in.at[e])] + [
            (block.at[pl.ds((start + e) * slots, slots)], rows.at[e, pl.ds(k * slots, slots)])
            for k, block in enumerate(blocks)
        ]
        loads.append(
            [
                pltpu.make_async_copy(source, place, sems.at[e, i])
                for i, (source, place) in enumerate(mine)
            ]
        )
    stores = []
    step = min(1024, features)
    for load in loads[0]:
        load.start()
    for e in range(experts):
        if e + 1 < experts:
            for load in loads[e + 1]:
                load.start()
        for load in loads[e]:
            load.wait()
        for at in range(0, features, step):
            sums[e, :, at : at + step] = jnp.dot(
                w_in[e], rows[e, :, at : at + step], preferred_element_type=jnp.float32
            ).astype(jnp.bfloat16)
        for r, out in enumerate(outs):
            at = pl.multiple_of(owners[r] * share, share)
            store = pltpu.make_async_copy(
                sums.at[e, pl.ds(at, share)], out.at[e], sems.at[e, len(blocks) + 1 + r]
            )
            store.start()
            stores.append(store)
    for store in stores:
        store.wait()


def partial_rows(owners, weighted, blocks, start, stop):
    total, width, slots = weighted.shape
    experts = stop - start
    features = blocks[0].shape[1]
    count = owners.shape[0]
    return pl.pallas_call(
        functools.partial(partial_kernel, start, total),
        out_shape=[jax.ShapeDtypeStruct((experts, width // count, features), jnp.bfloat16)]
        * count,
        in_specs=[pl.BlockSpec(memory_space=pltpu.SMEM)] + [HBM] * (1 + len(blocks)),
        out_specs=[HBM] * count,
        scratch_shapes=[
            pltpu.VMEM((experts, width, slots), jnp.bfloat16),
            pltpu.VMEM((experts, slots, features), jnp.bfloat16),
            pltpu.VMEM((experts, width, features), jnp.bfloat16),
            pltpu.SemaphoreType.DMA((experts, 1 + len(blocks) + count)),
        ],
        compiler_params=pltpu.CompilerParams(vmem_limit_bytes=16 * MIB),
        cost_estimate=pl.CostEstimate(
            flops=2 * experts * width * slots * features,
            bytes_accessed=2 * experts * (width + slots) * features,
            transcendentals=0,
        ),
    )(owners, weighted, *blocks)


def root_of(x):
    inverse = lax.rsqrt(x)
    root = x * inverse
    return root + 0.5 * inverse * (x - root * root)


def reciprocal(x):
    estimate = pl.reciprocal(x, approx=True)
    return estimate * (2.0 - x * estimate)


def adam_kernel(count, owners, kept, first, at, *refs):
    del at
    partials, (w, m1, m2) = refs[:count], refs[count : count + 3]
    partials = [partials[i : i + owners] for i in range(0, count, owners)]
    new_w, new_m1, new_m2, full, copy, grad = refs[count + 3 + kept :]
    _, rows, features = partials[0][0].shape
    tiles = features // LANES
    places = [(span, e) for span in partials for e in range(span[0].shape[0])]
    experts = len(places)
    unit = tiles * experts
    stride = unit + 1
    for e, (span, at) in enumerate(places):
        total = span[0][at].astype(jnp.float32)
        for part in span[1:]:
            total = total + part[at].astype(jnp.float32)
        for t in range(tiles):
            grad[pl.ds(t * experts + e, rows, stride=stride), :] = total[
                :, t * LANES : (t + 1) * LANES
            ]
    block = rows * unit
    base = pl.multiple_of((first + pl.program_id(0)) * block, block)
    for h in range(rows):
        here = slice(h * unit, (h + 1) * unit)
        there = pl.ds(base + h * unit, unit)
        g = grad[h * stride : h * stride + unit]
        one = beta_one * m1[there] + (1.0 - beta_one) * g
        two = beta_two * m2[there] + (1.0 - beta_two) * g * g
        new_m1[here] = one
        new_m2[here] = two
        old = w[there]
        root = reciprocal(root_of(two * (1.0 / bias_two)) + adam_epsilon)
        new = old - learn_rate * (one * (1.0 / bias_one) * root + decay_rate * old)
        new_w[here] = new
        copy[here] = new.astype(jnp.bfloat16)
        full[here] = new.astype(jnp.bfloat16)


def adam_rows(at, partials, w, m1, m2, total_rows, before, first, steps):
    owners = len(partials[0])
    partials = [part for span in partials for part in span]
    _, rows, features = partials[0].shape
    experts = sum(part.shape[0] for part in partials) // owners
    block = 16
    flat = block * experts * features // LANES
    count, kept = len(partials), len(before)
    whole = rows // block
    parts = [
        pl.BlockSpec((part.shape[0], block, features), lambda i, at: (0, first + i, 0))
        for part in partials
    ]
    line = pl.BlockSpec((flat, LANES), lambda i, at: (first + i, 0))
    placed = pl.BlockSpec((flat, LANES), lambda i, at: (at[0] * whole + first + i, 0))
    return pl.pallas_call(
        functools.partial(adam_kernel, count, owners, kept, first),
        grid_spec=pltpu.PrefetchScalarGridSpec(
            num_scalar_prefetch=1,
            grid=(steps,),
            in_specs=parts + [INSIDE] * 3 + [HBM] * kept,
            out_specs=[line] * 3 + [placed, line],
            scratch_shapes=[pltpu.VMEM((flat + block, LANES), jnp.float32)],
        ),
        out_shape=[jax.ShapeDtypeStruct(w.shape, jnp.float32)] * 3
        + [
            jax.ShapeDtypeStruct((total_rows, LANES), jnp.bfloat16),
            jax.ShapeDtypeStruct(w.shape, jnp.bfloat16),
        ],
        input_output_aliases={4 + count + i: i for i in range(kept)},
        compiler_params=pltpu.CompilerParams(vmem_limit_bytes=10 * MIB),
        cost_estimate=SMALL,
    )(at, *partials, w, m1, m2, *before)


def place_kernel(at, got, full, out):
    del at, full
    out[...] = got[...]


def place_rows(owner, got, full):
    steps = 6
    block = got.shape[0] // steps
    return pl.pallas_call(
        place_kernel,
        grid_spec=pltpu.PrefetchScalarGridSpec(
            num_scalar_prefetch=1,
            grid=(steps,),
            in_specs=[pl.BlockSpec((block, LANES), lambda i, at: (i, 0)), HBM],
            out_specs=pl.BlockSpec((block, LANES), lambda i, at: (at[0] * steps + i, 0)),
        ),
        out_shape=jax.ShapeDtypeStruct(full.shape, full.dtype),
        input_output_aliases={2: 0},
        compiler_params=pltpu.CompilerParams(vmem_limit_bytes=14 * MIB),
        cost_estimate=pl.CostEstimate(flops=0, bytes_accessed=4 * got.size, transcendentals=0),
    )(owner, got, full)


def finish_kernel(pieces, target, probs, hidden, *refs):
    back, (d_hidden, d_probs, rows, states, outs, sems) = refs[:-6], refs[-6:]
    count = back[0].shape[1]
    choices, width = hidden.shape
    slots = rows.shape[0]
    loads = [
        pltpu.make_async_copy(back[a].at[i], rows.at[pl.ds(n * count, count)], sems.at[n])
        for n, (a, i) in enumerate(pieces)
    ]
    loads.append(pltpu.make_async_copy(hidden, states, sems.at[len(pieces)]))
    for load in loads:
        load.start()
    targets, scales = target[...].T, probs[...].T
    for load in loads[:-1]:
        load.wait()
    ones = jnp.ones((TOP, width), jnp.bfloat16)
    across = (((1,), (1,)), ((), ()))
    step = 2 * LANES
    row = lax.broadcasted_iota(jnp.int32, (TOP, step), 0)
    choice = lax.broadcasted_iota(jnp.int32, (TOP, step), 1) % TOP
    token = lax.broadcasted_iota(jnp.int32, (step, choices // TOP), 0) // TOP
    lane = lax.broadcasted_iota(jnp.int32, (step, choices // TOP), 1)
    total = jnp.zeros((TOP, choices // TOP), jnp.float32)
    stores = []
    for n, at in enumerate(range(0, choices, step)):
        here = slice(at, at + step)

        def column(table):
            return jnp.concatenate([table[:, 2 * n : 2 * n + 1], table[:, 2 * n + 1 : 2 * n + 2]])

        places = lax.broadcasted_iota(jnp.int32, (step, slots), 1)
        onehot = jnp.where(places == column(targets).astype(jnp.int32), 1.0, 0.0)
        g = jnp.dot(onehot.astype(jnp.bfloat16), rows[...], preferred_element_type=jnp.float32)
        outs[here] = (column(scales) * g).astype(jnp.bfloat16)
        stores.append(
            pltpu.make_async_copy(outs.at[here], d_hidden.at[here], sems.at[len(loads) + n])
        )
        stores[n].start()
        if n == 0:
            loads[-1].wait()
        product = states[here].astype(jnp.float32) * g
        high = product.astype(jnp.bfloat16)
        low = (product - high.astype(jnp.float32)).astype(jnp.bfloat16)
        sums = lax.dot_general(
            ones, high, across, preferred_element_type=jnp.float32
        ) + lax.dot_general(ones, low, across, preferred_element_type=jnp.float32)
        sums = jnp.where(choice == row, sums, 0.0)
        high = sums.astype(jnp.bfloat16)
        low = (sums - high.astype(jnp.float32)).astype(jnp.bfloat16)
        chosen = jnp.where(token + at // TOP == lane, 1.0, 0.0).astype(jnp.bfloat16)
        total = (
            total
            + jnp.dot(high, chosen, preferred_element_type=jnp.float32)
            + jnp.dot(low, chosen, preferred_element_type=jnp.float32)
        )
    d_probs[...] = total
    for store in stores:
        store.wait()


def finish(target, probs, hidden, back, pieces):
    choices, width = hidden.shape
    slots = len(pieces) * back[0].shape[1]
    steps = choices // (2 * LANES)
    return pl.pallas_call(
        functools.partial(finish_kernel, pieces),
        out_shape=(
            jax.ShapeDtypeStruct((choices, width), jnp.bfloat16),
            jax.ShapeDtypeStruct((TOP, choices // TOP), jnp.float32),
        ),
        in_specs=[INSIDE, INSIDE] + [HBM] * (1 + len(back)),
        out_specs=(HBM, INSIDE),
        scratch_shapes=[
            pltpu.VMEM((slots, width), jnp.bfloat16),
            pltpu.VMEM((choices, width), jnp.bfloat16),
            pltpu.VMEM((choices, width), jnp.bfloat16),
            pltpu.SemaphoreType.DMA((len(pieces) + 1 + steps,)),
        ],
        compiler_params=pltpu.CompilerParams(vmem_limit_bytes=56 * MIB),
        cost_estimate=pl.CostEstimate(
            flops=2 * choices * slots * width, bytes_accessed=8 * hidden.size, transcendentals=0
        ),
    )(target, probs, hidden, *back)


def lane_view(array):
    h, e, d = array.shape
    return array.reshape(h, e, d // LANES, LANES).transpose(0, 2, 1, 3).reshape(-1, LANES)


def lane_unview(rows, shape):
    h, e, d = shape
    return rows.reshape(h, d // LANES, e, LANES).transpose(0, 2, 1, 3).reshape(shape)


def local(cotangent, hidden, probs, expert_ids, secondary, weight, moment1, moment2):
    token_count = cotangent.shape[0]
    top_k = expert_ids.shape[1]
    hidden_width = hidden.shape[2]
    experts = secondary.shape[1]
    size = lax.axis_size("inner")
    length = size // 4
    outer_size = lax.axis_size("outer")
    outer_at = lax.axis_index("outer")
    me = lax.axis_index("inner")
    choices = token_count * top_k
    slots = experts * CAP
    rows = weight.shape[0]

    flat_ids = expert_ids.reshape(choices)
    target = slot_targets(flat_ids)
    device = flat_ids // experts
    ring_steps = (ring_place(device // 4, length) - ring_place(me // 4, length)) % length
    relative = ring_steps * 4 + (device % 4 ^ me % 4)
    target = (relative - device) * slots + target
    all_slots = jnp.arange(size * slots, dtype=jnp.int32)
    matches = (all_slots[:, None] == target[None, :]).astype(jnp.bfloat16)
    weighted = (
        (probs[..., None] * hidden.astype(jnp.float32))
        .astype(jnp.bfloat16)
        .reshape(choices, hidden_width)
    )
    w_send = jnp.dot(matches, weighted, preferred_element_type=jnp.float32).astype(jnp.bfloat16)
    w_send = w_send.reshape(length, 4, slots, hidden_width)
    columns = tuple(
        v.astype(jnp.float32).reshape(choices // LANES, LANES) for v in (target, probs)
    )
    state = tuple(lane_view(a) for a in (weight, moment1, moment2))

    def move(block, steps, flip):
        return lax.ppermute(block, "inner", step_perm(size, steps, flip))

    tie = lax.optimization_barrier
    last = length - 1
    half = token_count // 2
    first = (me * experts).astype(jnp.int32)[None]
    tags = jnp.pad(expert_ids.astype(jnp.bfloat16), ((0, 0), (0, LANES - top_k)))
    own = jnp.concatenate([cotangent, tags], axis=1)
    by_expert = jnp.transpose(secondary, (1, 0, 2))
    near, parts, w_parts = {}, {}, {}
    d_rows, grads, back = {}, {}, {}

    def add_chunks(*chunks, keep=False):
        found = chunk_grads(first, [parts[j] for j in chunks], by_expert, keep)
        for j, d_chunk, g_chunk in zip(chunks, *found):
            d_rows[j], grads[j] = d_chunk, g_chunk

    def flips(arrays):
        return [move(a, 0, c) for c, a in enumerate(arrays, 1)]

    def whole(*arrays):
        return tuple((a, 0, a.shape[0]) for a in arrays)

    def halves(j):
        _, by_x, by_y = near[j]
        return (by_x[:half], by_y[half:])

    def far(low, high):
        return (move(low, 0, 2), move(high, 0, 1))

    for k in range(length + 1):
        moving = {}
        if k < last:
            moving["own"] = move(own, 1, 0)
        if k < length:
            moving["x"] = move(own, 0, 1)
            moving["y"] = move(own, 0, 2)
        if 1 < k < length:
            moving["far"] = far(*halves(k - 1))
        if k == length:
            both = zip(halves(last), first_cut)
            moving["far"] = far(*(jnp.concatenate(pair) for pair in both))
            for j in range(1, last - 1):
                back[j] = move(grads[j], -j, 0)
            moving["back"] = back
        if k > 2:
            add_chunks(k - 2)
        if k == 0:
            moving["columns"] = columns
        if k == 1:
            moving["cut"] = halves(0)
            moving["send"] = [w_send[j] for j in range(length)]
        if k == last - 1:
            moving["weights"] = by_expert
            w_parts[1] = move(w_send[1], 1, 0)
        if k == last:
            for j in range(last, 1, -1):
                w_parts[j] = move(w_send[j], j, 0)
        if k != 1:
            moving["send"] = w_send
        moving["done"] = (d_rows, grads, w_parts)
        moved = tie(moving)
        d_rows, grads, w_parts = moved["done"]
        w_send = moved["send"]
        if k == 0:
            columns = moved["columns"]
        if k == 1:
            first_cut = moved["cut"]
        if k == last - 1:
            by_expert = moved["weights"]
        if k == last:
            w_parts[0] = w_send[0]
            w_arrays = [w_parts[j] for j in range(length)]
            w_flipped = flips(regroup(w_arrays))
        if 1 < k < length:
            parts[k - 1] = whole(*near[k - 1]) + whole(*moved["far"])
        if k < length:
            near[k] = (own, moved["x"], moved["y"])
        own = moved.get("own")
    back = moved["back"]
    back[last - 1] = move(grads[last - 1], 1 - last, 0)
    parts[last] = whole(*near[last]) + tuple((f, 0, half) for f in moved["far"])
    parts[0] = whole(*near[0]) + tuple((f, half, half) for f in moved["far"])
    add_chunks(last, 0)
    back[last] = move(grads[last], -last, 0)
    back[0] = grads[0]
    back = [back[j] for j in range(length)]
    pieces = tuple((k, 0) if c == 0 else (length + c - 1, k) for k in range(length) for c in range(4))
    w_slots = order_slots(w_arrays + w_flipped, pieces)
    d_rows = [d_rows[j] for j in range(length)]

    def outer_perm(steps):
        return [(i, (i + steps) % outer_size) for i in range(outer_size)]

    owners = (outer_at + jnp.arange(outer_size, dtype=jnp.int32)) % outer_size
    partials = []
    for start, stop in ((0, experts // 2), (experts // 2, experts)):
        if start:
            d_rows, back = tie((d_rows, back))
        mine, *sent = partial_rows(owners, w_slots, d_rows, start, stop)
        partials.append(
            [mine]
            + [lax.ppermute(part, "outer", outer_perm(r)) for r, part in enumerate(sent, 1)]
        )
    partials, leaving = tie((partials, regroup(back)))
    flipped = flips(leaving)

    at = outer_at.astype(jnp.int32)[None]
    total_rows = secondary.size // LANES
    blocks = rows // 16
    cuts = [0, blocks - max(1, blocks // 6), blocks]
    outs = []
    for start, stop in zip(cuts[:-1], cuts[1:]):
        if stop == blocks:
            partials, flipped = tie((partials, flipped))
        outs = adam_rows(
            at, partials, *state, total_rows, outs, start, stop - start
        )
    new_weight, new_moment1, new_moment2, full, copy = outs
    for r in range(1, outer_size):
        got = lax.ppermute(copy, "outer", outer_perm(r))
        owner = (outer_at + outer_size - r) % outer_size
        full = place_rows(owner.astype(jnp.int32)[None], got, full)

    d_hidden, d_probs = finish(
        *columns, hidden.reshape(choices, hidden_width), back + flipped, pieces
    )
    return (
        d_hidden.reshape(hidden.shape),
        d_probs.T,
        lane_unview(new_weight, weight.shape),
        lane_unview(new_moment1, weight.shape),
        lane_unview(new_moment2, weight.shape),
        lane_unview(full, secondary.shape),
    )


def solution(mesh):
    in_specs = (
        P(("outer", "inner"), None),
        P(("outer", "inner"), None, None),
        P(("outer", "inner"), None),
        P(("outer", "inner"), None),
        P(None, "inner", None),
        P("outer", "inner", None),
        P("outer", "inner", None),
        P("outer", "inner", None),
    )
    out_specs = (
        P(("outer", "inner"), None, None),
        P(("outer", "inner"), None),
        P("outer", "inner", None),
        P("outer", "inner", None),
        P("outer", "inner", None),
        P(None, "inner", None),
    )
    return jax.shard_map(local, mesh=mesh, in_specs=in_specs, out_specs=out_specs, check_vma=False)
```

```python
import functools

import jax
import jax.numpy as jnp
from jax import lax
from jax.experimental import pallas as pl
from jax.experimental.pallas import tpu as pltpu
from jax.sharding import PartitionSpec as P

EXPERTS = 64
CAP = 24
TOP = 8
LANES = 128
MIB = 1 << 20
SMALL = pl.CostEstimate(flops=0, bytes_accessed=1 << 16, transcendentals=0)


beta_one = 0.9
beta_two = 0.95
adam_epsilon = 1e-08
learn_rate = 0.003
decay_rate = 0.1
bias_one = 1.0 - 0.9**20
bias_two = 1.0 - 0.95**20

HBM = pl.BlockSpec(memory_space=pltpu.HBM)
INSIDE = pl.BlockSpec(memory_space=pltpu.VMEM)


def slot_targets(flat_ids):
    count = flat_ids.shape[0]
    block = 128
    blocks = count // block
    onehot = (jnp.arange(EXPERTS, dtype=jnp.int32)[:, None] == flat_ids[None, :]).astype(
        jnp.bfloat16
    )
    tiles = onehot.reshape(EXPERTS, blocks, block)
    lower = (jnp.arange(block)[:, None] < jnp.arange(block)[None, :]).astype(jnp.bfloat16)
    within = jnp.einsum("ebk,kj->ebj", tiles, lower, preferred_element_type=jnp.float32)
    totals = jnp.sum(tiles.astype(jnp.float32), axis=2)
    small = (jnp.arange(blocks)[:, None] < jnp.arange(blocks)[None, :]).astype(jnp.float32)
    before = jnp.dot(totals, small, precision=lax.Precision.HIGHEST)
    ranking = (within + before[..., None]).reshape(EXPERTS, count)
    position = jnp.sum(ranking * onehot.astype(jnp.float32), axis=0).astype(jnp.int32)
    return flat_ids * CAP + position


def line_ring(length):
    return [0] + list(range(1, length, 2)) + list(range(2, length, 2))[::-1]


def ring_place(plane, length):
    return jnp.where(plane % 2 == 1, (plane + 1) // 2, (length - plane // 2) % length)


def ring_plane(place, length):
    up = 2 * place - 1
    down = 2 * (length - place)
    return jnp.where(place == 0, 0, jnp.where(up < length, up, down))


def step_perm(size, steps, flip):
    ring = line_ring(size // 4)
    after = {at: ring[(i + steps) % len(ring)] for i, at in enumerate(ring)}
    return [(i, after[i // 4] * 4 + (i % 4 ^ flip)) for i in range(size)]


def source_order(size):
    me = lax.axis_index("inner")
    length = size // 4
    steps = jnp.arange(length, dtype=jnp.int32)
    flips = jnp.arange(4, dtype=jnp.int32)
    at = ring_plane((ring_place(me // 4, length) - steps) % length, length)
    return (at[:, None] * 4 + (me % 4 ^ flips)[None, :]).reshape(size)


def grads_kernel(spans, keep, first, *refs):
    chunks = len(spans)
    parts = [
        [ref.at[pl.ds(*span)] for ref, span in zip(refs[5 * j :], spans[j])]
        for j in range(chunks)
    ]
    by_expert, outs = refs[5 * chunks], refs[5 * chunks + 1 : 7 * chunks + 1]
    all_rows, match, all_grads, weights, sems, weight_sems, *all_d_rows = refs[7 * chunks + 1 :]
    experts, width, features = by_expert.shape
    tokens = all_rows.shape[1] // 4
    slots = experts * CAP
    loads = []
    for j, pieces in enumerate(parts):
        at = 0
        loads.append([])
        for i, piece in enumerate(pieces):
            place = all_rows.at[j, pl.ds(at, piece.shape[0])]
            loads[j].append(pltpu.make_async_copy(piece, place, sems.at[j, i]))
            at += piece.shape[0]
    for load in loads[0]:
        load.start()
    weight_loads = [
        pltpu.make_async_copy(by_expert.at[e], weights.at[e], weight_sems.at[e])
        for e in range(experts)
    ]

    slot = lax.broadcasted_iota(jnp.int32, (slots, tokens), 0)
    expert = (first[0] + slot // CAP).astype(jnp.float32)
    place = (slot % CAP).astype(jnp.float32)
    earlier = lax.broadcasted_iota(jnp.int32, (tokens, tokens), 0)
    earlier = earlier < lax.broadcasted_iota(jnp.int32, (tokens, tokens), 1)
    earlier = jnp.where(earlier, 1.0, 0.0).astype(jnp.bfloat16)
    stores = []
    for j in range(chunks):
        rows, grads = all_rows.at[j], all_grads.at[j]
        d_rows = outs[2 * j] if keep else all_d_rows[0].at[j]
        for load in loads[j]:
            load.wait()
        if j == 0:
            for load in weight_loads:
                load.start()
        if j + 1 < chunks:
            for load in loads[j + 1]:
                load.start()
        hits = []
        for c in range(4):
            ids = rows[c * tokens : (c + 1) * tokens, features:].astype(jnp.float32).T
            named = jnp.zeros((slots, tokens), jnp.float32)
            for k in range(TOP):
                named = jnp.where(expert == ids[k : k + 1], 1.0, named)
            rank = jnp.dot(
                named.astype(jnp.bfloat16), earlier, preferred_element_type=jnp.float32
            )
            hits.append(jnp.where(rank == place, named, 0.0))
        blank = jnp.zeros((CAP, tokens), jnp.float32)
        lines = []
        for e in range(experts):
            for c in range(4):
                line = [blank] * 4
                line[c] = hits[c][e * CAP : (e + 1) * CAP]
                lines.append(jnp.concatenate(line, axis=1))
        match[...] = jnp.concatenate(lines, axis=0).astype(jnp.bfloat16)

        step = min(512, features)
        for at in range(0, features, step):
            d_rows[:, at : at + step] = jnp.dot(
                match[...], rows[:, at : at + step], preferred_element_type=jnp.float32
            ).astype(jnp.bfloat16)
        if not keep:
            stores.append(pltpu.make_async_copy(d_rows, outs[2 * j], sems.at[j, 5]))
            stores[-1].start()
        count = 4 * CAP
        found = []
        for e in range(experts):
            if j == 0:
                weight_loads[e].wait()
            found.append(
                lax.dot_general(
                    d_rows[e * count : (e + 1) * count, :],
                    weights[e],
                    (((1,), (1,)), ((), ())),
                    preferred_element_type=jnp.float32,
                )
            )
        for c in range(4):
            mine = [f[c * CAP : (c + 1) * CAP] for f in found]
            grads[c] = jnp.concatenate(mine, axis=0).astype(jnp.bfloat16)
        stores.append(pltpu.make_async_copy(grads, outs[2 * j + 1], sems.at[j, 6]))
        stores[-1].start()
    for store in stores:
        store.wait()


def chunk_grads(first, parts, by_expert, keep):
    experts, width, features = by_expert.shape
    tokens, columns = parts[0][0][0].shape
    spans = tuple(tuple(piece[1:] for piece in part) for part in parts)
    slots = experts * CAP
    chunks = len(parts)
    found = pl.pallas_call(
        functools.partial(grads_kernel, spans, keep),
        out_shape=[
            jax.ShapeDtypeStruct((4 * slots, features), jnp.bfloat16),
            jax.ShapeDtypeStruct((4, slots, width), jnp.bfloat16),
        ]
        * chunks,
        in_specs=[pl.BlockSpec(memory_space=pltpu.SMEM)] + [HBM] * (5 * chunks + 1),
        out_specs=[INSIDE if keep else HBM, HBM] * chunks,
        scratch_shapes=[
            pltpu.VMEM((chunks, 4 * tokens, columns), jnp.bfloat16),
            pltpu.VMEM((4 * slots, 4 * tokens), jnp.bfloat16),
            pltpu.VMEM((chunks, 4, slots, width), jnp.bfloat16),
            pltpu.VMEM(by_expert.shape, jnp.bfloat16),
            pltpu.SemaphoreType.DMA((chunks, 7)),
            pltpu.SemaphoreType.DMA((experts,)),
        ]
        + ([] if keep else [pltpu.VMEM((chunks, 4 * slots, features), jnp.bfloat16)]),
        compiler_params=pltpu.CompilerParams(vmem_limit_bytes=(52 if keep else 56) * MIB),
        cost_estimate=pl.CostEstimate(
            flops=8 * chunks * slots * features * (4 * tokens + width),
            bytes_accessed=8 * chunks * (slots + tokens) * features,
            transcendentals=0,
        ),
    )(first, *(piece[0] for part in parts for piece in part), by_expert)
    return found[::2], found[1::2]


def order_kernel(pieces, *refs):
    arrays, (out, rows, wide, turned, sems) = refs[:-5], refs[-5:]
    size, slots, width = rows.shape
    experts = slots // CAP
    loads = [
        pltpu.make_async_copy(arrays[a].at[i], rows.at[n], sems.at[n])
        for n, (a, i) in enumerate(pieces)
    ]
    for load in loads:
        load.start()
    for n, load in enumerate(loads):
        load.wait()
        wide[n] = rows[n].astype(jnp.float32)
    for e in range(experts):
        mine = [wide[n, e * CAP : (e + 1) * CAP] for n in range(size)]
        turned[e] = jnp.concatenate(mine, axis=0).T.astype(jnp.bfloat16)
    store = pltpu.make_async_copy(turned, out, sems.at[size])
    store.start()
    store.wait()


def order_slots(arrays, pieces):
    slots, width = arrays[0].shape[1:]
    size = len(pieces)
    shape = (slots // CAP, width, size * CAP)
    return pl.pallas_call(
        functools.partial(order_kernel, pieces),
        out_shape=jax.ShapeDtypeStruct(shape, jnp.bfloat16),
        in_specs=[HBM] * len(arrays),
        out_specs=HBM,
        scratch_shapes=[
            pltpu.VMEM((size, slots, width), jnp.bfloat16),
            pltpu.VMEM((size, slots, width), jnp.float32),
            pltpu.VMEM(shape, jnp.bfloat16),
            pltpu.SemaphoreType.DMA((size + 1,)),
        ],
        compiler_params=pltpu.CompilerParams(vmem_limit_bytes=8 * MIB),
        cost_estimate=pl.CostEstimate(
            flops=0, bytes_accessed=8 * size * slots * width, transcendentals=0
        ),
    )(*arrays)


def regroup_kernel(*refs):
    count = len(refs) - 5
    arrays, outs, (held, sems) = refs[:count], refs[count:-2], refs[-2:]
    loads = [
        pltpu.make_async_copy(a.at[pl.ds(1, 3)], held.at[k], sems.at[k])
        for k, a in enumerate(arrays)
    ]
    for load in loads:
        load.start()
    for load in loads:
        load.wait()
    stores = [
        pltpu.make_async_copy(held.at[:, c], out, sems.at[count + c])
        for c, out in enumerate(outs)
    ]
    for store in stores:
        store.start()
    for store in stores:
        store.wait()


def regroup(arrays):
    _, slots, width = arrays[0].shape
    count = len(arrays)
    return pl.pallas_call(
        regroup_kernel,
        out_shape=[jax.ShapeDtypeStruct((count, slots, width), jnp.bfloat16)] * 3,
        in_specs=[HBM] * count,
        out_specs=[HBM] * 3,
        scratch_shapes=[
            pltpu.VMEM((count, 3, slots, width), jnp.bfloat16),
            pltpu.SemaphoreType.DMA((count + 3,)),
        ],
        compiler_params=pltpu.CompilerParams(vmem_limit_bytes=3 * MIB),
        cost_estimate=pl.CostEstimate(
            flops=0, bytes_accessed=12 * count * slots * width, transcendentals=0
        ),
    )(*arrays)


def partial_kernel(start, total, owners, weighted, *refs):
    count = owners.shape[0]
    blocks, outs = refs[: -4 - count], refs[-4 - count : -4]
    w_in, rows, sums, sems = refs[-4:]
    experts, width, features = sums.shape
    share = width // count
    slots = blocks[0].shape[0] // total
    loads = []
    for e in range(experts):
        mine = [(weighted.at[start + e], w_in.at[e])] + [
            (block.at[pl.ds((start + e) * slots, slots)], rows.at[e, pl.ds(k * slots, slots)])
            for k, block in enumerate(blocks)
        ]
        loads.append(
            [
                pltpu.make_async_copy(source, place, sems.at[e, i])
                for i, (source, place) in enumerate(mine)
            ]
        )
    stores = []
    step = min(1024, features)
    for load in loads[0]:
        load.start()
    for e in range(experts):
        if e + 1 < experts:
            for load in loads[e + 1]:
                load.start()
        for load in loads[e]:
            load.wait()
        for at in range(0, features, step):
            sums[e, :, at : at + step] = jnp.dot(
                w_in[e], rows[e, :, at : at + step], preferred_element_type=jnp.float32
            ).astype(jnp.bfloat16)
        for r, out in enumerate(outs):
            at = pl.multiple_of(owners[r] * share, share)
            store = pltpu.make_async_copy(
                sums.at[e, pl.ds(at, share)], out.at[e], sems.at[e, len(blocks) + 1 + r]
            )
            store.start()
            stores.append(store)
    for store in stores:
        store.wait()


def partial_rows(owners, weighted, blocks, start, stop):
    total, width, slots = weighted.shape
    experts = stop - start
    features = blocks[0].shape[1]
    count = owners.shape[0]
    return pl.pallas_call(
        functools.partial(partial_kernel, start, total),
        out_shape=[jax.ShapeDtypeStruct((experts, width // count, features), jnp.bfloat16)]
        * count,
        in_specs=[pl.BlockSpec(memory_space=pltpu.SMEM)] + [HBM] * (1 + len(blocks)),
        out_specs=[HBM] * count,
        scratch_shapes=[
            pltpu.VMEM((experts, width, slots), jnp.bfloat16),
            pltpu.VMEM((experts, slots, features), jnp.bfloat16),
            pltpu.VMEM((experts, width, features), jnp.bfloat16),
            pltpu.SemaphoreType.DMA((experts, 1 + len(blocks) + count)),
        ],
        compiler_params=pltpu.CompilerParams(vmem_limit_bytes=9 * MIB),
        cost_estimate=pl.CostEstimate(
            flops=2 * experts * width * slots * features,
            bytes_accessed=2 * experts * (width + slots) * features,
            transcendentals=0,
        ),
    )(owners, weighted, *blocks)


def root_of(x):
    inverse = lax.rsqrt(x)
    root = x * inverse
    return root + 0.5 * inverse * (x - root * root)


def reciprocal(x):
    estimate = pl.reciprocal(x, approx=True)
    return estimate * (2.0 - x * estimate)


def adam_kernel(count, owners, kept, first, at, *refs):
    del at
    partials, (w, m1, m2) = refs[:count], refs[count : count + 3]
    partials = [partials[i : i + owners] for i in range(0, count, owners)]
    new_w, new_m1, new_m2, full, copy, grad = refs[count + 3 + kept :]
    _, rows, features = partials[0][0].shape
    tiles = features // LANES
    places = [(span, e) for span in partials for e in range(span[0].shape[0])]
    experts = len(places)
    unit = tiles * experts
    stride = unit + 1
    for e, (span, at) in enumerate(places):
        total = span[0][at].astype(jnp.float32)
        for part in span[1:]:
            total = total + part[at].astype(jnp.float32)
        for t in range(tiles):
            grad[pl.ds(t * experts + e, rows, stride=stride), :] = total[
                :, t * LANES : (t + 1) * LANES
            ]
    block = rows * unit
    base = pl.multiple_of((first + pl.program_id(0)) * block, block)
    for h in range(rows):
        here = slice(h * unit, (h + 1) * unit)
        there = pl.ds(base + h * unit, unit)
        g = grad[h * stride : h * stride + unit]
        one = beta_one * m1[there] + (1.0 - beta_one) * g
        two = beta_two * m2[there] + (1.0 - beta_two) * g * g
        new_m1[here] = one
        new_m2[here] = two
        old = w[there]
        root = reciprocal(root_of(two * (1.0 / bias_two)) + adam_epsilon)
        new = old - learn_rate * (one * (1.0 / bias_one) * root + decay_rate * old)
        new_w[here] = new
        copy[here] = new.astype(jnp.bfloat16)
        full[here] = new.astype(jnp.bfloat16)


def adam_rows(at, partials, w, m1, m2, total_rows, before, first, steps):
    owners = len(partials[0])
    partials = [part for span in partials for part in span]
    _, rows, features = partials[0].shape
    experts = sum(part.shape[0] for part in partials) // owners
    block = 16
    flat = block * experts * features // LANES
    count, kept = len(partials), len(before)
    whole = rows // block
    parts = [
        pl.BlockSpec((part.shape[0], block, features), lambda i, at: (0, first + i, 0))
        for part in partials
    ]
    line = pl.BlockSpec((flat, LANES), lambda i, at: (first + i, 0))
    placed = pl.BlockSpec((flat, LANES), lambda i, at: (at[0] * whole + first + i, 0))
    return pl.pallas_call(
        functools.partial(adam_kernel, count, owners, kept, first),
        grid_spec=pltpu.PrefetchScalarGridSpec(
            num_scalar_prefetch=1,
            grid=(steps,),
            in_specs=parts + [INSIDE] * 3 + [HBM] * kept,
            out_specs=[line] * 3 + [placed, line],
            scratch_shapes=[pltpu.VMEM((flat + block, LANES), jnp.float32)],
        ),
        out_shape=[jax.ShapeDtypeStruct(w.shape, jnp.float32)] * 3
        + [
            jax.ShapeDtypeStruct((total_rows, LANES), jnp.bfloat16),
            jax.ShapeDtypeStruct(w.shape, jnp.bfloat16),
        ],
        input_output_aliases={4 + count + i: i for i in range(kept)},
        compiler_params=pltpu.CompilerParams(vmem_limit_bytes=10 * MIB),
        cost_estimate=SMALL,
    )(at, *partials, w, m1, m2, *before)


def place_kernel(at, got, full, out):
    del at, full
    out[...] = got[...]


def place_rows(owner, got, full):
    steps = 6
    block = got.shape[0] // steps
    return pl.pallas_call(
        place_kernel,
        grid_spec=pltpu.PrefetchScalarGridSpec(
            num_scalar_prefetch=1,
            grid=(steps,),
            in_specs=[pl.BlockSpec((block, LANES), lambda i, at: (i, 0)), HBM],
            out_specs=pl.BlockSpec((block, LANES), lambda i, at: (at[0] * steps + i, 0)),
        ),
        out_shape=jax.ShapeDtypeStruct(full.shape, full.dtype),
        input_output_aliases={2: 0},
        compiler_params=pltpu.CompilerParams(vmem_limit_bytes=14 * MIB),
        cost_estimate=pl.CostEstimate(flops=0, bytes_accessed=4 * got.size, transcendentals=0),
    )(owner, got, full)


def finish_kernel(pieces, target, probs, hidden, *refs):
    back, (d_hidden, d_probs, rows, states, outs, sems) = refs[:-6], refs[-6:]
    count = back[0].shape[1]
    choices, width = hidden.shape
    slots = rows.shape[0]
    loads = [
        pltpu.make_async_copy(back[a].at[i], rows.at[pl.ds(n * count, count)], sems.at[n])
        for n, (a, i) in enumerate(pieces)
    ]
    loads.append(pltpu.make_async_copy(hidden, states, sems.at[len(pieces)]))
    for load in loads:
        load.start()
    targets, scales = target[...].T, probs[...].T
    for load in loads[:-1]:
        load.wait()
    ones = jnp.ones((TOP, width), jnp.bfloat16)
    across = (((1,), (1,)), ((), ()))
    step = 2 * LANES
    row = lax.broadcasted_iota(jnp.int32, (TOP, step), 0)
    choice = lax.broadcasted_iota(jnp.int32, (TOP, step), 1) % TOP
    token = lax.broadcasted_iota(jnp.int32, (step, choices // TOP), 0) // TOP
    lane = lax.broadcasted_iota(jnp.int32, (step, choices // TOP), 1)
    total = jnp.zeros((TOP, choices // TOP), jnp.float32)
    stores = []
    for n, at in enumerate(range(0, choices, step)):
        here = slice(at, at + step)

        def column(table):
            return jnp.concatenate([table[:, 2 * n : 2 * n + 1], table[:, 2 * n + 1 : 2 * n + 2]])

        places = lax.broadcasted_iota(jnp.int32, (step, slots), 1)
        onehot = jnp.where(places == column(targets).astype(jnp.int32), 1.0, 0.0)
        g = jnp.dot(onehot.astype(jnp.bfloat16), rows[...], preferred_element_type=jnp.float32)
        outs[here] = (column(scales) * g).astype(jnp.bfloat16)
        stores.append(
            pltpu.make_async_copy(outs.at[here], d_hidden.at[here], sems.at[len(loads) + n])
        )
        stores[n].start()
        if n == 0:
            loads[-1].wait()
        product = states[here].astype(jnp.float32) * g
        high = product.astype(jnp.bfloat16)
        low = (product - high.astype(jnp.float32)).astype(jnp.bfloat16)
        sums = lax.dot_general(
            ones, high, across, preferred_element_type=jnp.float32
        ) + lax.dot_general(ones, low, across, preferred_element_type=jnp.float32)
        sums = jnp.where(choice == row, sums, 0.0)
        high = sums.astype(jnp.bfloat16)
        low = (sums - high.astype(jnp.float32)).astype(jnp.bfloat16)
        chosen = jnp.where(token + at // TOP == lane, 1.0, 0.0).astype(jnp.bfloat16)
        total = (
            total
            + jnp.dot(high, chosen, preferred_element_type=jnp.float32)
            + jnp.dot(low, chosen, preferred_element_type=jnp.float32)
        )
    d_probs[...] = total
    for store in stores:
        store.wait()


def finish(target, probs, hidden, back, pieces):
    choices, width = hidden.shape
    slots = len(pieces) * back[0].shape[1]
    steps = choices // (2 * LANES)
    return pl.pallas_call(
        functools.partial(finish_kernel, pieces),
        out_shape=(
            jax.ShapeDtypeStruct((choices, width), jnp.bfloat16),
            jax.ShapeDtypeStruct((TOP, choices // TOP), jnp.float32),
        ),
        in_specs=[INSIDE, INSIDE] + [HBM] * (1 + len(back)),
        out_specs=(HBM, INSIDE),
        scratch_shapes=[
            pltpu.VMEM((slots, width), jnp.bfloat16),
            pltpu.VMEM((choices, width), jnp.bfloat16),
            pltpu.VMEM((choices, width), jnp.bfloat16),
            pltpu.SemaphoreType.DMA((len(pieces) + 1 + steps,)),
        ],
        compiler_params=pltpu.CompilerParams(vmem_limit_bytes=56 * MIB),
        cost_estimate=pl.CostEstimate(
            flops=2 * choices * slots * width, bytes_accessed=8 * hidden.size, transcendentals=0
        ),
    )(target, probs, hidden, *back)


def lane_view(array):
    h, e, d = array.shape
    return array.reshape(h, e, d // LANES, LANES).transpose(0, 2, 1, 3).reshape(-1, LANES)


def lane_unview(rows, shape):
    h, e, d = shape
    return rows.reshape(h, d // LANES, e, LANES).transpose(0, 2, 1, 3).reshape(shape)


def local(cotangent, hidden, probs, expert_ids, secondary, weight, moment1, moment2):
    token_count = cotangent.shape[0]
    top_k = expert_ids.shape[1]
    hidden_width = hidden.shape[2]
    experts = secondary.shape[1]
    size = lax.axis_size("inner")
    length = size // 4
    outer_size = lax.axis_size("outer")
    outer_at = lax.axis_index("outer")
    me = lax.axis_index("inner")
    choices = token_count * top_k
    slots = experts * CAP
    rows = weight.shape[0]

    flat_ids = expert_ids.reshape(choices)
    target = slot_targets(flat_ids)
    device = flat_ids // experts
    ring_steps = (ring_place(device // 4, length) - ring_place(me // 4, length)) % length
    relative = ring_steps * 4 + (device % 4 ^ me % 4)
    target = (relative - device) * slots + target
    all_slots = jnp.arange(size * slots, dtype=jnp.int32)
    matches = (all_slots[:, None] == target[None, :]).astype(jnp.bfloat16)
    weighted = (
        (probs[..., None] * hidden.astype(jnp.float32))
        .astype(jnp.bfloat16)
        .reshape(choices, hidden_width)
    )
    w_send = jnp.dot(matches, weighted, preferred_element_type=jnp.float32).astype(jnp.bfloat16)
    w_send = w_send.reshape(length, 4, slots, hidden_width)
    columns = tuple(
        v.astype(jnp.float32).reshape(choices // LANES, LANES) for v in (target, probs)
    )
    state = tuple(lane_view(a) for a in (weight, moment1, moment2))

    def move(block, steps, flip):
        return lax.ppermute(block, "inner", step_perm(size, steps, flip))

    tie = lax.optimization_barrier
    last = length - 1
    half = token_count // 2
    first = (me * experts).astype(jnp.int32)[None]
    tags = jnp.pad(expert_ids.astype(jnp.bfloat16), ((0, 0), (0, LANES - top_k)))
    own = jnp.concatenate([cotangent, tags], axis=1)
    by_expert = jnp.transpose(secondary, (1, 0, 2))
    near, parts, w_parts = {}, {}, {}
    d_rows, grads, back = {}, {}, {}

    def add_chunks(*chunks, keep=False):
        found = chunk_grads(first, [parts[j] for j in chunks], by_expert, keep)
        for j, d_chunk, g_chunk in zip(chunks, *found):
            d_rows[j], grads[j] = d_chunk, g_chunk

    def flips(arrays):
        return [move(a, 0, c) for c, a in enumerate(arrays, 1)]

    def whole(*arrays):
        return tuple((a, 0, a.shape[0]) for a in arrays)

    def halves(j):
        _, by_x, by_y = near[j]
        return (by_x[:half], by_y[half:])

    def far(low, high):
        return (move(low, 0, 2), move(high, 0, 1))

    for k in range(length + 1):
        moving = {}
        if k < last:
            moving["own"] = move(own, 1, 0)
        if k < length:
            moving["x"] = move(own, 0, 1)
            moving["y"] = move(own, 0, 2)
        if 1 < k < length:
            moving["far"] = far(*halves(k - 1))
        if k == length:
            both = zip(halves(last), first_cut)
            moving["far"] = far(*(jnp.concatenate(pair) for pair in both))
            for j in range(1, last - 1):
                back[j] = move(grads[j], -j, 0)
            moving["back"] = back
        if k > 2:
            add_chunks(k - 2)
        if k == 0:
            moving["columns"] = columns
        if k == 1:
            moving["cut"] = halves(0)
            moving["send"] = [w_send[j] for j in range(length)]
        if k == last - 1:
            moving["weights"] = by_expert
            w_parts[1] = move(w_send[1], 1, 0)
        if k == last:
            for j in range(last, 1, -1):
                w_parts[j] = move(w_send[j], j, 0)
        if k != 1:
            moving["send"] = w_send
        moving["done"] = (d_rows, grads, w_parts)
        moved = tie(moving)
        d_rows, grads, w_parts = moved["done"]
        w_send = moved["send"]
        if k == 0:
            columns = moved["columns"]
        if k == 1:
            first_cut = moved["cut"]
        if k == last - 1:
            by_expert = moved["weights"]
        if k == last:
            w_parts[0] = w_send[0]
            w_arrays = [w_parts[j] for j in range(length)]
            w_flipped = flips(regroup(w_arrays))
        if 1 < k < length:
            parts[k - 1] = whole(*near[k - 1]) + whole(*moved["far"])
        if k < length:
            near[k] = (own, moved["x"], moved["y"])
        own = moved.get("own")
    back = moved["back"]
    back[last - 1] = move(grads[last - 1], 1 - last, 0)
    parts[last] = whole(*near[last]) + tuple((f, 0, half) for f in moved["far"])
    parts[0] = whole(*near[0]) + tuple((f, half, half) for f in moved["far"])
    add_chunks(last, 0)
    back[last] = move(grads[last], -last, 0)
    back[0] = grads[0]
    back = [back[j] for j in range(length)]
    pieces = tuple((k, 0) if c == 0 else (length + c - 1, k) for k in range(length) for c in range(4))
    w_slots = order_slots(w_arrays + w_flipped, pieces)
    d_rows = [d_rows[j] for j in range(length)]

    def outer_perm(steps):
        return [(i, (i + steps) % outer_size) for i in range(outer_size)]

    owners = (outer_at + jnp.arange(outer_size, dtype=jnp.int32)) % outer_size
    partials = []
    for start, stop in ((0, experts // 2), (experts // 2, experts)):
        if start:
            d_rows, back = tie((d_rows, back))
        mine, *sent = partial_rows(owners, w_slots, d_rows, start, stop)
        partials.append(
            [mine]
            + [lax.ppermute(part, "outer", outer_perm(r)) for r, part in enumerate(sent, 1)]
        )
    partials, leaving = tie((partials, regroup(back)))
    flipped = flips(leaving)

    at = outer_at.astype(jnp.int32)[None]
    total_rows = secondary.size // LANES
    blocks = rows // 16
    cuts = [0, blocks - max(1, blocks // 6), blocks]
    outs = []
    for start, stop in zip(cuts[:-1], cuts[1:]):
        if stop == blocks:
            partials, flipped = tie((partials, flipped))
        outs = adam_rows(
            at, partials, *state, total_rows, outs, start, stop - start
        )
    new_weight, new_moment1, new_moment2, full, copy = outs
    for r in range(1, outer_size):
        got = lax.ppermute(copy, "outer", outer_perm(r))
        owner = (outer_at + outer_size - r) % outer_size
        full = place_rows(owner.astype(jnp.int32)[None], got, full)

    d_hidden, d_probs = finish(
        *columns, hidden.reshape(choices, hidden_width), back + flipped, pieces
    )
    return (
        d_hidden.reshape(hidden.shape),
        d_probs.T,
        lane_unview(new_weight, weight.shape),
        lane_unview(new_moment1, weight.shape),
        lane_unview(new_moment2, weight.shape),
        lane_unview(full, secondary.shape),
    )


def solution(mesh):
    in_specs = (
        P(("outer", "inner"), None),
        P(("outer", "inner"), None, None),
        P(("outer", "inner"), None),
        P(("outer", "inner"), None),
        P(None, "inner", None),
        P("outer", "inner", None),
        P("outer", "inner", None),
        P("outer", "inner", None),
    )
    out_specs = (
        P(("outer", "inner"), None, None),
        P(("outer", "inner"), None),
        P("outer", "inner", None),
        P("outer", "inner", None),
        P("outer", "inner", None),
        P(None, "inner", None),
    )
    return jax.shard_map(local, mesh=mesh, in_specs=in_specs, out_specs=out_specs, check_vma=False)
```

```python
import functools

import jax
import jax.numpy as jnp
from jax import lax
from jax.experimental import pallas as pl
from jax.experimental.pallas import tpu as pltpu
from jax.sharding import PartitionSpec as P

EXPERTS = 64
CAP = 24
TOP = 8
LANES = 128
MIB = 1 << 20
SMALL = pl.CostEstimate(flops=0, bytes_accessed=1 << 16, transcendentals=0)


beta_one = 0.9
beta_two = 0.95
adam_epsilon = 1e-08
learn_rate = 0.003
decay_rate = 0.1
bias_one = 1.0 - 0.9**20
bias_two = 1.0 - 0.95**20

HBM = pl.BlockSpec(memory_space=pltpu.HBM)
INSIDE = pl.BlockSpec(memory_space=pltpu.VMEM)


def slot_targets(flat_ids):
    count = flat_ids.shape[0]
    block = 128
    blocks = count // block
    onehot = (jnp.arange(EXPERTS, dtype=jnp.int32)[:, None] == flat_ids[None, :]).astype(
        jnp.bfloat16
    )
    tiles = onehot.reshape(EXPERTS, blocks, block)
    lower = (jnp.arange(block)[:, None] < jnp.arange(block)[None, :]).astype(jnp.bfloat16)
    within = jnp.einsum("ebk,kj->ebj", tiles, lower, preferred_element_type=jnp.float32)
    totals = jnp.sum(tiles.astype(jnp.float32), axis=2)
    small = (jnp.arange(blocks)[:, None] < jnp.arange(blocks)[None, :]).astype(jnp.float32)
    before = jnp.dot(totals, small, precision=lax.Precision.HIGHEST)
    ranking = (within + before[..., None]).reshape(EXPERTS, count)
    position = jnp.sum(ranking * onehot.astype(jnp.float32), axis=0).astype(jnp.int32)
    return flat_ids * CAP + position


def line_ring(length):
    return [0] + list(range(1, length, 2)) + list(range(2, length, 2))[::-1]


def ring_place(plane, length):
    return jnp.where(plane % 2 == 1, (plane + 1) // 2, (length - plane // 2) % length)


def ring_plane(place, length):
    up = 2 * place - 1
    down = 2 * (length - place)
    return jnp.where(place == 0, 0, jnp.where(up < length, up, down))


def step_perm(size, steps, flip):
    ring = line_ring(size // 4)
    after = {at: ring[(i + steps) % len(ring)] for i, at in enumerate(ring)}
    return [(i, after[i // 4] * 4 + (i % 4 ^ flip)) for i in range(size)]


def source_order(size):
    me = lax.axis_index("inner")
    length = size // 4
    steps = jnp.arange(length, dtype=jnp.int32)
    flips = jnp.arange(4, dtype=jnp.int32)
    at = ring_plane((ring_place(me // 4, length) - steps) % length, length)
    return (at[:, None] * 4 + (me % 4 ^ flips)[None, :]).reshape(size)


def grads_kernel(spans, keep, first, *refs):
    chunks = len(spans)
    parts = [
        [ref.at[pl.ds(*span)] for ref, span in zip(refs[5 * j :], spans[j])]
        for j in range(chunks)
    ]
    by_expert, outs = refs[5 * chunks], refs[5 * chunks + 1 : 7 * chunks + 1]
    all_rows, match, all_grads, weights, sems, weight_sems, *all_d_rows = refs[7 * chunks + 1 :]
    experts, width, features = by_expert.shape
    tokens = all_rows.shape[1] // 4
    slots = experts * CAP
    loads = []
    for j, pieces in enumerate(parts):
        at = 0
        loads.append([])
        for i, piece in enumerate(pieces):
            place = all_rows.at[j, pl.ds(at, piece.shape[0])]
            loads[j].append(pltpu.make_async_copy(piece, place, sems.at[j, i]))
            loads[j][i].start()
            at += piece.shape[0]
    weight_loads = [
        pltpu.make_async_copy(by_expert.at[e], weights.at[e], weight_sems.at[e])
        for e in range(experts)
    ]

    slot = lax.broadcasted_iota(jnp.int32, (slots, tokens), 0)
    expert = (first[0] + slot // CAP).astype(jnp.float32)
    place = (slot % CAP).astype(jnp.float32)
    earlier = lax.broadcasted_iota(jnp.int32, (tokens, tokens), 0)
    earlier = earlier < lax.broadcasted_iota(jnp.int32, (tokens, tokens), 1)
    earlier = jnp.where(earlier, 1.0, 0.0).astype(jnp.bfloat16)
    stores = []
    for j in range(chunks):
        rows = all_rows.at[j]
        d_rows = outs[2 * j] if keep else all_d_rows[0].at[j]
        for load in loads[j]:
            load.wait()
        if j == 0:
            for load in weight_loads:
                load.start()
        hits = []
        for c in range(4):
            ids = rows[c * tokens : (c + 1) * tokens, features:].astype(jnp.float32).T
            named = jnp.zeros((slots, tokens), jnp.float32)
            for k in range(TOP):
                named = jnp.where(expert == ids[k : k + 1], 1.0, named)
            rank = jnp.dot(
                named.astype(jnp.bfloat16), earlier, preferred_element_type=jnp.float32
            )
            hits.append(jnp.where(rank == place, named, 0.0))
        blank = jnp.zeros((CAP, tokens), jnp.float32)
        lines = []
        for e in range(experts):
            for c in range(4):
                line = [blank] * 4
                line[c] = hits[c][e * CAP : (e + 1) * CAP]
                lines.append(jnp.concatenate(line, axis=1))
        match[...] = jnp.concatenate(lines, axis=0).astype(jnp.bfloat16)

        step = min(512, features)
        for at in range(0, features, step):
            d_rows[:, at : at + step] = jnp.dot(
                match[...], rows[:, at : at + step], preferred_element_type=jnp.float32
            ).astype(jnp.bfloat16)
        if not keep:
            stores.append(pltpu.make_async_copy(d_rows, outs[2 * j], sems.at[j, 5]))
            stores[-1].start()

    count = 4 * CAP
    found = []
    for e in range(experts):
        weight_loads[e].wait()
        mine = [
            (outs[2 * j] if keep else all_d_rows[0].at[j])[e * count : (e + 1) * count, :]
            for j in range(chunks)
        ]
        found.append(
            lax.dot_general(
                mine[0] if chunks == 1 else jnp.concatenate(mine, axis=0),
                weights[e],
                (((1,), (1,)), ((), ())),
                preferred_element_type=jnp.float32,
            )
        )
    for j in range(chunks):
        grads = all_grads.at[j]
        for c in range(4):
            at = j * count + c * CAP
            mine = [f[at : at + CAP] for f in found]
            grads[c] = jnp.concatenate(mine, axis=0).astype(jnp.bfloat16)
        stores.append(pltpu.make_async_copy(grads, outs[2 * j + 1], sems.at[j, 6]))
        stores[-1].start()
    for store in stores:
        store.wait()


def chunk_grads(first, parts, by_expert, keep):
    experts, width, features = by_expert.shape
    tokens, columns = parts[0][0][0].shape
    spans = tuple(tuple(piece[1:] for piece in part) for part in parts)
    slots = experts * CAP
    chunks = len(parts)
    found = pl.pallas_call(
        functools.partial(grads_kernel, spans, keep),
        out_shape=[
            jax.ShapeDtypeStruct((4 * slots, features), jnp.bfloat16),
            jax.ShapeDtypeStruct((4, slots, width), jnp.bfloat16),
        ]
        * chunks,
        in_specs=[pl.BlockSpec(memory_space=pltpu.SMEM)] + [HBM] * (5 * chunks + 1),
        out_specs=[INSIDE if keep else HBM, HBM] * chunks,
        scratch_shapes=[
            pltpu.VMEM((chunks, 4 * tokens, columns), jnp.bfloat16),
            pltpu.VMEM((4 * slots, 4 * tokens), jnp.bfloat16),
            pltpu.VMEM((chunks, 4, slots, width), jnp.bfloat16),
            pltpu.VMEM(by_expert.shape, jnp.bfloat16),
            pltpu.SemaphoreType.DMA((chunks, 7)),
            pltpu.SemaphoreType.DMA((experts,)),
        ]
        + ([] if keep else [pltpu.VMEM((chunks, 4 * slots, features), jnp.bfloat16)]),
        compiler_params=pltpu.CompilerParams(vmem_limit_bytes=(52 if keep else 56) * MIB),
        cost_estimate=pl.CostEstimate(
            flops=8 * chunks * slots * features * (4 * tokens + width),
            bytes_accessed=8 * chunks * (slots + tokens) * features,
            transcendentals=0,
        ),
    )(first, *(piece[0] for part in parts for piece in part), by_expert)
    return found[::2], found[1::2]


def order_kernel(pieces, *refs):
    arrays, (out, rows, wide, turned, sems) = refs[:-5], refs[-5:]
    size, slots, width = rows.shape
    experts = slots // CAP
    loads = [
        pltpu.make_async_copy(arrays[a].at[i], rows.at[n], sems.at[n])
        for n, (a, i) in enumerate(pieces)
    ]
    for load in loads:
        load.start()
    for n, load in enumerate(loads):
        load.wait()
        wide[n] = rows[n].astype(jnp.float32)
    for e in range(experts):
        mine = [wide[n, e * CAP : (e + 1) * CAP] for n in range(size)]
        turned[e] = jnp.concatenate(mine, axis=0).T.astype(jnp.bfloat16)
    store = pltpu.make_async_copy(turned, out, sems.at[size])
    store.start()
    store.wait()


def order_slots(arrays, pieces):
    slots, width = arrays[0].shape[1:]
    size = len(pieces)
    shape = (slots // CAP, width, size * CAP)
    return pl.pallas_call(
        functools.partial(order_kernel, pieces),
        out_shape=jax.ShapeDtypeStruct(shape, jnp.bfloat16),
        in_specs=[HBM] * len(arrays),
        out_specs=HBM,
        scratch_shapes=[
            pltpu.VMEM((size, slots, width), jnp.bfloat16),
            pltpu.VMEM((size, slots, width), jnp.float32),
            pltpu.VMEM(shape, jnp.bfloat16),
            pltpu.SemaphoreType.DMA((size + 1,)),
        ],
        compiler_params=pltpu.CompilerParams(vmem_limit_bytes=10 * MIB),
        cost_estimate=pl.CostEstimate(
            flops=0, bytes_accessed=8 * size * slots * width, transcendentals=0
        ),
    )(*arrays)


def regroup_kernel(*refs):
    count = len(refs) - 5
    arrays, outs, (held, sems) = refs[:count], refs[count:-2], refs[-2:]
    loads = [
        pltpu.make_async_copy(a.at[pl.ds(1, 3)], held.at[k], sems.at[k])
        for k, a in enumerate(arrays)
    ]
    for load in loads:
        load.start()
    for load in loads:
        load.wait()
    stores = [
        pltpu.make_async_copy(held.at[:, c], out, sems.at[count + c])
        for c, out in enumerate(outs)
    ]
    for store in stores:
        store.start()
    for store in stores:
        store.wait()


def regroup(arrays):
    _, slots, width = arrays[0].shape
    count = len(arrays)
    return pl.pallas_call(
        regroup_kernel,
        out_shape=[jax.ShapeDtypeStruct((count, slots, width), jnp.bfloat16)] * 3,
        in_specs=[HBM] * count,
        out_specs=[HBM] * 3,
        scratch_shapes=[
            pltpu.VMEM((count, 3, slots, width), jnp.bfloat16),
            pltpu.SemaphoreType.DMA((count + 3,)),
        ],
        compiler_params=pltpu.CompilerParams(vmem_limit_bytes=10 * MIB),
        cost_estimate=pl.CostEstimate(
            flops=0, bytes_accessed=12 * count * slots * width, transcendentals=0
        ),
    )(*arrays)


def partial_kernel(start, total, owners, weighted, *refs):
    count = owners.shape[0]
    blocks, outs = refs[: -4 - count], refs[-4 - count : -4]
    w_in, rows, sums, sems = refs[-4:]
    experts, width, features = sums.shape
    share = width // count
    slots = blocks[0].shape[0] // total
    loads = []
    for e in range(experts):
        mine = [(weighted.at[start + e], w_in.at[e])] + [
            (block.at[pl.ds((start + e) * slots, slots)], rows.at[e, pl.ds(k * slots, slots)])
            for k, block in enumerate(blocks)
        ]
        loads.append(
            [
                pltpu.make_async_copy(source, place, sems.at[e, i])
                for i, (source, place) in enumerate(mine)
            ]
        )
    stores = []
    step = min(1024, features)
    for load in loads[0]:
        load.start()
    for e in range(experts):
        if e + 1 < experts:
            for load in loads[e + 1]:
                load.start()
        for load in loads[e]:
            load.wait()
        for at in range(0, features, step):
            sums[e, :, at : at + step] = jnp.dot(
                w_in[e], rows[e, :, at : at + step], preferred_element_type=jnp.float32
            ).astype(jnp.bfloat16)
        for r, out in enumerate(outs):
            at = pl.multiple_of(owners[r] * share, share)
            store = pltpu.make_async_copy(
                sums.at[e, pl.ds(at, share)], out.at[e], sems.at[e, len(blocks) + 1 + r]
            )
            store.start()
            stores.append(store)
    for store in stores:
        store.wait()


def partial_rows(owners, weighted, blocks, start, stop):
    total, width, slots = weighted.shape
    experts = stop - start
    features = blocks[0].shape[1]
    count = owners.shape[0]
    return pl.pallas_call(
        functools.partial(partial_kernel, start, total),
        out_shape=[jax.ShapeDtypeStruct((experts, width // count, features), jnp.bfloat16)]
        * count,
        in_specs=[pl.BlockSpec(memory_space=pltpu.SMEM)] + [HBM] * (1 + len(blocks)),
        out_specs=[HBM] * count,
        scratch_shapes=[
            pltpu.VMEM((experts, width, slots), jnp.bfloat16),
            pltpu.VMEM((experts, slots, features), jnp.bfloat16),
            pltpu.VMEM((experts, width, features), jnp.bfloat16),
            pltpu.SemaphoreType.DMA((experts, 1 + len(blocks) + count)),
        ],
        compiler_params=pltpu.CompilerParams(vmem_limit_bytes=16 * MIB),
        cost_estimate=pl.CostEstimate(
            flops=2 * experts * width * slots * features,
            bytes_accessed=2 * experts * (width + slots) * features,
            transcendentals=0,
        ),
    )(owners, weighted, *blocks)


def root_of(x):
    inverse = lax.rsqrt(x)
    root = x * inverse
    return root + 0.5 * inverse * (x - root * root)


def reciprocal(x):
    estimate = pl.reciprocal(x, approx=True)
    return estimate * (2.0 - x * estimate)


def adam_kernel(count, owners, kept, first, at, *refs):
    del at
    partials, (w, m1, m2) = refs[:count], refs[count : count + 3]
    partials = [partials[i : i + owners] for i in range(0, count, owners)]
    new_w, new_m1, new_m2, full, copy, grad = refs[count + 3 + kept :]
    _, rows, features = partials[0][0].shape
    tiles = features // LANES
    places = [(span, e) for span in partials for e in range(span[0].shape[0])]
    experts = len(places)
    unit = tiles * experts
    stride = unit + 1
    for e, (span, at) in enumerate(places):
        total = span[0][at].astype(jnp.float32)
        for part in span[1:]:
            total = total + part[at].astype(jnp.float32)
        for t in range(tiles):
            grad[pl.ds(t * experts + e, rows, stride=stride), :] = total[
                :, t * LANES : (t + 1) * LANES
            ]
    block = rows * unit
    base = pl.multiple_of((first + pl.program_id(0)) * block, block)
    for h in range(rows):
        here = slice(h * unit, (h + 1) * unit)
        there = pl.ds(base + h * unit, unit)
        g = grad[h * stride : h * stride + unit]
        one = beta_one * m1[there] + (1.0 - beta_one) * g
        two = beta_two * m2[there] + (1.0 - beta_two) * g * g
        new_m1[here] = one
        new_m2[here] = two
        old = w[there]
        root = reciprocal(root_of(two * (1.0 / bias_two)) + adam_epsilon)
        new = old - learn_rate * (one * (1.0 / bias_one) * root + decay_rate * old)
        new_w[here] = new
        copy[here] = new.astype(jnp.bfloat16)
        full[here] = new.astype(jnp.bfloat16)


def adam_rows(at, partials, w, m1, m2, total_rows, before, first, steps):
    owners = len(partials[0])
    partials = [part for span in partials for part in span]
    _, rows, features = partials[0].shape
    experts = sum(part.shape[0] for part in partials) // owners
    block = 16
    flat = block * experts * features // LANES
    count, kept = len(partials), len(before)
    whole = rows // block
    parts = [
        pl.BlockSpec((part.shape[0], block, features), lambda i, at: (0, first + i, 0))
        for part in partials
    ]
    line = pl.BlockSpec((flat, LANES), lambda i, at: (first + i, 0))
    placed = pl.BlockSpec((flat, LANES), lambda i, at: (at[0] * whole + first + i, 0))
    return pl.pallas_call(
        functools.partial(adam_kernel, count, owners, kept, first),
        grid_spec=pltpu.PrefetchScalarGridSpec(
            num_scalar_prefetch=1,
            grid=(steps,),
            in_specs=parts + [INSIDE] * 3 + [HBM] * kept,
            out_specs=[line] * 3 + [placed, line],
            scratch_shapes=[pltpu.VMEM((flat + block, LANES), jnp.float32)],
        ),
        out_shape=[jax.ShapeDtypeStruct(w.shape, jnp.float32)] * 3
        + [
            jax.ShapeDtypeStruct((total_rows, LANES), jnp.bfloat16),
            jax.ShapeDtypeStruct(w.shape, jnp.bfloat16),
        ],
        input_output_aliases={4 + count + i: i for i in range(kept)},
        compiler_params=pltpu.CompilerParams(vmem_limit_bytes=10 * MIB),
        cost_estimate=SMALL,
    )(at, *partials, w, m1, m2, *before)


def place_kernel(at, got, full, out):
    del at, full
    out[...] = got[...]


def place_rows(owner, got, full):
    steps = 6
    block = got.shape[0] // steps
    return pl.pallas_call(
        place_kernel,
        grid_spec=pltpu.PrefetchScalarGridSpec(
            num_scalar_prefetch=1,
            grid=(steps,),
            in_specs=[pl.BlockSpec((block, LANES), lambda i, at: (i, 0)), HBM],
            out_specs=pl.BlockSpec((block, LANES), lambda i, at: (at[0] * steps + i, 0)),
        ),
        out_shape=jax.ShapeDtypeStruct(full.shape, full.dtype),
        input_output_aliases={2: 0},
        compiler_params=pltpu.CompilerParams(vmem_limit_bytes=14 * MIB),
        cost_estimate=pl.CostEstimate(flops=0, bytes_accessed=4 * got.size, transcendentals=0),
    )(owner, got, full)


def finish_kernel(pieces, target, probs, hidden, *refs):
    back, (d_hidden, d_probs, rows, states, outs, sems) = refs[:-6], refs[-6:]
    count = back[0].shape[1]
    choices, width = hidden.shape
    slots = rows.shape[0]
    loads = [
        pltpu.make_async_copy(back[a].at[i], rows.at[pl.ds(n * count, count)], sems.at[n])
        for n, (a, i) in enumerate(pieces)
    ]
    loads.append(pltpu.make_async_copy(hidden, states, sems.at[len(pieces)]))
    for load in loads:
        load.start()
    targets, scales = target[...].T, probs[...].T
    for load in loads[:-1]:
        load.wait()
    ones = jnp.ones((TOP, width), jnp.bfloat16)
    across = (((1,), (1,)), ((), ()))
    step = 2 * LANES
    row = lax.broadcasted_iota(jnp.int32, (TOP, step), 0)
    choice = lax.broadcasted_iota(jnp.int32, (TOP, step), 1) % TOP
    token = lax.broadcasted_iota(jnp.int32, (step, choices // TOP), 0) // TOP
    lane = lax.broadcasted_iota(jnp.int32, (step, choices // TOP), 1)
    total = jnp.zeros((TOP, choices // TOP), jnp.float32)
    stores = []
    for n, at in enumerate(range(0, choices, step)):
        here = slice(at, at + step)

        def column(table):
            return jnp.concatenate([table[:, 2 * n : 2 * n + 1], table[:, 2 * n + 1 : 2 * n + 2]])

        places = lax.broadcasted_iota(jnp.int32, (step, slots), 1)
        onehot = jnp.where(places == column(targets).astype(jnp.int32), 1.0, 0.0)
        g = jnp.dot(onehot.astype(jnp.bfloat16), rows[...], preferred_element_type=jnp.float32)
        outs[here] = (column(scales) * g).astype(jnp.bfloat16)
        stores.append(
            pltpu.make_async_copy(outs.at[here], d_hidden.at[here], sems.at[len(loads) + n])
        )
        stores[n].start()
        if n == 0:
            loads[-1].wait()
        product = states[here].astype(jnp.float32) * g
        high = product.astype(jnp.bfloat16)
        low = (product - high.astype(jnp.float32)).astype(jnp.bfloat16)
        sums = lax.dot_general(
            ones, high, across, preferred_element_type=jnp.float32
        ) + lax.dot_general(ones, low, across, preferred_element_type=jnp.float32)
        sums = jnp.where(choice == row, sums, 0.0)
        high = sums.astype(jnp.bfloat16)
        low = (sums - high.astype(jnp.float32)).astype(jnp.bfloat16)
        chosen = jnp.where(token + at // TOP == lane, 1.0, 0.0).astype(jnp.bfloat16)
        total = (
            total
            + jnp.dot(high, chosen, preferred_element_type=jnp.float32)
            + jnp.dot(low, chosen, preferred_element_type=jnp.float32)
        )
    d_probs[...] = total
    for store in stores:
        store.wait()


def finish(target, probs, hidden, back, pieces):
    choices, width = hidden.shape
    slots = len(pieces) * back[0].shape[1]
    steps = choices // (2 * LANES)
    return pl.pallas_call(
        functools.partial(finish_kernel, pieces),
        out_shape=(
            jax.ShapeDtypeStruct((choices, width), jnp.bfloat16),
            jax.ShapeDtypeStruct((TOP, choices // TOP), jnp.float32),
        ),
        in_specs=[INSIDE, INSIDE] + [HBM] * (1 + len(back)),
        out_specs=(HBM, INSIDE),
        scratch_shapes=[
            pltpu.VMEM((slots, width), jnp.bfloat16),
            pltpu.VMEM((choices, width), jnp.bfloat16),
            pltpu.VMEM((choices, width), jnp.bfloat16),
            pltpu.SemaphoreType.DMA((len(pieces) + 1 + steps,)),
        ],
        compiler_params=pltpu.CompilerParams(vmem_limit_bytes=56 * MIB),
        cost_estimate=pl.CostEstimate(
            flops=2 * choices * slots * width, bytes_accessed=8 * hidden.size, transcendentals=0
        ),
    )(target, probs, hidden, *back)


def lane_view(array):
    h, e, d = array.shape
    return array.reshape(h, e, d // LANES, LANES).transpose(0, 2, 1, 3).reshape(-1, LANES)


def lane_unview(rows, shape):
    h, e, d = shape
    return rows.reshape(h, d // LANES, e, LANES).transpose(0, 2, 1, 3).reshape(shape)


def local(cotangent, hidden, probs, expert_ids, secondary, weight, moment1, moment2):
    token_count = cotangent.shape[0]
    top_k = expert_ids.shape[1]
    hidden_width = hidden.shape[2]
    experts = secondary.shape[1]
    size = lax.axis_size("inner")
    length = size // 4
    outer_size = lax.axis_size("outer")
    outer_at = lax.axis_index("outer")
    me = lax.axis_index("inner")
    choices = token_count * top_k
    slots = experts * CAP
    rows = weight.shape[0]

    flat_ids = expert_ids.reshape(choices)
    target = slot_targets(flat_ids)
    device = flat_ids // experts
    ring_steps = (ring_place(device // 4, length) - ring_place(me // 4, length)) % length
    relative = ring_steps * 4 + (device % 4 ^ me % 4)
    target = (relative - device) * slots + target
    all_slots = jnp.arange(size * slots, dtype=jnp.int32)
    matches = (all_slots[:, None] == target[None, :]).astype(jnp.bfloat16)
    weighted = (
        (probs[..., None] * hidden.astype(jnp.float32))
        .astype(jnp.bfloat16)
        .reshape(choices, hidden_width)
    )
    w_send = jnp.dot(matches, weighted, preferred_element_type=jnp.float32).astype(jnp.bfloat16)
    w_send = w_send.reshape(length, 4, slots, hidden_width)
    columns = tuple(
        v.astype(jnp.float32).reshape(choices // LANES, LANES) for v in (target, probs)
    )
    state = tuple(lane_view(a) for a in (weight, moment1, moment2))

    def move(block, steps, flip):
        return lax.ppermute(block, "inner", step_perm(size, steps, flip))

    tie = lax.optimization_barrier
    last = length - 1
    half = token_count // 2
    first = (me * experts).astype(jnp.int32)[None]
    tags = jnp.pad(expert_ids.astype(jnp.bfloat16), ((0, 0), (0, LANES - top_k)))
    own = jnp.concatenate([cotangent, tags], axis=1)
    by_expert = jnp.transpose(secondary, (1, 0, 2))
    near, parts, w_parts = {}, {}, {}
    d_rows, grads, back = {}, {}, {}

    def add_chunks(*chunks, keep=False):
        found = chunk_grads(first, [parts[j] for j in chunks], by_expert, keep)
        for j, d_chunk, g_chunk in zip(chunks, *found):
            d_rows[j], grads[j] = d_chunk, g_chunk

    def flips(arrays):
        return [move(a, 0, c) for c, a in enumerate(arrays, 1)]

    def whole(*arrays):
        return tuple((a, 0, a.shape[0]) for a in arrays)

    def halves(j):
        _, by_x, by_y = near[j]
        return (by_x[:half], by_y[half:])

    def far(low, high):
        return (move(low, 0, 2), move(high, 0, 1))

    for k in range(length + 1):
        moving = {}
        if k < last:
            moving["own"] = move(own, 1, 0)
        if k < length:
            moving["x"] = move(own, 0, 1)
            moving["y"] = move(own, 0, 2)
        if 1 < k < length:
            moving["far"] = far(*halves(k - 1))
        if k == length:
            both = zip(halves(last), first_cut)
            moving["far"] = far(*(jnp.concatenate(pair) for pair in both))
            for j in range(1, last - 1):
                back[j] = move(grads[j], -j, 0)
            moving["back"] = back
        if k > 2:
            add_chunks(k - 2)
        if k == 0:
            moving["columns"] = columns
        if k == 1:
            moving["cut"] = halves(0)
            moving["send"] = [w_send[j] for j in range(length)]
        if k == last - 1:
            moving["weights"] = by_expert
            w_parts[1] = move(w_send[1], 1, 0)
        if k == last:
            for j in range(last, 1, -1):
                w_parts[j] = move(w_send[j], j, 0)
        if k != 1:
            moving["send"] = w_send
        moving["done"] = (d_rows, grads, w_parts)
        moved = tie(moving)
        d_rows, grads, w_parts = moved["done"]
        w_send = moved["send"]
        if k == 0:
            columns = moved["columns"]
        if k == 1:
            first_cut = moved["cut"]
        if k == last - 1:
            by_expert = moved["weights"]
        if k == last:
            w_parts[0] = w_send[0]
            w_arrays = [w_parts[j] for j in range(length)]
            w_flipped = flips(regroup(w_arrays))
        if 1 < k < length:
            parts[k - 1] = whole(*near[k - 1]) + whole(*moved["far"])
        if k < length:
            near[k] = (own, moved["x"], moved["y"])
        own = moved.get("own")
    back = moved["back"]
    back[last - 1] = move(grads[last - 1], 1 - last, 0)
    parts[last] = whole(*near[last]) + tuple((f, 0, half) for f in moved["far"])
    parts[0] = whole(*near[0]) + tuple((f, half, half) for f in moved["far"])
    add_chunks(last, 0)
    back[last] = move(grads[last], -last, 0)
    back[0] = grads[0]
    back = [back[j] for j in range(length)]
    pieces = tuple((k, 0) if c == 0 else (length + c - 1, k) for k in range(length) for c in range(4))
    w_slots = order_slots(w_arrays + w_flipped, pieces)
    d_rows = [d_rows[j] for j in range(length)]

    def outer_perm(steps):
        return [(i, (i + steps) % outer_size) for i in range(outer_size)]

    owners = (outer_at + jnp.arange(outer_size, dtype=jnp.int32)) % outer_size
    partials = []
    for start, stop in ((0, experts // 2), (experts // 2, experts)):
        if start:
            d_rows, back = tie((d_rows, back))
        mine, *sent = partial_rows(owners, w_slots, d_rows, start, stop)
        partials.append(
            [mine]
            + [lax.ppermute(part, "outer", outer_perm(r)) for r, part in enumerate(sent, 1)]
        )
    partials, leaving = tie((partials, regroup(back)))
    flipped = flips(leaving)

    at = outer_at.astype(jnp.int32)[None]
    total_rows = secondary.size // LANES
    blocks = rows // 16
    cuts = [0, blocks - max(1, blocks // 6), blocks]
    outs = []
    for start, stop in zip(cuts[:-1], cuts[1:]):
        if stop == blocks:
            partials, flipped = tie((partials, flipped))
        outs = adam_rows(
            at, partials, *state, total_rows, outs, start, stop - start
        )
    new_weight, new_moment1, new_moment2, full, copy = outs
    for r in range(1, outer_size):
        got = lax.ppermute(copy, "outer", outer_perm(r))
        owner = (outer_at + outer_size - r) % outer_size
        full = place_rows(owner.astype(jnp.int32)[None], got, full)

    d_hidden, d_probs = finish(
        *columns, hidden.reshape(choices, hidden_width), back + flipped, pieces
    )
    return (
        d_hidden.reshape(hidden.shape),
        d_probs.T,
        lane_unview(new_weight, weight.shape),
        lane_unview(new_moment1, weight.shape),
        lane_unview(new_moment2, weight.shape),
        lane_unview(full, secondary.shape),
    )


def solution(mesh):
    in_specs = (
        P(("outer", "inner"), None),
        P(("outer", "inner"), None, None),
        P(("outer", "inner"), None),
        P(("outer", "inner"), None),
        P(None, "inner", None),
        P("outer", "inner", None),
        P("outer", "inner", None),
        P("outer", "inner", None),
    )
    out_specs = (
        P(("outer", "inner"), None, None),
        P(("outer", "inner"), None),
        P("outer", "inner", None),
        P("outer", "inner", None),
        P("outer", "inner", None),
        P(None, "inner", None),
    )
    return jax.shard_map(local, mesh=mesh, in_specs=in_specs, out_specs=out_specs, check_vma=False)
```
